512 devices in a mesh: grp: 8 (over z_hi, x), exp: 64 (over y, z_lo, core).
Axes of the slice: x: 4, y: 4, z: 16 (z_hi: 2, z_lo: 8; z = z_hi * 8 + z_lo), core: 2. Of those that a mesh axis runs over, the one named last changes fastest.
Arguments:
- counts: int32 [64], P('exp'), may hold values from 1 to 4095
- up_weights: bfloat16 [64, 4096, 1536], P('exp', 'grp'), may hold values from -16 to 16
- sketch: bfloat16 [1536, 256], replicated, may hold values from -0.15625 to 0.15625
Outputs:
- base: bfloat16 [4096, 1536], P(('grp', 'exp'))
- basis: float32 [64, 4096, 256], P('exp', 'grp')
- coefficients: float32 [64, 256, 1536], P('exp')
The draws below stay inside these ranges and needn't reach their ends.
All inputs are finite; a program needn't handle non-finite values.
Results may differ from the reference program's by a relative error of at most 0.001.
Values may be sent and summed in bfloat16 or wider, within the bound.
No kernel may reach another device: no remote copies, remote signals or barrier semaphores. Data moves between devices by JAX's collectives and lax.ppermute only.
A program may use at most 64 MiB of HBM per device.

```python
import math
import jax
import jax.numpy as jnp
from jax import lax

D = 4096
FF = 1536
RANK = 256
EXPERTS = 64


def with_ends(result, key, least, top_value):
    shape = result.shape
    place = [jax.random.randint(jax.random.fold_in(key, axis), (), 0, shape[axis]) for axis in range(len(shape))]
    result = result.at[tuple(place)].set(least)
    longest = shape.index(max(shape))
    place[longest] = (place[longest] + 1) % shape[longest]
    return result.at[tuple(place)].set(top_value)


def strengthened(values, own_key, source, target, shards_of, factor):
    def block_of(dim):
        return (jnp.arange(values.shape[dim]) // (values.shape[dim] // shards_of)).reshape((-1,) + (1,) * (values.ndim - 1 - dim))

    one_side = jax.random.permutation(own_key, shards_of)[block_of(target)]
    second = (block_of(target) + shards_of // 2) % shards_of
    return jnp.where((block_of(source) == one_side) | (block_of(source) == second), factor * values, values)


def block_levels(key, extent, split, low, high):
    factor_of, own = 1.0, jax.random.fold_in(key, 6)
    for axis_at, shards_of in split:
        steps = jnp.exp(jax.random.uniform(jax.random.fold_in(own, axis_at), (shards_of,), jnp.float32, low / len(split), high / len(split)))
        factor_of = factor_of * jnp.repeat(steps, extent[axis_at] // shards_of).reshape([-1 if axis == axis_at else 1 for axis in range(len(extent))])
    return factor_of


def centred(stream_key, extent, width, most, cuts=(), held_as=jnp.bfloat16):
    loudness = block_levels(stream_key, extent, cuts, -0.22, 0.18) if cuts else 1.0
    array = jax.random.normal(stream_key, extent, jnp.float32) * width * loudness
    return jnp.minimum(jnp.maximum(array, -most), most).astype(held_as)


def gaussian_with(stream_key, extent, spread, limit, cuts, heavy, dtype=jnp.bfloat16):
    values = spread * jax.random.normal(stream_key, extent, jnp.float32)
    if cuts:
        values = values * block_levels(stream_key, extent, cuts, -0.22, 0.18)
    return jnp.clip(strengthened(values, jax.random.fold_in(stream_key, 3), *heavy), -limit, limit).astype(dtype)


def setup_inputs(seed: int = 0) -> dict:
    key_list = jax.random.split(jax.random.key(seed), 4)
    counts = with_ends(jax.random.randint(key_list[0], (EXPERTS,), 1, 4096), jax.random.fold_in(key_list[0], 1), 1, 4095).astype(jnp.int32)
    up_weights = gaussian_with(key_list[1], (EXPERTS, D, FF), 1.0, 16.0, ((0, 64), (1, 8)), (0, 1, 64, 4.0))
    sketch = centred(key_list[2], (FF, RANK), FF ** -0.5, 0.15625)
    return dict(counts=counts, up_weights=up_weights, sketch=sketch)


def reference(counts, up_weights, sketch):
    freq = counts.astype(jnp.float32)
    share = freq / jnp.sum(freq)

    def accumulate(totals, item):
        weight, factor = item
        summed_now, sketched_now = totals
        summed_now = summed_now + factor * weight.astype(jnp.float32)
        sketched_now = sketched_now + factor * jnp.dot(weight.astype(jnp.float32), sketch.astype(jnp.float32), preferred_element_type=jnp.float32)
        return ((summed_now, sketched_now), None)
    start = (jnp.zeros((D, FF), jnp.float32), jnp.zeros((D, RANK), jnp.float32))
    (summed, base_sketch), unused = lax.scan(accumulate, start, (up_weights, share))
    base = summed.astype(jnp.bfloat16)

    def one_expert(weight):
        range_rows = jnp.dot(weight.astype(jnp.float32), sketch.astype(jnp.float32), preferred_element_type=jnp.float32) - base_sketch
        gram = jnp.dot(range_rows.T, range_rows, precision=lax.Precision.HIGHEST)
        lower = jnp.linalg.cholesky(gram)
        ortho = lax.linalg.triangular_solve(lower, range_rows, left_side=False, lower=True, transpose_a=True)
        ortho_short = ortho.astype(jnp.bfloat16)
        ortho_back = lax.optimization_barrier(ortho_short).astype(jnp.float32)
        ortho_rest = (ortho - ortho_back).astype(jnp.bfloat16)
        dims = (((0,), (0,)), ((), ()))
        coeff = lax.dot_general(ortho_short.astype(jnp.float32), weight.astype(jnp.float32), dims, preferred_element_type=jnp.float32)
        coeff = coeff + lax.dot_general(ortho_rest.astype(jnp.float32), weight.astype(jnp.float32), dims, preferred_element_type=jnp.float32)
        coeff = coeff - lax.dot_general(ortho_short.astype(jnp.float32), base.astype(jnp.float32), dims, preferred_element_type=jnp.float32)
        coeff = coeff - lax.dot_general(ortho_rest.astype(jnp.float32), base.astype(jnp.float32), dims, preferred_element_type=jnp.float32)
        return (ortho * math.sqrt(D), coeff)
    basis, coefficients = lax.map(one_expert, up_weights)
    return (base, basis, coefficients)
```

```python
import math

import jax
import jax.numpy as jnp
from jax import lax
from jax.sharding import PartitionSpec as P

F32, BF16 = jnp.float32, jnp.bfloat16
HIGHEST = lax.Precision.HIGHEST
contract_rows = (((0,), (0,)), ((), ()))

YN, ZN, CN, XN, HN = 4, 8, 2, 4, 2
YC_GROUPS = [[y * 16 + z * 2 + c for y in range(YN) for c in range(CN)] for z in range(ZN)]
Z_GROUPS = [[y * 16 + z * 2 + c for z in range(ZN)] for y in range(YN) for c in range(CN)]
Y_GROUPS = [[y * 16 + z * 2 + c for y in range(YN)] for z in range(ZN) for c in range(CN)]
OTHER_CORE = [(i, i ^ 1) for i in range(64)]
X_GROUPS = [[h * 4 + x for x in range(XN)] for h in range(HN)]
OTHER_HALF = [(i, i ^ 4) for i in range(8)]


def along_x(k):
    return [(i, i ^ k) for i in range(8)]


def parts_of(value):
    first = lax.reduce_precision(value, 8, 7)
    rest = value - first
    second = lax.reduce_precision(rest, 8, 7)
    return [first.astype(BF16), second.astype(BF16), (rest - second).astype(BF16)]


def per_device(counts, up_weights, sketch):
    rows, ff = up_weights.shape[1:]
    rank = sketch.shape[1]
    piece = rows // 64
    own = up_weights[0].reshape(YN, ZN, CN, piece, ff).transpose(0, 2, 1, 3, 4)
    own = own.reshape(YN * CN, ZN * piece, ff)

    lane = lax.broadcasted_iota(jnp.int32, (YN * CN, ZN * piece, 128), 2)
    count = counts[0]
    tag = jnp.where(lane == 0, count // 64, jnp.where(lane == 1, count % 64, 0)).astype(BF16)
    got = lax.all_to_all(
        jnp.concatenate([own, tag], axis=2), "exp", 0, 0, axis_index_groups=YC_GROUPS
    )
    freq = got[:, 0, ff].astype(F32) * 64 + got[:, 0, ff + 1].astype(F32)
    weighted = jnp.sum(freq[:, None, None] * got[:, :, :ff].astype(F32), axis=0)
    freq_sum = jnp.broadcast_to(jnp.sum(freq), (ZN, piece, 128))

    sums = lax.all_to_all(
        jnp.concatenate([weighted.reshape(ZN, piece, ff), freq_sum], axis=2),
        "exp", 0, 0, axis_index_groups=Z_GROUPS,
    )
    sums = jnp.sum(sums, axis=0)
    base_rows = sums[:, :ff] / sums[:, ff : ff + 1]
    base_piece = base_rows.astype(BF16)
    sketched = jnp.dot(base_rows, sketch.astype(F32), precision=HIGHEST)

    wide = ff + 3 * rank
    load = jnp.concatenate([base_piece] + parts_of(sketched), axis=1)
    load = lax.all_to_all(
        jnp.broadcast_to(load, (ZN, piece, wide)), "exp", 0, 0, axis_index_groups=Z_GROUPS
    ).reshape(ZN * piece, wide)
    load = lax.all_to_all(
        jnp.broadcast_to(load, (YN, ZN * piece, wide)), "exp", 0, 0, axis_index_groups=Y_GROUPS
    )
    other = lax.ppermute(load, "exp", OTHER_CORE)
    first = lax.axis_index("exp") % 2 == 0
    slab = jnp.stack([jnp.where(first, load, other), jnp.where(first, other, load)], axis=1)
    slab = slab.reshape(rows, wide)
    base = slab[:, :ff]
    base_sketch = (
        slab[:, ff : ff + rank].astype(F32)
        + slab[:, ff + rank : ff + 2 * rank].astype(F32)
        + slab[:, ff + 2 * rank :].astype(F32)
    )

    own = own.reshape(rows, ff)
    range_rows = jnp.dot(own, sketch, preferred_element_type=F32) - base_sketch
    gram = jnp.dot(range_rows.T, range_rows, precision=HIGHEST)
    three = jnp.concatenate(parts_of(range_rows), axis=1)
    delta = lax.dot_general(three, own, contract_rows, preferred_element_type=F32)
    delta = delta - lax.dot_general(three, base, contract_rows, preferred_element_type=F32)
    delta = delta[:rank] + delta[rank : 2 * rank] + delta[2 * rank :]

    both = jnp.concatenate([gram, delta], axis=1).reshape(XN, rank // XN, rank + ff)
    both = lax.all_to_all(both, "grp", 0, 0, axis_index_groups=X_GROUPS)
    both = jnp.sum(both, axis=0)
    both = both + lax.ppermute(both, "grp", OTHER_HALF)
    at_x = lax.axis_index("grp") % XN

    def gathered(block):
        whole = jnp.zeros((XN,) + block.shape, F32)
        whole = lax.dynamic_update_slice(whole, block[None], (at_x, 0, 0))
        for k in (1, 3, 2):
            came = lax.ppermute(block, "grp", along_x(k))
            whole = lax.dynamic_update_slice(whole, came[None], (at_x ^ k, 0, 0))
        return whole.reshape(XN * block.shape[0], block.shape[1])

    gram = gathered(both[:, :rank])
    delta = gathered(both[:, rank:])
    lower = jnp.linalg.cholesky(gram)
    inverse = lax.linalg.triangular_solve(
        lower, jnp.eye(rank, dtype=F32), left_side=True, lower=True
    )
    ortho = lax.dot_general(
        range_rows, inverse, (((1,), (1,)), ((), ())), precision=HIGHEST
    )
    coeff = jnp.dot(inverse, delta, precision=HIGHEST)
    width_total = rows * lax.axis_size("grp")
    basis = ortho * math.sqrt(width_total)
    basis = basis.reshape(YN, CN, ZN, piece, rank).transpose(0, 2, 1, 3, 4)
    return (base_piece, basis.reshape(1, rows, rank), coeff[None])


def solution(mesh):
    placed = (P("exp"), P("exp", "grp", None), P())
    return jax.shard_map(
        per_device,
        mesh=mesh,
        in_specs=placed,
        out_specs=(P(("grp", "exp"), None), P("exp", "grp", None), P("exp", None, None)),
        check_vma=False,
    )
```

```python
import math

import jax
import jax.numpy as jnp
from jax import lax
from jax.sharding import PartitionSpec as P

F32, BF16 = jnp.float32, jnp.bfloat16
HIGHEST = lax.Precision.HIGHEST
contract_rows = (((0,), (0,)), ((), ()))

YN, ZN, CN, XN, HN = 4, 8, 2, 4, 2
YC_GROUPS = [[y * 16 + z * 2 + c for y in range(YN) for c in range(CN)] for z in range(ZN)]
Z_GROUPS = [[y * 16 + z * 2 + c for z in range(ZN)] for y in range(YN) for c in range(CN)]
Y_GROUPS = [[y * 16 + z * 2 + c for y in range(YN)] for z in range(ZN) for c in range(CN)]
OTHER_CORE = [(i, i ^ 1) for i in range(64)]
OTHER_HALF = [(i, i ^ 4) for i in range(8)]


def along_x(k):
    return [(i, i ^ k) for i in range(8)]


def parts_of(value):
    first = lax.reduce_precision(value, 8, 7)
    rest = value - first
    second = lax.reduce_precision(rest, 8, 7)
    return [first.astype(BF16), second.astype(BF16), (rest - second).astype(BF16)]


def per_device(counts, up_weights, sketch):
    rows, ff = up_weights.shape[1:]
    rank = sketch.shape[1]
    piece = rows // 64
    own = up_weights[0].reshape(YN, ZN, CN, piece, ff).transpose(0, 2, 1, 3, 4)
    own = own.reshape(YN * CN, ZN * piece, ff)

    lane = lax.broadcasted_iota(jnp.int32, (YN * CN, ZN * piece, 128), 2)
    count = counts[0]
    tag = jnp.where(lane == 0, count // 64, jnp.where(lane == 1, count % 64, 0)).astype(BF16)
    got = lax.all_to_all(
        jnp.concatenate([own, tag], axis=2), "exp", 0, 0, axis_index_groups=YC_GROUPS
    )
    freq = got[:, 0, ff].astype(F32) * 64 + got[:, 0, ff + 1].astype(F32)
    weighted = jnp.sum(freq[:, None, None] * got[:, :, :ff].astype(F32), axis=0)
    freq_sum = jnp.broadcast_to(jnp.sum(freq), (ZN, piece, 128))

    sums = lax.all_to_all(
        jnp.concatenate([weighted.reshape(ZN, piece, ff), freq_sum], axis=2),
        "exp", 0, 0, axis_index_groups=Z_GROUPS,
    )
    sums = jnp.sum(sums, axis=0)
    base_rows = sums[:, :ff] / sums[:, ff : ff + 1]
    base_piece = base_rows.astype(BF16)
    sketched = jnp.dot(base_rows, sketch.astype(F32), precision=HIGHEST)

    wide = ff + 3 * rank
    load = jnp.concatenate([base_piece] + parts_of(sketched), axis=1)
    load = lax.all_to_all(
        jnp.broadcast_to(load, (ZN, piece, wide)), "exp", 0, 0, axis_index_groups=Z_GROUPS
    ).reshape(ZN * piece, wide)
    load = lax.all_to_all(
        jnp.broadcast_to(load, (YN, ZN * piece, wide)), "exp", 0, 0, axis_index_groups=Y_GROUPS
    )
    other = lax.ppermute(load, "exp", OTHER_CORE)
    first = lax.axis_index("exp") % 2 == 0
    slab = jnp.stack([jnp.where(first, load, other), jnp.where(first, other, load)], axis=1)
    slab = slab.reshape(rows, wide)
    base = slab[:, :ff]
    base_sketch = (
        slab[:, ff : ff + rank].astype(F32)
        + slab[:, ff + rank : ff + 2 * rank].astype(F32)
        + slab[:, ff + 2 * rank :].astype(F32)
    )

    own = own.reshape(rows, ff)
    range_rows = jnp.dot(own, sketch, preferred_element_type=F32) - base_sketch
    gram = jnp.dot(range_rows.T, range_rows, precision=HIGHEST)
    three = jnp.concatenate(parts_of(range_rows), axis=1)
    delta = lax.dot_general(three, own, contract_rows, preferred_element_type=F32)
    delta = delta - lax.dot_general(three, base, contract_rows, preferred_element_type=F32)
    delta = delta[:rank] + delta[rank : 2 * rank] + delta[2 * rank :]

    at_x = lax.axis_index("grp") % XN

    def summed_along_x(whole):
        blocks = whole.reshape(XN, rank // XN, whole.shape[1])
        total = lax.dynamic_index_in_dim(blocks, at_x, 0, keepdims=False)
        for k in (1, 3, 2):
            block = lax.dynamic_index_in_dim(blocks, at_x ^ k, 0, keepdims=False)
            total = total + lax.ppermute(block, "grp", along_x(k))
        return total

    def gathered(block):
        whole = jnp.zeros((XN,) + block.shape, F32)
        whole = lax.dynamic_update_slice(whole, block[None], (at_x, 0, 0))
        for k in (1, 3, 2):
            came = lax.ppermute(block, "grp", along_x(k))
            whole = lax.dynamic_update_slice(whole, came[None], (at_x ^ k, 0, 0))
        return whole.reshape(XN * block.shape[0], block.shape[1])

    gram = summed_along_x(gram)
    delta = summed_along_x(delta)
    gram = gram + lax.ppermute(gram, "grp", OTHER_HALF)
    delta, gram = lax.optimization_barrier((delta, gram))
    delta = delta + lax.ppermute(delta, "grp", OTHER_HALF)
    gram = gathered(gram)
    delta = gathered(delta)
    lower = jnp.linalg.cholesky(gram)
    inverse = lax.linalg.triangular_solve(
        lower, jnp.eye(rank, dtype=F32), left_side=True, lower=True
    )
    ortho = lax.dot_general(
        range_rows, inverse, (((1,), (1,)), ((), ())), precision=HIGHEST
    )
    coeff = jnp.dot(inverse, delta, precision=HIGHEST)
    width_total = rows * lax.axis_size("grp")
    basis = ortho * math.sqrt(width_total)
    basis = basis.reshape(YN, CN, ZN, piece, rank).transpose(0, 2, 1, 3, 4)
    return (base_piece, basis.reshape(1, rows, rank), coeff[None])


def solution(mesh):
    placed = (P("exp"), P("exp", "grp", None), P())
    return jax.shard_map(
        per_device,
        mesh=mesh,
        in_specs=placed,
        out_specs=(P(("grp", "exp"), None), P("exp", "grp", None), P("exp", None, None)),
        check_vma=False,
    )
```

```python
import math

import jax
import jax.numpy as jnp
from jax import lax
from jax.experimental import pallas as pl
from jax.experimental.pallas import tpu as pltpu
from jax.sharding import PartitionSpec as P

F32, BF16 = jnp.float32, jnp.bfloat16
HIGHEST = lax.Precision.HIGHEST
contract_rows = (((0,), (0,)), ((), ()))

YN, ZN, CN, XN, HN = 4, 8, 2, 4, 2
YC_GROUPS = [[y * 16 + z * 2 + c for y in range(YN) for c in range(CN)] for z in range(ZN)]
Z_GROUPS = [[y * 16 + z * 2 + c for z in range(ZN)] for y in range(YN) for c in range(CN)]
Y_GROUPS = [[y * 16 + z * 2 + c for y in range(YN)] for z in range(ZN) for c in range(CN)]
OTHER_CORE = [(i, i ^ 1) for i in range(64)]
OTHER_HALF = [(i, i ^ 4) for i in range(8)]


def along_x(k):
    return [(i, i ^ k) for i in range(8)]


def parts_of(value):
    first = lax.reduce_precision(value, 8, 7)
    rest = value - first
    second = lax.reduce_precision(rest, 8, 7)
    return [first.astype(BF16), second.astype(BF16), (rest - second).astype(BF16)]


PANEL = 64


def eye(n):
    row, col = (lax.broadcasted_iota(jnp.int32, (n, n), d) for d in (0, 1))
    return jnp.where(row == col, 1.0, 0.0).astype(F32)


def inverse_root(value):
    guess = lax.rsqrt(value)
    return guess * (1.5 - 0.5 * value * guess * guess)


def inverse_factor_of_panel(square):
    n = square.shape[0]
    work = jnp.concatenate([square, eye(n)], axis=1)
    row = lax.broadcasted_iota(jnp.int32, work.shape, 0)
    for j in range(0, n, 2):
        left = jnp.broadcast_to(work[:, j : j + 1], work.shape)
        right = jnp.broadcast_to(work[:, j + 1 : j + 2], work.shape)
        scale = inverse_root(left[j : j + 1])
        cross = left[j + 1 : j + 2] * scale
        scale_next = inverse_root(right[j + 1 : j + 2] - cross * cross)
        top = work[j : j + 1] * scale
        low = (work[j + 1 : j + 2] - cross * top) * scale_next
        left = left * scale
        right = (right - left * cross) * scale_next
        rest = jnp.where(row > j + 1, work - left * top - right * low, work)
        work = jnp.where(row == j, top, jnp.where(row == j + 1, low, rest))
    return work[:, n:]


def inverse_factor_kernel(gram_ref, inverse_ref, work_ref):
    n = gram_ref.shape[0]
    work_ref[:, :n] = gram_ref[...]
    work_ref[:, n:] = eye(n)
    for at in range(0, n, PANEL):
        end = at + PANEL
        own = inverse_factor_of_panel(work_ref[at:end, at:end])
        done = jnp.dot(own, work_ref[at:end], precision=HIGHEST, preferred_element_type=F32)
        inverse_ref[at:end] = done[:, n:]
        if end < n:
            below = lax.dot_general(
                work_ref[end:, at:end], own, (((1,), (1,)), ((), ())),
                precision=HIGHEST, preferred_element_type=F32,
            )
            work_ref[end:] = work_ref[end:] - jnp.dot(
                below, done, precision=HIGHEST, preferred_element_type=F32
            )


def inverse_factor(gram):
    n = gram.shape[0]
    vmem = pl.BlockSpec(memory_space=pltpu.VMEM)
    return pl.pallas_call(
        inverse_factor_kernel,
        out_shape=jax.ShapeDtypeStruct((n, n), F32),
        in_specs=[vmem],
        out_specs=vmem,
        scratch_shapes=[pltpu.VMEM((n, 2 * n), F32)],
        compiler_params=pltpu.CompilerParams(vmem_limit_bytes=16 * 2**20),
        cost_estimate=pl.CostEstimate(flops=10**9, bytes_accessed=2**19, transcendentals=0),
        name="inverse_factor",
    )(gram)


def per_device(counts, up_weights, sketch):
    rows, ff = up_weights.shape[1:]
    rank = sketch.shape[1]
    piece = rows // 64
    own = up_weights[0].reshape(YN, ZN, CN, piece, ff).transpose(0, 2, 1, 3, 4)
    own = own.reshape(YN * CN, ZN * piece, ff)

    lane = lax.broadcasted_iota(jnp.int32, (YN * CN, ZN * piece, 128), 2)
    count = counts[0]
    tag = jnp.where(lane == 0, count // 64, jnp.where(lane == 1, count % 64, 0)).astype(BF16)
    got = lax.all_to_all(
        jnp.concatenate([own, tag], axis=2), "exp", 0, 0, axis_index_groups=YC_GROUPS
    )
    freq = got[:, 0, ff].astype(F32) * 64 + got[:, 0, ff + 1].astype(F32)
    weighted = jnp.sum(freq[:, None, None] * got[:, :, :ff].astype(F32), axis=0)
    freq_sum = jnp.broadcast_to(jnp.sum(freq), (ZN, piece, 128))

    sums = lax.all_to_all(
        jnp.concatenate([weighted.reshape(ZN, piece, ff), freq_sum], axis=2),
        "exp", 0, 0, axis_index_groups=Z_GROUPS,
    )
    sums = jnp.sum(sums, axis=0)
    base_rows = sums[:, :ff] / sums[:, ff : ff + 1]
    base_piece = base_rows.astype(BF16)
    sketched = jnp.dot(base_rows, sketch.astype(F32), precision=HIGHEST)

    wide = ff + 3 * rank
    load = jnp.concatenate([base_piece] + parts_of(sketched), axis=1)
    load = lax.all_to_all(
        jnp.broadcast_to(load, (ZN, piece, wide)), "exp", 0, 0, axis_index_groups=Z_GROUPS
    ).reshape(ZN * piece, wide)
    load = lax.all_to_all(
        jnp.broadcast_to(load, (YN, ZN * piece, wide)), "exp", 0, 0, axis_index_groups=Y_GROUPS
    )
    other = lax.ppermute(load, "exp", OTHER_CORE)
    first = lax.axis_index("exp") % 2 == 0
    slab = jnp.stack([jnp.where(first, load, other), jnp.where(first, other, load)], axis=1)
    slab = slab.reshape(rows, wide)
    base = slab[:, :ff]
    base_sketch = (
        slab[:, ff : ff + rank].astype(F32)
        + slab[:, ff + rank : ff + 2 * rank].astype(F32)
        + slab[:, ff + 2 * rank :].astype(F32)
    )

    own = own.reshape(rows, ff)
    range_rows = jnp.dot(own, sketch, preferred_element_type=F32) - base_sketch
    gram = jnp.dot(range_rows.T, range_rows, precision=HIGHEST)
    three = jnp.concatenate(parts_of(range_rows), axis=1)
    delta = lax.dot_general(three, own, contract_rows, preferred_element_type=F32)
    delta = delta - lax.dot_general(three, base, contract_rows, preferred_element_type=F32)
    delta = delta[:rank] + delta[rank : 2 * rank] + delta[2 * rank :]

    at_x = lax.axis_index("grp") % XN

    def sent_along_x(whole):
        blocks = whole.reshape(XN, rank // XN, whole.shape[1])
        own = lax.dynamic_index_in_dim(blocks, at_x, 0, keepdims=False)
        came = [
            lax.ppermute(
                lax.dynamic_index_in_dim(blocks, at_x ^ k, 0, keepdims=False),
                "grp", along_x(k),
            )
            for k in (1, 3, 2)
        ]
        return [own] + came

    def gathered(block):
        whole = jnp.zeros((XN,) + block.shape, F32)
        whole = lax.dynamic_update_slice(whole, block[None], (at_x, 0, 0))
        for k in (1, 3, 2):
            came = lax.ppermute(block, "grp", along_x(k))
            whole = lax.dynamic_update_slice(whole, came[None], (at_x ^ k, 0, 0))
        return whole.reshape(XN * block.shape[0], block.shape[1])

    gram = sent_along_x(gram)
    gram, delta = lax.optimization_barrier((gram, delta))
    delta = sum(sent_along_x(delta))
    gram = sum(gram)
    gram_came = lax.ppermute(gram, "grp", OTHER_HALF)
    delta_came = lax.ppermute(delta, "grp", OTHER_HALF)
    gram_came, delta = lax.optimization_barrier((gram_came, delta))
    inverse = inverse_factor(gathered(gram + gram_came))
    inverse, delta_came = lax.optimization_barrier((inverse, delta_came))
    delta = gathered(delta + delta_came)
    ortho = lax.dot_general(
        range_rows, inverse, (((1,), (1,)), ((), ())), precision=HIGHEST
    )
    coeff = jnp.dot(inverse, delta, precision=HIGHEST)
    width_total = rows * lax.axis_size("grp")
    basis = ortho * math.sqrt(width_total)
    basis = basis.reshape(YN, CN, ZN, piece, rank).transpose(0, 2, 1, 3, 4)
    return (base_piece, basis.reshape(1, rows, rank), coeff[None])


def solution(mesh):
    placed = (P("exp"), P("exp", "grp", None), P())
    return jax.shard_map(
        per_device,
        mesh=mesh,
        in_specs=placed,
        out_specs=(P(("grp", "exp"), None), P("exp", "grp", None), P("exp", None, None)),
        check_vma=False,
    )
```

```python
import math

import jax
import jax.numpy as jnp
from jax import lax
from jax.experimental import pallas as pl
from jax.experimental.pallas import tpu as pltpu
from jax.sharding import PartitionSpec as P

F32, BF16 = jnp.float32, jnp.bfloat16
HIGHEST = lax.Precision.HIGHEST
MIB = 2**20

YN, FN, NN, CN, XN = 4, 4, 2, 2, 4


def at(y, far, near, core):
    return y * 16 + (2 * far + near) * 2 + core


CYN_GROUPS = [
    [at(y, f, n, c) for c in range(CN) for y in range(YN) for n in range(NN)] for f in range(FN)
]
YN_GROUPS = [
    [at(y, f, n, c) for y in range(YN) for n in range(NN)] for f in range(FN) for c in range(CN)
]
FAR_GROUPS = [
    [at(y, f, n, c) for f in range(FN)]
    for y in range(YN) for n in range(NN) for c in range(CN)
]
OTHER_CORE = [(i, i ^ 1) for i in range(64)]
OTHER_HALF = [(i, i ^ 4) for i in range(8)]
ALONG_X = [[(i, i ^ k) for i in range(8)] for k in range(XN)]

PANEL = 64


def parts_of(value):
    first = lax.reduce_precision(value, 8, 7)
    rest = value - first
    second = lax.reduce_precision(rest, 8, 7)
    return [first.astype(BF16), second.astype(BF16), (rest - second).astype(BF16)]


def eye(n):
    row, col = (lax.broadcasted_iota(jnp.int32, (n, n), d) for d in (0, 1))
    return jnp.where(row == col, 1.0, 0.0).astype(F32)


def inverse_root(value):
    guess = lax.rsqrt(value)
    return guess * (1.5 - 0.5 * value * guess * guess)


def inverse_factor_of_panel(square):
    n = square.shape[0]
    work = jnp.concatenate([square, eye(n)], axis=1)
    row = lax.broadcasted_iota(jnp.int32, work.shape, 0)
    for j in range(0, n, 2):
        left = jnp.broadcast_to(work[:, j : j + 1], work.shape)
        right = jnp.broadcast_to(work[:, j + 1 : j + 2], work.shape)
        scale = inverse_root(left[j : j + 1])
        cross = left[j + 1 : j + 2] * scale
        scale_next = inverse_root(right[j + 1 : j + 2] - cross * cross)
        top = work[j : j + 1] * scale
        low = (work[j + 1 : j + 2] - cross * top) * scale_next
        left = left * scale
        right = (right - left * cross) * scale_next
        rest = jnp.where(row > j + 1, work - left * top - right * low, work)
        work = jnp.where(row == j, top, jnp.where(row == j + 1, low, rest))
    return work[:, n:]


def inverse_factor_kernel(place_ref, own_ref, *refs):
    came_refs, inverse_ref, work_ref = refs[:-2], refs[-2], refs[-1]
    n = inverse_ref.shape[0]
    block = own_ref.shape[0]
    for k, ref in enumerate((own_ref,) + came_refs):
        start = pl.multiple_of((place_ref[0] ^ k) * block, block)
        work_ref[pl.ds(start, block), :n] = ref[...]
    work_ref[:, n:] = eye(n)
    for top in range(0, n, PANEL):
        end = top + PANEL
        own = inverse_factor_of_panel(work_ref[top:end, top:end])
        done = jnp.dot(own, work_ref[top:end], precision=HIGHEST, preferred_element_type=F32)
        inverse_ref[top:end] = done[:, n:]
        if end < n:
            below = lax.dot_general(
                work_ref[end:, top:end], own, (((1,), (1,)), ((), ())),
                precision=HIGHEST, preferred_element_type=F32,
            )
            work_ref[end:] = work_ref[end:] - jnp.dot(
                below, done, precision=HIGHEST, preferred_element_type=F32
            )


VMEM = pl.BlockSpec(memory_space=pltpu.VMEM)
SMEM = pl.BlockSpec(memory_space=pltpu.SMEM)


def inverse_factor(place, blocks):
    n = blocks[0].shape[1]
    return pl.pallas_call(
        inverse_factor_kernel,
        out_shape=jax.ShapeDtypeStruct((n, n), F32),
        in_specs=[SMEM] + [VMEM] * len(blocks),
        out_specs=VMEM,
        scratch_shapes=[pltpu.VMEM((n, 2 * n), F32)],
        compiler_params=pltpu.CompilerParams(vmem_limit_bytes=16 * MIB),
        cost_estimate=pl.CostEstimate(flops=2**20, bytes_accessed=2**19, transcendentals=0),
        name="inverse_factor",
    )(place, *blocks)


def products_kernel(place_ref, mine_ref, other_ref, own_ref, sketch_ref, both_ref, range_ref):
    half, wide = mine_ref.shape
    ff, rank = sketch_ref.shape
    block = rank // XN
    core, x = place_ref[0], place_ref[1]
    gram = jnp.zeros((rank, rank), F32)
    delta = jnp.zeros((rank, ff), F32)
    for load_ref, at_core in ((mine_ref, core), (other_ref, 1 - core)):
        rows = pl.ds(pl.multiple_of(at_core * half, half), half)
        own = own_ref[rows, :]
        base_sketch = (
            load_ref[:, ff : ff + rank].astype(F32)
            + load_ref[:, ff + rank : ff + 2 * rank].astype(F32)
            + load_ref[:, ff + 2 * rank :].astype(F32)
        )
        range_rows = jnp.dot(own, sketch_ref[...], preferred_element_type=F32) - base_sketch
        range_ref[rows, :] = range_rows
        turned = range_rows.T
        gram += jnp.dot(turned, range_rows, precision=HIGHEST, preferred_element_type=F32)
        base = load_ref[:, :ff]
        for step in range(3):
            part = turned.astype(BF16)
            turned = turned - part.astype(F32)
            delta += jnp.dot(part, own, preferred_element_type=F32)
            delta -= jnp.dot(part, base, preferred_element_type=F32)
    for b in range(XN):
        both_ref[b ^ x, :, :rank] = gram[b * block : (b + 1) * block]
        both_ref[b ^ x, :, rank:] = delta[b * block : (b + 1) * block]


def products(place, mine, other, own, sketch):
    rows, ff = own.shape
    rank = sketch.shape[1]
    return pl.pallas_call(
        products_kernel,
        out_shape=(
            jax.ShapeDtypeStruct((XN, rank // XN, rank + ff), F32),
            jax.ShapeDtypeStruct((rows, rank), F32),
        ),
        in_specs=[SMEM] + [VMEM] * 4,
        out_specs=(VMEM, VMEM),
        compiler_params=pltpu.CompilerParams(vmem_limit_bytes=40 * MIB),
        cost_estimate=pl.CostEstimate(flops=4 * 10**9, bytes_accessed=8 * MIB, transcendentals=0),
        name="products",
    )(place, mine, other, own, sketch)


def per_device(counts, up_weights, sketch):
    rows, ff = up_weights.shape[1:]
    rank = sketch.shape[1]
    piece = rows // 64
    own = up_weights[0].reshape(YN, FN, NN, CN, piece, ff).transpose(3, 0, 2, 1, 4, 5)
    members = CN * YN * NN
    own = own.reshape(members, FN * piece, ff)

    lane = lax.broadcasted_iota(jnp.int32, (members, FN * piece, 128), 2)
    count = counts[0]
    tag = jnp.where(lane == 0, count // 64, jnp.where(lane == 1, count % 64, 0)).astype(BF16)
    got = lax.all_to_all(
        jnp.concatenate([own, tag], axis=2), "exp", 0, 0, axis_index_groups=CYN_GROUPS
    )
    freq = got[:, 0, ff].astype(F32) * 64 + got[:, 0, ff + 1].astype(F32)
    weighted = jnp.sum(freq[:, None, None] * got[:, :, :ff].astype(F32), axis=0)
    freq_sum = jnp.broadcast_to(jnp.sum(freq), (FN, piece, 128))

    sums = lax.all_to_all(
        jnp.concatenate([weighted.reshape(FN, piece, ff), freq_sum], axis=2),
        "exp", 0, 0, axis_index_groups=FAR_GROUPS,
    )
    sums = jnp.sum(sums, axis=0)
    base_rows = sums[:, :ff] / sums[:, ff : ff + 1]
    base_piece = base_rows.astype(BF16)
    sketched = jnp.dot(base_rows, sketch.astype(F32), precision=HIGHEST)

    wide = ff + 3 * rank
    load = jnp.concatenate([base_piece] + parts_of(sketched), axis=1)
    load = lax.all_to_all(
        jnp.broadcast_to(load, (FN, piece, wide)), "exp", 0, 0, axis_index_groups=FAR_GROUPS
    ).reshape(FN * piece, wide)
    load = lax.all_to_all(
        jnp.broadcast_to(load, (YN * NN, FN * piece, wide)),
        "exp", 0, 0, axis_index_groups=YN_GROUPS,
    ).reshape(rows // CN, wide)
    other = lax.ppermute(load, "exp", OTHER_CORE)

    at_core, at_x = lax.axis_index("exp") % CN, lax.axis_index("grp") % XN
    both, range_rows = products(
        jnp.stack([at_core, at_x]), load, other, own.reshape(rows, ff), sketch
    )

    both = both[0] + sum(lax.ppermute(both[k], "grp", ALONG_X[k]) for k in (1, 2, 3))
    gram, delta = both[:, :rank], both[:, rank:]
    gram = gram + lax.ppermute(gram, "grp", OTHER_HALF)
    delta_came = lax.ppermute(delta, "grp", OTHER_HALF)
    inverse = inverse_factor(
        at_x.reshape(1), [gram] + [lax.ppermute(gram, "grp", ALONG_X[k]) for k in (1, 2, 3)]
    )
    inverse, delta_came = lax.optimization_barrier((inverse, delta_came))
    delta = delta + delta_came
    whole = jnp.zeros((XN,) + delta.shape, F32)
    whole = lax.dynamic_update_slice(whole, delta[None], (at_x, 0, 0))
    for k in (1, 2, 3):
        came = lax.ppermute(delta, "grp", ALONG_X[k])
        whole = lax.dynamic_update_slice(whole, came[None], (at_x ^ k, 0, 0))
    coeff = jnp.dot(inverse, whole.reshape(rank, ff), precision=HIGHEST)

    ortho = lax.dot_general(
        range_rows, inverse, (((1,), (1,)), ((), ())), precision=HIGHEST
    )
    basis = ortho * math.sqrt(rows * lax.axis_size("grp"))
    basis = basis.reshape(CN, YN, NN, FN, piece, rank).transpose(1, 3, 2, 0, 4, 5)
    return (base_piece, basis.reshape(1, rows, rank), coeff[None])


def solution(mesh):
    placed = (P("exp"), P("exp", "grp", None), P())
    return jax.shard_map(
        per_device,
        mesh=mesh,
        in_specs=placed,
        out_specs=(P(("grp", "exp"), None), P("exp", "grp", None), P("exp", None, None)),
        check_vma=False,
    )
```

```python
import math

import jax
import jax.numpy as jnp
from jax import lax
from jax.experimental import pallas as pl
from jax.experimental.pallas import tpu as pltpu
from jax.sharding import PartitionSpec as P

F32, BF16 = jnp.float32, jnp.bfloat16
HIGHEST = lax.Precision.HIGHEST
MIB = 2**20

YN, FN, NN, CN, XN = 4, 4, 2, 2, 4


def at(y, far, near, core):
    return y * 16 + (2 * far + near) * 2 + core


CYN_GROUPS = [
    [at(y, f, n, c) for c in range(CN) for y in range(YN) for n in range(NN)] for f in range(FN)
]
YN_GROUPS = [
    [at(y, f, n, c) for y in range(YN) for n in range(NN)] for f in range(FN) for c in range(CN)
]
FAR_GROUPS = [
    [at(y, f, n, c) for f in range(FN)]
    for y in range(YN) for n in range(NN) for c in range(CN)
]
OTHER_CORE = [(i, i ^ 1) for i in range(64)]
OTHER_HALF = [(i, i ^ 4) for i in range(8)]
ALONG_X = [[(i, i ^ k) for i in range(8)] for k in range(XN)]

PANEL = 64


def parts_of(value):
    first = lax.reduce_precision(value, 8, 7)
    rest = value - first
    second = lax.reduce_precision(rest, 8, 7)
    return [first.astype(BF16), second.astype(BF16), (rest - second).astype(BF16)]


def eye(n):
    row, col = (lax.broadcasted_iota(jnp.int32, (n, n), d) for d in (0, 1))
    return jnp.where(row == col, 1.0, 0.0).astype(F32)


def inverse_root(value):
    guess = lax.rsqrt(value)
    return guess * (1.5 - 0.5 * value * guess * guess)


def inverse_factor_of_panel(square):
    n = square.shape[0]
    work = jnp.concatenate([square, eye(n)], axis=1)
    row = lax.broadcasted_iota(jnp.int32, work.shape, 0)
    for j in range(0, n, 2):
        left = jnp.broadcast_to(work[:, j : j + 1], work.shape)
        right = jnp.broadcast_to(work[:, j + 1 : j + 2], work.shape)
        scale = inverse_root(left[j : j + 1])
        cross = left[j + 1 : j + 2] * scale
        scale_next = inverse_root(right[j + 1 : j + 2] - cross * cross)
        top = work[j : j + 1] * scale
        low = (work[j + 1 : j + 2] - cross * top) * scale_next
        left = left * scale
        right = (right - left * cross) * scale_next
        rest = jnp.where(row > j + 1, work - left * top - right * low, work)
        work = jnp.where(row == j, top, jnp.where(row == j + 1, low, rest))
    return work[:, n:]


def inverse_factor_kernel(place_ref, own_ref, *refs):
    came_refs, inverse_ref, work_ref = refs[:-2], refs[-2], refs[-1]
    n = inverse_ref.shape[0]
    block = own_ref.shape[0]
    for k, ref in enumerate((own_ref,) + came_refs):
        start = pl.multiple_of((place_ref[0] ^ k) * block, block)
        work_ref[pl.ds(start, block), :n] = ref[...]
    work_ref[:, n:] = eye(n)
    for top in range(0, n, PANEL):
        end = top + PANEL
        own = inverse_factor_of_panel(work_ref[top:end, top:end])
        done = jnp.dot(own, work_ref[top:end], precision=HIGHEST, preferred_element_type=F32)
        inverse_ref[top:end] = done[:, n:]
        if end < n:
            below = lax.dot_general(
                work_ref[end:, top:end], own, (((1,), (1,)), ((), ())),
                precision=HIGHEST, preferred_element_type=F32,
            )
            work_ref[end:] = work_ref[end:] - jnp.dot(
                below, done, precision=HIGHEST, preferred_element_type=F32
            )


VMEM = pl.BlockSpec(memory_space=pltpu.VMEM)
SMEM = pl.BlockSpec(memory_space=pltpu.SMEM)


def inverse_factor(place, blocks):
    n = blocks[0].shape[1]
    return pl.pallas_call(
        inverse_factor_kernel,
        out_shape=jax.ShapeDtypeStruct((n, n), F32),
        in_specs=[SMEM] + [VMEM] * len(blocks),
        out_specs=VMEM,
        scratch_shapes=[pltpu.VMEM((n, 2 * n), F32)],
        compiler_params=pltpu.CompilerParams(vmem_limit_bytes=16 * MIB),
        cost_estimate=pl.CostEstimate(flops=2**29, bytes_accessed=2**10, transcendentals=0),
        name="inverse_factor",
    )(place, *blocks)


def products_kernel(place_ref, mine_ref, other_ref, own_ref, sketch_ref, both_ref, range_ref):
    half, wide = mine_ref.shape
    ff, rank = sketch_ref.shape
    block = rank // XN
    core, x = place_ref[0], place_ref[1]
    gram = jnp.zeros((rank, rank), F32)
    delta = jnp.zeros((rank, ff), F32)
    for load_ref, at_core in ((mine_ref, core), (other_ref, 1 - core)):
        rows = pl.ds(pl.multiple_of(at_core * half, half), half)
        own = own_ref[rows, :]
        base_sketch = (
            load_ref[:, ff : ff + rank].astype(F32)
            + load_ref[:, ff + rank : ff + 2 * rank].astype(F32)
            + load_ref[:, ff + 2 * rank :].astype(F32)
        )
        range_rows = jnp.dot(own, sketch_ref[...], preferred_element_type=F32) - base_sketch
        range_ref[rows, :] = range_rows
        turned = range_rows.T
        gram += jnp.dot(turned, range_rows, precision=HIGHEST, preferred_element_type=F32)
        base = load_ref[:, :ff]
        for step in range(3):
            part = turned.astype(BF16)
            turned = turned - part.astype(F32)
            delta += jnp.dot(part, own, preferred_element_type=F32)
            delta -= jnp.dot(part, base, preferred_element_type=F32)
    for b in range(XN):
        both_ref[b ^ x, :, :rank] = gram[b * block : (b + 1) * block]
        both_ref[b ^ x, :, rank:] = delta[b * block : (b + 1) * block]


def products(place, mine, other, own, sketch):
    rows, ff = own.shape
    rank = sketch.shape[1]
    return pl.pallas_call(
        products_kernel,
        out_shape=(
            jax.ShapeDtypeStruct((XN, rank // XN, rank + ff), F32),
            jax.ShapeDtypeStruct((rows, rank), F32),
        ),
        in_specs=[SMEM] + [VMEM] * 4,
        out_specs=(VMEM, VMEM),
        compiler_params=pltpu.CompilerParams(vmem_limit_bytes=40 * MIB),
        cost_estimate=pl.CostEstimate(flops=4 * 10**9, bytes_accessed=8 * MIB, transcendentals=0),
        name="products",
    )(place, mine, other, own, sketch)


def per_device(counts, up_weights, sketch):
    rows, ff = up_weights.shape[1:]
    rank = sketch.shape[1]
    piece = rows // 64
    own = up_weights[0].reshape(YN, FN, NN, CN, piece, ff).transpose(3, 0, 2, 1, 4, 5)
    members = CN * YN * NN
    own = own.reshape(members, FN * piece, ff)

    lane = lax.broadcasted_iota(jnp.int32, (members, FN * piece, 128), 2)
    count = counts[0]
    tag = jnp.where(lane == 0, count // 64, jnp.where(lane == 1, count % 64, 0)).astype(BF16)
    got = lax.all_to_all(
        jnp.concatenate([own, tag], axis=2), "exp", 0, 0, axis_index_groups=CYN_GROUPS
    )
    freq = got[:, 0, ff].astype(F32) * 64 + got[:, 0, ff + 1].astype(F32)
    weighted = jnp.sum(freq[:, None, None] * got[:, :, :ff].astype(F32), axis=0)
    freq_sum = jnp.broadcast_to(jnp.sum(freq), (FN, piece, 128))

    sums = lax.all_to_all(
        jnp.concatenate([weighted.reshape(FN, piece, ff), freq_sum], axis=2),
        "exp", 0, 0, axis_index_groups=FAR_GROUPS,
    )
    sums = jnp.sum(sums, axis=0)
    base_rows = sums[:, :ff] / sums[:, ff : ff + 1]
    base_piece = base_rows.astype(BF16)
    sketched = jnp.dot(base_rows, sketch.astype(F32), precision=HIGHEST)

    wide = ff + 3 * rank
    load = jnp.concatenate([base_piece] + parts_of(sketched), axis=1)
    load = lax.all_to_all(
        jnp.broadcast_to(load, (FN, piece, wide)), "exp", 0, 0, axis_index_groups=FAR_GROUPS
    ).reshape(FN * piece, wide)
    load = lax.all_to_all(
        jnp.broadcast_to(load, (YN * NN, FN * piece, wide)),
        "exp", 0, 0, axis_index_groups=YN_GROUPS,
    ).reshape(rows // CN, wide)
    other = lax.ppermute(load, "exp", OTHER_CORE)

    at_core, at_x = lax.axis_index("exp") % CN, lax.axis_index("grp") % XN
    both, range_rows = products(
        jnp.stack([at_core, at_x]), load, other, own.reshape(rows, ff), sketch
    )

    both = both[0] + sum(lax.ppermute(both[k], "grp", ALONG_X[k]) for k in (2, 3, 1))
    gram, delta = both[:, :rank], both[:, rank:]
    gram = gram + lax.ppermute(gram, "grp", OTHER_HALF)
    delta_came = lax.ppermute(delta, "grp", OTHER_HALF)
    inverse = inverse_factor(
        at_x.reshape(1), [gram] + [lax.ppermute(gram, "grp", ALONG_X[k]) for k in (1, 2, 3)]
    )
    inverse, delta_came = lax.optimization_barrier((inverse, delta_came))
    delta = delta + delta_came
    whole = jnp.zeros((XN,) + delta.shape, F32)
    whole = lax.dynamic_update_slice(whole, delta[None], (at_x, 0, 0))
    for k in (2, 3, 1):
        came = lax.ppermute(delta, "grp", ALONG_X[k])
        whole = lax.dynamic_update_slice(whole, came[None], (at_x ^ k, 0, 0))
    coeff = jnp.dot(inverse, whole.reshape(rank, ff), precision=HIGHEST)

    ortho = lax.dot_general(
        range_rows, inverse, (((1,), (1,)), ((), ())), precision=HIGHEST
    )
    basis = ortho * math.sqrt(rows * lax.axis_size("grp"))
    basis = basis.reshape(CN, YN, NN, FN, piece, rank).transpose(1, 3, 2, 0, 4, 5)
    return (base_piece, basis.reshape(1, rows, rank), coeff[None])


def solution(mesh):
    placed = (P("exp"), P("exp", "grp", None), P())
    return jax.shard_map(
        per_device,
        mesh=mesh,
        in_specs=placed,
        out_specs=(P(("grp", "exp"), None), P("exp", "grp", None), P("exp", None, None)),
        check_vma=False,
    )
```

```python
import math

import jax
import jax.numpy as jnp
from jax import lax
from jax.experimental import pallas as pl
from jax.experimental.pallas import tpu as pltpu
from jax.sharding import PartitionSpec as P

F32, BF16 = jnp.float32, jnp.bfloat16
HIGHEST = lax.Precision.HIGHEST
MIB = 2**20

YN, FN, NN, CN, XN = 4, 4, 2, 2, 4


def at(y, far, near, core):
    return y * 16 + (2 * far + near) * 2 + core


CYN_GROUPS = [
    [at(y, f, n, c) for c in range(CN) for y in range(YN) for n in range(NN)] for f in range(FN)
]
YN_GROUPS = [
    [at(y, f, n, c) for y in range(YN) for n in range(NN)] for f in range(FN) for c in range(CN)
]
FAR_GROUPS = [
    [at(y, f, n, c) for f in range(FN)]
    for y in range(YN) for n in range(NN) for c in range(CN)
]
OTHER_CORE = [(i, i ^ 1) for i in range(64)]
OTHER_HALF = [(i, i ^ 4) for i in range(8)]
ALONG_X = [[(i, i ^ k) for i in range(8)] for k in range(XN)]

PANEL = 64
TOP_POWER = 13


def parts_of(value):
    first = lax.reduce_precision(value, 8, 7)
    rest = value - first
    second = lax.reduce_precision(rest, 8, 7)
    return [first.astype(BF16), second.astype(BF16), (rest - second).astype(BF16)]


def eye(n):
    row, col = (lax.broadcasted_iota(jnp.int32, (n, n), d) for d in (0, 1))
    return jnp.where(row == col, 1.0, 0.0).astype(F32)


def inverse_root(value):
    guess = lax.rsqrt(value)
    return guess * (1.5 - 0.5 * value * guess * guess)


def inverse_factor_of_panel(square):
    n = square.shape[0]
    work = jnp.concatenate([square, eye(n)], axis=1)
    row = lax.broadcasted_iota(jnp.int32, work.shape, 0)
    for j in range(0, n, 2):
        left = jnp.broadcast_to(work[:, j : j + 1], work.shape)
        right = jnp.broadcast_to(work[:, j + 1 : j + 2], work.shape)
        scale = inverse_root(left[j : j + 1])
        cross = left[j + 1 : j + 2] * scale
        scale_next = inverse_root(right[j + 1 : j + 2] - cross * cross)
        top = work[j : j + 1] * scale
        low = (work[j + 1 : j + 2] - cross * top) * scale_next
        left = left * scale
        right = (right - left * cross) * scale_next
        rest = jnp.where(row > j + 1, work - left * top - right * low, work)
        work = jnp.where(row == j, top, jnp.where(row == j + 1, low, rest))
    return work[:, n:]


def inverse_factor_kernel(place_ref, own_ref, *refs):
    came_refs, inverse_ref, work_ref = refs[:-2], refs[-2], refs[-1]
    n = inverse_ref.shape[0]
    block = own_ref.shape[0]
    for k, ref in enumerate((own_ref,) + came_refs):
        start = pl.multiple_of((place_ref[0] ^ k) * block, block)
        work_ref[pl.ds(start, block), :n] = ref[...]
    work_ref[:, n:] = eye(n)
    for top in range(0, n, PANEL):
        end = top + PANEL
        own = inverse_factor_of_panel(work_ref[top:end, top:end])
        done = jnp.dot(own, work_ref[top:end], precision=HIGHEST, preferred_element_type=F32)
        inverse_ref[top:end] = done[:, n:]
        if end < n:
            below = lax.dot_general(
                work_ref[end:, top:end], own, (((1,), (1,)), ((), ())),
                precision=HIGHEST, preferred_element_type=F32,
            )
            work_ref[end:] = work_ref[end:] - jnp.dot(
                below, done, precision=HIGHEST, preferred_element_type=F32
            )


VMEM = pl.BlockSpec(memory_space=pltpu.VMEM)
SMEM = pl.BlockSpec(memory_space=pltpu.SMEM)


def inverse_factor(place, blocks):
    n = blocks[0].shape[1]
    return pl.pallas_call(
        inverse_factor_kernel,
        out_shape=jax.ShapeDtypeStruct((n, n), F32),
        in_specs=[SMEM] + [VMEM] * len(blocks),
        out_specs=VMEM,
        scratch_shapes=[pltpu.VMEM((n, 2 * n), F32)],
        compiler_params=pltpu.CompilerParams(vmem_limit_bytes=16 * MIB),
        cost_estimate=pl.CostEstimate(flops=2**29, bytes_accessed=2**10, transcendentals=0),
        name="inverse_factor",
    )(place, *blocks)


def products_kernel(place_ref, mine_ref, other_ref, own_ref, sketch_ref, both_ref, range_ref):
    half, wide = mine_ref.shape
    ff, rank = sketch_ref.shape
    block, slab = rank // XN, ff // XN
    core, x = place_ref[0], place_ref[1]
    gram = jnp.zeros((rank, rank), F32)
    delta = jnp.zeros((rank, ff), F32)
    for load_ref, at_core in ((mine_ref, core), (other_ref, 1 - core)):
        rows = pl.ds(pl.multiple_of(at_core * half, half), half)
        own = own_ref[rows, :]
        base_sketch = (
            load_ref[:, ff : ff + rank].astype(F32)
            + load_ref[:, ff + rank : ff + 2 * rank].astype(F32)
            + load_ref[:, ff + 2 * rank :].astype(F32)
        )
        range_rows = jnp.dot(own, sketch_ref[...], preferred_element_type=F32) - base_sketch
        range_ref[rows, :] = range_rows
        turned = range_rows.T
        gram += jnp.dot(turned, range_rows, precision=HIGHEST, preferred_element_type=F32)
        base = load_ref[:, :ff]
        for step in range(3):
            part = turned.astype(BF16)
            turned = turned - part.astype(F32)
            delta += jnp.dot(part, own, preferred_element_type=F32)
            delta -= jnp.dot(part, base, preferred_element_type=F32)
    both_ref[:, rank:, rank:] = jnp.zeros((XN, block, slab - rank), F32)
    for b in range(XN):
        both_ref[b ^ x, :rank, :] = delta[:, b * slab : (b + 1) * slab]
        both_ref[b ^ x, rank:, :rank] = gram[b * block : (b + 1) * block]


def products(place, mine, other, own, sketch):
    rows, ff = own.shape
    rank = sketch.shape[1]
    return pl.pallas_call(
        products_kernel,
        out_shape=(
            jax.ShapeDtypeStruct((XN, rank + rank // XN, ff // XN), F32),
            jax.ShapeDtypeStruct((rows, rank), F32),
        ),
        in_specs=[SMEM] + [VMEM] * 4,
        out_specs=(VMEM, VMEM),
        compiler_params=pltpu.CompilerParams(vmem_limit_bytes=40 * MIB),
        cost_estimate=pl.CostEstimate(flops=4 * 10**9, bytes_accessed=8 * MIB, transcendentals=0),
        name="products",
    )(place, mine, other, own, sketch)


def finished_kernel(inverse_ref, own_ref, came_ref, out_ref):
    rank = inverse_ref.shape[0]
    values = jnp.dot(
        inverse_ref[...], own_ref[...] + came_ref[...],
        precision=HIGHEST, preferred_element_type=F32,
    )
    top = jnp.max(jnp.max(jnp.abs(values), axis=0, keepdims=True), axis=1, keepdims=True)
    power = jnp.floor(jnp.log(jnp.maximum(top, 1e-30)) * (1 / math.log(2)))
    out_ref[:rank] = values * jnp.exp2(TOP_POWER - power)
    out_ref[rank:] = jnp.broadcast_to(power, (out_ref.shape[0] - rank, out_ref.shape[1]))


def finished(inverse, own, came):
    rank, slab = own.shape
    return pl.pallas_call(
        finished_kernel,
        out_shape=jax.ShapeDtypeStruct((rank + 16, slab), F32),
        in_specs=[VMEM] * 3,
        out_specs=VMEM,
        compiler_params=pltpu.CompilerParams(vmem_limit_bytes=16 * MIB),
        name="finished",
    )(inverse, own, came)


def assembled_kernel(place_ref, *refs):
    blocks, out_ref, sems = refs[:XN], refs[XN], refs[XN + 1]
    slab = blocks[0].shape[1]
    copies = []
    for k, ref in enumerate(blocks):
        start = pl.multiple_of((place_ref[0] ^ k) * slab, slab)
        copies.append(pltpu.make_async_copy(ref, out_ref.at[:, pl.ds(start, slab)], sems.at[k]))
    for copy in copies:
        copy.start()
    for copy in copies:
        copy.wait()


def assembled(place, blocks):
    rank, slab = blocks[0].shape
    return pl.pallas_call(
        assembled_kernel,
        out_shape=jax.ShapeDtypeStruct((rank, XN * slab), F32),
        in_specs=[SMEM] + [VMEM] * XN,
        out_specs=pl.BlockSpec(memory_space=pl.ANY),
        scratch_shapes=[pltpu.SemaphoreType.DMA((XN,))],
        compiler_params=pltpu.CompilerParams(vmem_limit_bytes=16 * MIB),
        name="assembled",
    )(place, *blocks)


def per_device(counts, up_weights, sketch):
    rows, ff = up_weights.shape[1:]
    rank = sketch.shape[1]
    piece = rows // 64
    own = up_weights[0].reshape(YN, FN, NN, CN, piece, ff).transpose(3, 0, 2, 1, 4, 5)
    members = CN * YN * NN
    own = own.reshape(members, FN * piece, ff)

    lane = lax.broadcasted_iota(jnp.int32, (members, FN * piece, 128), 2)
    count = counts[0]
    tag = jnp.where(lane == 0, count // 64, jnp.where(lane == 1, count % 64, 0)).astype(BF16)
    got = lax.all_to_all(
        jnp.concatenate([own, tag], axis=2), "exp", 0, 0, axis_index_groups=CYN_GROUPS
    )
    freq = got[:, 0, ff].astype(F32) * 64 + got[:, 0, ff + 1].astype(F32)
    weighted = jnp.sum(freq[:, None, None] * got[:, :, :ff].astype(F32), axis=0)
    freq_sum = jnp.broadcast_to(jnp.sum(freq), (FN, piece, 128))

    sums = lax.all_to_all(
        jnp.concatenate([weighted.reshape(FN, piece, ff), freq_sum], axis=2),
        "exp", 0, 0, axis_index_groups=FAR_GROUPS,
    )
    sums = jnp.sum(sums, axis=0)
    base_rows = sums[:, :ff] / sums[:, ff : ff + 1]
    base_piece = base_rows.astype(BF16)
    sketched = jnp.dot(base_rows, sketch.astype(F32), precision=HIGHEST)

    wide = ff + 3 * rank
    load = jnp.concatenate([base_piece] + parts_of(sketched), axis=1)
    load = lax.all_to_all(
        jnp.broadcast_to(load, (FN, piece, wide)), "exp", 0, 0, axis_index_groups=FAR_GROUPS
    ).reshape(FN * piece, wide)
    load = lax.all_to_all(
        jnp.broadcast_to(load, (YN * NN, FN * piece, wide)),
        "exp", 0, 0, axis_index_groups=YN_GROUPS,
    ).reshape(rows // CN, wide)
    other = lax.ppermute(load, "exp", OTHER_CORE)

    at_core, at_x = lax.axis_index("exp") % CN, lax.axis_index("grp") % XN
    both, range_rows = products(
        jnp.stack([at_core, at_x]), load, other, own.reshape(rows, ff), sketch
    )

    both = both[0] + sum(lax.ppermute(both[k], "grp", ALONG_X[k]) for k in (2, 3, 1))
    gram, delta = both[rank:, :rank], both[:rank]
    gram = gram + lax.ppermute(gram, "grp", OTHER_HALF)
    delta_came = lax.ppermute(delta, "grp", OTHER_HALF)
    place = at_x.reshape(1)
    inverse = inverse_factor(
        place, [gram] + [lax.ppermute(gram, "grp", ALONG_X[k]) for k in (1, 2, 3)]
    )
    inverse, delta_came = lax.optimization_barrier((inverse, delta_came))
    block = lax.optimization_barrier(finished(inverse, delta, delta_came).astype(jnp.float16))
    blocks = {0: block}
    for k in (2, 3, 1):
        blocks[k] = lax.ppermute(block, "grp", ALONG_X[k])
    blocks = {k: block.astype(F32) for k, block in blocks.items()}
    coeff = assembled(
        place,
        [blocks[k][:rank] * jnp.exp2(blocks[k][rank : rank + 1, :1] - TOP_POWER) for k in range(XN)],
    )

    ortho = lax.dot_general(
        range_rows, inverse, (((1,), (1,)), ((), ())), precision=HIGHEST
    )
    basis = ortho * math.sqrt(rows * lax.axis_size("grp"))
    basis = basis.reshape(CN, YN, NN, FN, piece, rank).transpose(1, 3, 2, 0, 4, 5)
    return (base_piece, basis.reshape(1, rows, rank), coeff[None])


def solution(mesh):
    placed = (P("exp"), P("exp", "grp", None), P())
    return jax.shard_map(
        per_device,
        mesh=mesh,
        in_specs=placed,
        out_specs=(P(("grp", "exp"), None), P("exp", "grp", None), P("exp", None, None)),
        check_vma=False,
    )
```

```python
import math

import jax
import jax.numpy as jnp
from jax import lax
from jax.experimental import pallas as pl
from jax.experimental.pallas import tpu as pltpu
from jax.sharding import PartitionSpec as P

F32, BF16 = jnp.float32, jnp.bfloat16
HIGHEST = lax.Precision.HIGHEST
MIB = 2**20

YN, FN, NN, CN, XN = 4, 4, 2, 2, 4


def at(y, far, near, core):
    return y * 16 + (2 * far + near) * 2 + core


CYN_GROUPS = [
    [at(y, f, n, c) for c in range(CN) for y in range(YN) for n in range(NN)] for f in range(FN)
]
YN_GROUPS = [
    [at(y, f, n, c) for y in range(YN) for n in range(NN)] for f in range(FN) for c in range(CN)
]
FAR_GROUPS = [
    [at(y, f, n, c) for f in range(FN)]
    for y in range(YN) for n in range(NN) for c in range(CN)
]
OTHER_CORE = [(i, i ^ 1) for i in range(64)]
OTHER_HALF = [(i, i ^ 4) for i in range(8)]
ALONG_X = [[(i, i ^ k) for i in range(8)] for k in range(XN)]

PANEL = 64
TOP_POWER = 13
FACTOR_COST = 2**29


def parts_of(value):
    first = lax.reduce_precision(value, 8, 7)
    rest = value - first
    second = lax.reduce_precision(rest, 8, 7)
    return [first.astype(BF16), second.astype(BF16), (rest - second).astype(BF16)]


def eye(n):
    row, col = (lax.broadcasted_iota(jnp.int32, (n, n), d) for d in (0, 1))
    return jnp.where(row == col, 1.0, 0.0).astype(F32)


def inverse_root(value):
    guess = lax.rsqrt(value)
    return guess * (1.5 - 0.5 * value * guess * guess)


def inverse_factor_of_panel(square):
    n = square.shape[0]
    work = jnp.concatenate([square, eye(n)], axis=1)
    row = lax.broadcasted_iota(jnp.int32, work.shape, 0)
    for j in range(0, n, 2):
        left = jnp.broadcast_to(work[:, j : j + 1], work.shape)
        right = jnp.broadcast_to(work[:, j + 1 : j + 2], work.shape)
        scale = inverse_root(left[j : j + 1])
        cross = left[j + 1 : j + 2] * scale
        scale_next = inverse_root(right[j + 1 : j + 2] - cross * cross)
        top = work[j : j + 1] * scale
        low = (work[j + 1 : j + 2] - cross * top) * scale_next
        left = left * scale
        right = (right - left * cross) * scale_next
        rest = jnp.where(row > j + 1, work - left * top - right * low, work)
        work = jnp.where(row == j, top, jnp.where(row == j + 1, low, rest))
    return work[:, n:]


def inverse_factor_kernel(place_ref, own_ref, *refs):
    came_refs, inverse_ref, work_ref = refs[:-2], refs[-2], refs[-1]
    n = inverse_ref.shape[0]
    block = n // XN
    held = []
    for ref in (own_ref,) + came_refs:
        packed = ref[...]
        width = packed.shape[1] // 2
        held.append(jnp.concatenate([packed[:, :width], packed[:, width:]], axis=0))
    for x in range(XN):

        @pl.when(place_ref[0] == x)
        def _():
            for b in range(XN):
                rows = pl.ds(b * block, block)
                for j in range(XN - 1):
                    c = (b + j) % XN
                    part = held[b ^ x][:, j * block : (j + 1) * block]
                    work_ref[rows, c * block : (c + 1) * block] = part
                c = (b + XN - 1) % XN
                work_ref[rows, c * block : (c + 1) * block] = held[c ^ x][:, block : 2 * block].T

    work_ref[:, n:] = eye(n)
    for top in range(0, n, PANEL):
        end = top + PANEL
        own = inverse_factor_of_panel(work_ref[top:end, top:end])
        done = jnp.dot(own, work_ref[top:end], precision=HIGHEST, preferred_element_type=F32)
        inverse_ref[top:end] = done[:, n:]
        if end < n:
            below = lax.dot_general(
                work_ref[end:, top:end], own, (((1,), (1,)), ((), ())),
                precision=HIGHEST, preferred_element_type=F32,
            )
            work_ref[end:] = work_ref[end:] - jnp.dot(
                below, done, precision=HIGHEST, preferred_element_type=F32
            )


VMEM = pl.BlockSpec(memory_space=pltpu.VMEM)
SMEM = pl.BlockSpec(memory_space=pltpu.SMEM)


def inverse_factor(place, blocks, n):
    return pl.pallas_call(
        inverse_factor_kernel,
        out_shape=jax.ShapeDtypeStruct((n, n), F32),
        in_specs=[SMEM] + [VMEM] * len(blocks),
        out_specs=VMEM,
        scratch_shapes=[pltpu.VMEM((n, 2 * n), F32)],
        compiler_params=pltpu.CompilerParams(vmem_limit_bytes=16 * MIB),
        cost_estimate=pl.CostEstimate(flops=FACTOR_COST, bytes_accessed=2**10, transcendentals=0),
        name="inverse_factor",
    )(place, *blocks)


def range_product(turned, own, base):
    total = None
    for step in range(3):
        part = turned.astype(BF16)
        turned = turned - part.astype(F32)
        term = jnp.dot(part, own, preferred_element_type=F32)
        term -= jnp.dot(part, base, preferred_element_type=F32)
        total = term if total is None else total + term
    return total


def first_products_kernel(place_ref, mine_ref, other_ref, own_ref, sketch_ref, out_ref, range_ref):
    half = mine_ref.shape[0]
    ff, rank = sketch_ref.shape
    block, slab, chunk = rank // XN, ff // XN, rank // 2
    core, x = place_ref[0], place_ref[1]
    gram = jnp.zeros((rank, rank), F32)
    delta = jnp.zeros((chunk, ff), F32)
    for load_ref, at_core in ((mine_ref, core), (other_ref, 1 - core)):
        rows = pl.ds(pl.multiple_of(at_core * half, half), half)
        own = own_ref[rows, :]
        base_sketch = (
            load_ref[:, ff : ff + rank].astype(F32)
            + load_ref[:, ff + rank : ff + 2 * rank].astype(F32)
            + load_ref[:, ff + 2 * rank :].astype(F32)
        )
        range_rows = jnp.dot(own, sketch_ref[...], preferred_element_type=F32) - base_sketch
        range_ref[rows, :] = range_rows
        turned = range_rows.T
        gram += jnp.dot(turned, range_rows, precision=HIGHEST, preferred_element_type=F32)
        delta += range_product(turned[:chunk], own, load_ref[:, :ff])
    for b in range(XN):
        mine = gram[b * block : (b + 1) * block]
        kept = jnp.concatenate(
            [mine[:, (b + j) % XN * block :][:, :block] for j in range(XN - 1)], axis=1
        )
        packed = jnp.concatenate([kept[: block // 2], kept[block // 2 :]], axis=1)
        out_ref[b ^ x, : block // 2, :] = packed
        out_ref[b ^ x, block // 2 :, :] = delta[:, b * slab : (b + 1) * slab]


def first_products(place, mine, other, own, sketch):
    rows, ff = own.shape
    rank = sketch.shape[1]
    return pl.pallas_call(
        first_products_kernel,
        out_shape=(
            jax.ShapeDtypeStruct((XN, rank // XN // 2 + rank // 2, ff // XN), F32),
            jax.ShapeDtypeStruct((rows, rank), F32),
        ),
        in_specs=[SMEM] + [VMEM] * 4,
        out_specs=(VMEM, VMEM),
        compiler_params=pltpu.CompilerParams(vmem_limit_bytes=40 * MIB),
        cost_estimate=pl.CostEstimate(flops=3 * 10**9, bytes_accessed=2**10, transcendentals=0),
        name="first_products",
    )(place, mine, other, own, sketch)


def second_products_kernel(place_ref, mine_ref, other_ref, own_ref, range_ref, out_ref):
    half = mine_ref.shape[0]
    ff, rank = own_ref.shape[1], range_ref.shape[1]
    slab, chunk = ff // XN, rank // 2
    core, x = place_ref[0], place_ref[1]
    delta = jnp.zeros((chunk, ff), F32)
    for load_ref, at_core in ((mine_ref, core), (other_ref, 1 - core)):
        rows = pl.ds(pl.multiple_of(at_core * half, half), half)
        delta += range_product(range_ref[rows, chunk:].T, own_ref[rows, :], load_ref[:, :ff])
    for b in range(XN):
        out_ref[b ^ x] = delta[:, b * slab : (b + 1) * slab]


def second_products(place, mine, other, own, range_rows):
    ff, rank = own.shape[1], range_rows.shape[1]
    return pl.pallas_call(
        second_products_kernel,
        out_shape=jax.ShapeDtypeStruct((XN, rank // 2, ff // XN), F32),
        in_specs=[SMEM] + [VMEM] * 4,
        out_specs=VMEM,
        compiler_params=pltpu.CompilerParams(vmem_limit_bytes=40 * MIB),
        cost_estimate=pl.CostEstimate(flops=2 * 10**9, bytes_accessed=2**10, transcendentals=0),
        name="second_products",
    )(place, mine, other, own, range_rows)


def finished_kernel(inverse_ref, *refs):
    out_ref = refs[-1]
    rank = inverse_ref.shape[0]
    chunk = rank // 2
    values = sum(
        jnp.dot(
            inverse_ref[:, i * chunk : (i + 1) * chunk], refs[2 * i][...] + refs[2 * i + 1][...],
            precision=HIGHEST, preferred_element_type=F32,
        )
        for i in range(2)
    )
    top = jnp.max(jnp.max(jnp.abs(values), axis=0, keepdims=True), axis=1, keepdims=True)
    power = jnp.floor(jnp.log(jnp.maximum(top, 1e-30)) * (1 / math.log(2)))
    out_ref[:rank] = values * jnp.exp2(TOP_POWER - power)
    out_ref[rank:] = jnp.broadcast_to(power, (out_ref.shape[0] - rank, out_ref.shape[1]))


def finished(inverse, chunks):
    rank, slab = inverse.shape[0], chunks[0].shape[1]
    return pl.pallas_call(
        finished_kernel,
        out_shape=jax.ShapeDtypeStruct((rank + 16, slab), F32),
        in_specs=[VMEM] * (1 + len(chunks)),
        out_specs=VMEM,
        compiler_params=pltpu.CompilerParams(vmem_limit_bytes=16 * MIB),
        name="finished",
    )(inverse, *chunks)


def assembled_kernel(place_ref, *refs):
    blocks, (out_ref, held_ref, sems) = refs[:XN], refs[XN:]
    rank, slab = held_ref.shape[1:]
    copies = []
    for k, ref in enumerate(blocks):
        held_ref[k] = ref[:rank] * jnp.exp2(ref[rank : rank + 1] - TOP_POWER)
        start = pl.multiple_of((place_ref[0] ^ k) * slab, slab)
        copy = pltpu.make_async_copy(
            held_ref.at[k], out_ref.at[:, pl.ds(start, slab)], sems.at[k]
        )
        copy.start()
        copies.append(copy)
    for copy in copies:
        copy.wait()


def assembled(place, blocks):
    rank, slab = blocks[0].shape[0] - 16, blocks[0].shape[1]
    return pl.pallas_call(
        assembled_kernel,
        out_shape=jax.ShapeDtypeStruct((rank, XN * slab), F32),
        in_specs=[SMEM] + [VMEM] * XN,
        out_specs=pl.BlockSpec(memory_space=pl.ANY),
        scratch_shapes=[pltpu.VMEM((XN, rank, slab), F32), pltpu.SemaphoreType.DMA((XN,))],
        compiler_params=pltpu.CompilerParams(vmem_limit_bytes=16 * MIB),
        name="assembled",
    )(place, *blocks)


def per_device(counts, up_weights, sketch):
    rows, ff = up_weights.shape[1:]
    rank = sketch.shape[1]
    piece = rows // 64
    own = up_weights[0].reshape(YN, FN, NN, CN, piece, ff).transpose(3, 0, 2, 1, 4, 5)
    members = CN * YN * NN
    own = own.reshape(members, FN * piece, ff)

    lane = lax.broadcasted_iota(jnp.int32, (members, FN * piece, 128), 2)
    count = counts[0]
    tag = jnp.where(lane == 0, count // 64, jnp.where(lane == 1, count % 64, 0)).astype(BF16)
    got = lax.all_to_all(
        jnp.concatenate([own, tag], axis=2), "exp", 0, 0, axis_index_groups=CYN_GROUPS
    )
    freq = got[:, 0, ff].astype(F32) * 64 + got[:, 0, ff + 1].astype(F32)
    weighted = jnp.sum(freq[:, None, None] * got[:, :, :ff].astype(F32), axis=0)
    freq_sum = jnp.broadcast_to(jnp.sum(freq), (FN, piece, 128))

    sums = lax.all_to_all(
        jnp.concatenate([weighted.reshape(FN, piece, ff), freq_sum], axis=2),
        "exp", 0, 0, axis_index_groups=FAR_GROUPS,
    )
    sums = jnp.sum(sums, axis=0)
    base_rows = sums[:, :ff] / sums[:, ff : ff + 1]
    base_piece = base_rows.astype(BF16)
    sketched = jnp.dot(base_rows, sketch.astype(F32), precision=HIGHEST)

    wide = ff + 3 * rank
    load = jnp.concatenate([base_piece] + parts_of(sketched), axis=1)
    load = lax.all_to_all(
        jnp.broadcast_to(load, (FN, piece, wide)), "exp", 0, 0, axis_index_groups=FAR_GROUPS
    ).reshape(FN * piece, wide)
    load = lax.all_to_all(
        jnp.broadcast_to(load, (YN * NN, FN * piece, wide)),
        "exp", 0, 0, axis_index_groups=YN_GROUPS,
    ).reshape(rows // CN, wide)
    other = lax.ppermute(load, "exp", OTHER_CORE)

    at_core, at_x = lax.axis_index("exp") % CN, lax.axis_index("grp") % XN
    place, own = jnp.stack([at_core, at_x]), own.reshape(rows, ff)

    def along_x(blocks):
        return [blocks[0]] + [lax.ppermute(blocks[k], "grp", ALONG_X[k]) for k in (2, 3, 1)]

    first, range_rows = first_products(place, load, other, own, sketch)
    first = along_x(first)
    second = along_x(second_products(place, load, other, own, range_rows))
    first = sum(first)
    packed = rank // XN // 2
    gram, first = first[:packed], first[packed:]
    gram_came = lax.ppermute(gram, "grp", OTHER_HALF)
    _, second = lax.optimization_barrier((gram_came, second))
    gram, second = gram + gram_came, sum(second)
    chunks = [first, lax.ppermute(first, "grp", OTHER_HALF)]
    chunks += [second, lax.ppermute(second, "grp", OTHER_HALF)]
    inverse = inverse_factor(
        at_x.reshape(1),
        [gram] + [lax.ppermute(gram, "grp", ALONG_X[k]) for k in (1, 2, 3)],
        rank,
    )
    inverse, chunks = lax.optimization_barrier((inverse, chunks))
    block = lax.optimization_barrier(finished(inverse, chunks).astype(jnp.float16))
    blocks = {0: block}
    for k in (2, 3, 1):
        blocks[k] = lax.ppermute(block, "grp", ALONG_X[k])
    coeff = assembled(at_x.reshape(1), [blocks[k].astype(F32) for k in range(XN)])

    ortho = lax.dot_general(
        range_rows, inverse, (((1,), (1,)), ((), ())), precision=HIGHEST
    )
    basis = ortho * math.sqrt(rows * lax.axis_size("grp"))
    basis = basis.reshape(CN, YN, NN, FN, piece, rank).transpose(1, 3, 2, 0, 4, 5)
    return (base_piece, basis.reshape(1, rows, rank), coeff[None])


def solution(mesh):
    placed = (P("exp"), P("exp", "grp", None), P())
    return jax.shard_map(
        per_device,
        mesh=mesh,
        in_specs=placed,
        out_specs=(P(("grp", "exp"), None), P("exp", "grp", None), P("exp", None, None)),
        check_vma=False,
    )
```

```python
import math

import jax
import jax.numpy as jnp
from jax import lax
from jax.experimental import pallas as pl
from jax.experimental.pallas import tpu as pltpu
from jax.sharding import PartitionSpec as P

F32, BF16 = jnp.float32, jnp.bfloat16
HIGHEST = lax.Precision.HIGHEST
MIB = 2**20

YN, FN, NN, CN, XN = 4, 4, 2, 2, 4


def at(y, far, near, core):
    return y * 16 + (2 * far + near) * 2 + core


CYN_GROUPS = [
    [at(y, f, n, c) for c in range(CN) for y in range(YN) for n in range(NN)] for f in range(FN)
]
YN_GROUPS = [
    [at(y, f, n, c) for y in range(YN) for n in range(NN)] for f in range(FN) for c in range(CN)
]
FAR_GROUPS = [
    [at(y, f, n, c) for f in range(FN)]
    for y in range(YN) for n in range(NN) for c in range(CN)
]
OTHER_CORE = [(i, i ^ 1) for i in range(64)]
OTHER_HALF = [(i, i ^ 4) for i in range(8)]
ALONG_X = [[(i, i ^ k) for i in range(8)] for k in range(XN)]

PANEL, STEP = 64, 8
TOP_POWER = 13
FACTOR_COST = 2**29
FIRST = 64


def parts_of(value):
    first = lax.reduce_precision(value, 8, 7)
    rest = value - first
    second = lax.reduce_precision(rest, 8, 7)
    return [first.astype(BF16), second.astype(BF16), (rest - second).astype(BF16)]


def eye(n):
    row, col = (lax.broadcasted_iota(jnp.int32, (n, n), d) for d in (0, 1))
    return jnp.where(row == col, 1.0, 0.0).astype(F32)


def inverse_factor_of_panel(square):
    n = square.shape[0]
    work = jnp.concatenate([square, eye(n)], axis=1)
    tiles = [work[t : t + STEP] for t in range(0, n, STEP)]
    row = lax.broadcasted_iota(jnp.int32, tiles[0].shape, 0)
    for t in range(n // STEP):
        columns = {
            u: [
                jnp.broadcast_to(tiles[u][:, t * STEP + s :][:, :1], tiles[u].shape)
                for s in range(STEP)
            ]
            for u in range(t, n // STEP)
        }
        lower, scale, done = {}, [], []
        for s in range(STEP):
            pivot = columns[t][s][s : s + 1]
            for m in range(s):
                pivot = pivot - lower[s, m] * lower[s, m]
            scale.append(lax.rsqrt(pivot))
            for q in range(s + 1, STEP):
                entry = columns[t][s][q : q + 1]
                for m in range(s):
                    entry = entry - lower[q, m] * lower[s, m]
                lower[q, s] = entry * scale[s]
            line = tiles[t][s : s + 1]
            for m in range(s):
                line = line - lower[s, m] * done[m]
            done.append(line * scale[s])
        for u in range(t + 1, n // STEP):
            factors = []
            for s in range(STEP):
                factor = columns[u][s]
                for m in range(s):
                    factor = factor - factors[m] * lower[s, m]
                factors.append(factor * scale[s])
                tiles[u] = tiles[u] - factors[s] * done[s]
        for s in range(STEP):
            tiles[t] = jnp.where(row == s, done[s], tiles[t])
    return jnp.concatenate(tiles, axis=0)[:, n:]


def inverse_factor_kernel(place_ref, own_ref, *refs):
    came_refs, inverse_ref, work_ref = refs[:-2], refs[-2], refs[-1]
    n = inverse_ref.shape[0]
    block = n // XN
    held = []
    for ref in (own_ref,) + came_refs:
        packed = ref[...]
        width = packed.shape[1] // 2
        held.append(jnp.concatenate([packed[:, :width], packed[:, width:]], axis=0))
    for x in range(XN):

        @pl.when(place_ref[0] == x)
        def _():
            for b in range(XN):
                rows = pl.ds(b * block, block)
                for j in range(XN - 1):
                    c = (b + j) % XN
                    part = held[b ^ x][:, j * block : (j + 1) * block]
                    work_ref[rows, c * block : (c + 1) * block] = part
                c = (b + XN - 1) % XN
                work_ref[rows, c * block : (c + 1) * block] = held[c ^ x][:, block : 2 * block].T

    work_ref[:, n:] = eye(n)
    for top in range(0, n, PANEL):
        end = top + PANEL
        own = inverse_factor_of_panel(work_ref[top:end, top:end])
        done = jnp.dot(own, work_ref[top:end], precision=HIGHEST, preferred_element_type=F32)
        inverse_ref[top:end] = done[:, n:]
        if end < n:
            below = lax.dot_general(
                work_ref[end:, top:end], own, (((1,), (1,)), ((), ())),
                precision=HIGHEST, preferred_element_type=F32,
            )
            work_ref[end:] = work_ref[end:] - jnp.dot(
                below, done, precision=HIGHEST, preferred_element_type=F32
            )


VMEM = pl.BlockSpec(memory_space=pltpu.VMEM)
SMEM = pl.BlockSpec(memory_space=pltpu.SMEM)


def inverse_factor(place, blocks, n):
    return pl.pallas_call(
        inverse_factor_kernel,
        out_shape=jax.ShapeDtypeStruct((n, n), F32),
        in_specs=[SMEM] + [VMEM] * len(blocks),
        out_specs=VMEM,
        scratch_shapes=[pltpu.VMEM((n, 2 * n), F32)],
        compiler_params=pltpu.CompilerParams(vmem_limit_bytes=16 * MIB),
        cost_estimate=pl.CostEstimate(flops=FACTOR_COST, bytes_accessed=2**10, transcendentals=0),
        name="inverse_factor",
    )(place, *blocks)


def range_product(turned, own, base):
    total = None
    for step in range(3):
        part = turned.astype(BF16)
        turned = turned - part.astype(F32)
        term = jnp.dot(part, own, preferred_element_type=F32)
        term -= jnp.dot(part, base, preferred_element_type=F32)
        total = term if total is None else total + term
    return total


def products_kernel(place_ref, mine_ref, other_ref, own_ref, sketch_ref, out_ref, range_ref):
    half = mine_ref.shape[0]
    ff, rank = sketch_ref.shape
    block, slab = rank // XN, ff // XN
    core, x = place_ref[0], place_ref[1]
    gram = jnp.zeros((rank, rank), F32)
    delta = jnp.zeros((rank, ff), F32)
    for load_ref, at_core in ((mine_ref, core), (other_ref, 1 - core)):
        rows = pl.ds(pl.multiple_of(at_core * half, half), half)
        own = own_ref[rows, :]
        base_sketch = (
            load_ref[:, ff : ff + rank].astype(F32)
            + load_ref[:, ff + rank : ff + 2 * rank].astype(F32)
            + load_ref[:, ff + 2 * rank :].astype(F32)
        )
        range_rows = jnp.dot(own, sketch_ref[...], preferred_element_type=F32) - base_sketch
        range_ref[rows, :] = range_rows
        turned = range_rows.T
        gram += jnp.dot(turned, range_rows, precision=HIGHEST, preferred_element_type=F32)
        delta += range_product(turned, own, load_ref[:, :ff])
    for b in range(XN):
        mine = gram[b * block : (b + 1) * block]
        kept = jnp.concatenate(
            [mine[:, (b + j) % XN * block :][:, :block] for j in range(XN - 1)], axis=1
        )
        packed = jnp.concatenate([kept[: block // 2], kept[block // 2 :]], axis=1)
        out_ref[b ^ x, : block // 2, :] = packed
        out_ref[b ^ x, block // 2 :, :] = delta[:, b * slab : (b + 1) * slab]


def products(place, mine, other, own, sketch):
    rows, ff = own.shape
    rank = sketch.shape[1]
    return pl.pallas_call(
        products_kernel,
        out_shape=(
            jax.ShapeDtypeStruct((XN, rank // XN // 2 + rank, ff // XN), F32),
            jax.ShapeDtypeStruct((rows, rank), F32),
        ),
        in_specs=[SMEM] + [VMEM] * 4,
        out_specs=(VMEM, VMEM),
        compiler_params=pltpu.CompilerParams(vmem_limit_bytes=40 * MIB),
        cost_estimate=pl.CostEstimate(flops=5 * 10**9, bytes_accessed=2**10, transcendentals=0),
        name="products",
    )(place, mine, other, own, sketch)


def finished_kernel(inverse_ref, *refs):
    pairs, (out_ref, sums_ref) = refs[:-2], refs[-2:]
    rank = inverse_ref.shape[0]
    top = 0
    for i in range(0, len(pairs), 2):
        end = top + pairs[i].shape[0]
        sums_ref[top:end] = pairs[i][...] + pairs[i + 1][...]
        top = end
    values = jnp.dot(
        inverse_ref[...], sums_ref[...], precision=HIGHEST, preferred_element_type=F32
    )
    most = jnp.max(jnp.max(jnp.abs(values), axis=0, keepdims=True), axis=1, keepdims=True)
    power = jnp.floor(jnp.log(jnp.maximum(most, 1e-30)) * (1 / math.log(2)))
    out_ref[:rank] = values * jnp.exp2(TOP_POWER - power)
    out_ref[rank:] = jnp.broadcast_to(power, (out_ref.shape[0] - rank, out_ref.shape[1]))


def finished(inverse, pairs):
    rank, slab = inverse.shape[0], pairs[0].shape[1]
    return pl.pallas_call(
        finished_kernel,
        out_shape=jax.ShapeDtypeStruct((rank + 16, slab), F32),
        in_specs=[VMEM] * (1 + len(pairs)),
        out_specs=VMEM,
        scratch_shapes=[pltpu.VMEM((rank, slab), F32)],
        compiler_params=pltpu.CompilerParams(vmem_limit_bytes=16 * MIB),
        name="finished",
    )(inverse, *pairs)


def assembled_kernel(place_ref, *refs):
    blocks, (out_ref, held_ref, sems) = refs[:XN], refs[XN:]
    rank, slab = held_ref.shape[1:]
    copies = []
    for k, ref in enumerate(blocks):
        held_ref[k] = ref[:rank] * jnp.exp2(ref[rank : rank + 1] - TOP_POWER)
        start = pl.multiple_of((place_ref[0] ^ k) * slab, slab)
        copy = pltpu.make_async_copy(
            held_ref.at[k], out_ref.at[:, pl.ds(start, slab)], sems.at[k]
        )
        copy.start()
        copies.append(copy)
    for copy in copies:
        copy.wait()


def assembled(place, blocks):
    rank, slab = blocks[0].shape[0] - 16, blocks[0].shape[1]
    return pl.pallas_call(
        assembled_kernel,
        out_shape=jax.ShapeDtypeStruct((rank, XN * slab), F32),
        in_specs=[SMEM] + [VMEM] * XN,
        out_specs=pl.BlockSpec(memory_space=pl.ANY),
        scratch_shapes=[pltpu.VMEM((XN, rank, slab), F32), pltpu.SemaphoreType.DMA((XN,))],
        compiler_params=pltpu.CompilerParams(vmem_limit_bytes=16 * MIB),
        name="assembled",
    )(place, *blocks)


def per_device(counts, up_weights, sketch):
    rows, ff = up_weights.shape[1:]
    rank = sketch.shape[1]
    piece = rows // 64
    own = up_weights[0].reshape(YN, FN, NN, CN, piece, ff).transpose(3, 0, 2, 1, 4, 5)
    members = CN * YN * NN
    own = own.reshape(members, FN * piece, ff)

    lane = lax.broadcasted_iota(jnp.int32, (members, FN * piece, 128), 2)
    count = counts[0]
    tag = jnp.where(lane == 0, count // 64, jnp.where(lane == 1, count % 64, 0)).astype(BF16)
    got = lax.all_to_all(
        jnp.concatenate([own, tag], axis=2), "exp", 0, 0, axis_index_groups=CYN_GROUPS
    )
    freq = got[:, 0, ff].astype(F32) * 64 + got[:, 0, ff + 1].astype(F32)
    weighted = jnp.sum(freq[:, None, None] * got[:, :, :ff].astype(F32), axis=0)
    freq_sum = jnp.broadcast_to(jnp.sum(freq), (FN, piece, 128))

    sums = lax.all_to_all(
        jnp.concatenate([weighted.reshape(FN, piece, ff), freq_sum], axis=2),
        "exp", 0, 0, axis_index_groups=FAR_GROUPS,
    )
    sums = jnp.sum(sums, axis=0)
    base_rows = sums[:, :ff] / sums[:, ff : ff + 1]
    base_piece = base_rows.astype(BF16)
    sketched = jnp.dot(base_rows, sketch.astype(F32), precision=HIGHEST)

    wide = ff + 3 * rank
    load = jnp.concatenate([base_piece] + parts_of(sketched), axis=1)
    load = lax.all_to_all(
        jnp.broadcast_to(load, (FN, piece, wide)), "exp", 0, 0, axis_index_groups=FAR_GROUPS
    ).reshape(FN * piece, wide)
    load = lax.all_to_all(
        jnp.broadcast_to(load, (YN * NN, FN * piece, wide)),
        "exp", 0, 0, axis_index_groups=YN_GROUPS,
    ).reshape(rows // CN, wide)
    other = lax.ppermute(load, "exp", OTHER_CORE)

    at_core, at_x = lax.axis_index("exp") % CN, lax.axis_index("grp") % XN
    place, own = jnp.stack([at_core, at_x]), own.reshape(rows, ff)

    blocks, range_rows = products(place, load, other, own, sketch)
    total = blocks[0] + sum(lax.ppermute(blocks[k], "grp", ALONG_X[k]) for k in (2, 3, 1))
    packed = rank // XN // 2
    first, second = total[: packed + FIRST], total[packed + FIRST :]
    first_came = lax.ppermute(first, "grp", OTHER_HALF)
    second_came = lax.ppermute(second, "grp", OTHER_HALF)
    gram = first[:packed] + first_came[:packed]
    inverse = inverse_factor(
        at_x.reshape(1),
        [gram] + [lax.ppermute(gram, "grp", ALONG_X[k]) for k in (1, 2, 3)],
        rank,
    )
    pairs = [first[packed:], first_came[packed:], second, second_came]
    inverse, pairs = lax.optimization_barrier((inverse, pairs))
    block = lax.optimization_barrier(finished(inverse, pairs).astype(jnp.float16))
    blocks = {0: block}
    for k in (2, 3, 1):
        blocks[k] = lax.ppermute(block, "grp", ALONG_X[k])
    coeff = assembled(at_x.reshape(1), [blocks[k].astype(F32) for k in range(XN)])

    ortho = lax.dot_general(
        range_rows, inverse, (((1,), (1,)), ((), ())), precision=HIGHEST
    )
    basis = ortho * math.sqrt(rows * lax.axis_size("grp"))
    basis = basis.reshape(CN, YN, NN, FN, piece, rank).transpose(1, 3, 2, 0, 4, 5)
    return (base_piece, basis.reshape(1, rows, rank), coeff[None])


def solution(mesh):
    placed = (P("exp"), P("exp", "grp", None), P())
    return jax.shard_map(
        per_device,
        mesh=mesh,
        in_specs=placed,
        out_specs=(P(("grp", "exp"), None), P("exp", "grp", None), P("exp", None, None)),
        check_vma=False,
    )
```

```python
import math

import jax
import jax.numpy as jnp
from jax import lax
from jax.experimental import pallas as pl
from jax.experimental.pallas import tpu as pltpu
from jax.sharding import PartitionSpec as P

F32, BF16 = jnp.float32, jnp.bfloat16
HIGHEST = lax.Precision.HIGHEST
MIB = 2**20

YN, FN, NN, CN, XN = 4, 4, 2, 2, 4


def at(y, far, near, core):
    return y * 16 + (2 * far + near) * 2 + core


CYN_GROUPS = [
    [at(y, f, n, c) for c in range(CN) for y in range(YN) for n in range(NN)] for f in range(FN)
]
YN_GROUPS = [
    [at(y, f, n, c) for y in range(YN) for n in range(NN)] for f in range(FN) for c in range(CN)
]
FAR_GROUPS = [
    [at(y, f, n, c) for f in range(FN)]
    for y in range(YN) for n in range(NN) for c in range(CN)
]
OTHER_CORE = [(i, i ^ 1) for i in range(64)]
OTHER_HALF = [(i, i ^ 4) for i in range(8)]
X_GROUPS = [[h * XN + x for x in range(XN)] for h in range(2)]
ALONG_X = [[(i, i ^ k) for i in range(8)] for k in range(XN)]

PANEL, STEP = 64, 8
TOP_POWER = 13
FACTOR_COST = 2**29


def parts_of(value):
    first = lax.reduce_precision(value, 8, 7)
    rest = value - first
    second = lax.reduce_precision(rest, 8, 7)
    return [first.astype(BF16), second.astype(BF16), (rest - second).astype(BF16)]


def eye(n):
    row, col = (lax.broadcasted_iota(jnp.int32, (n, n), d) for d in (0, 1))
    return jnp.where(row == col, 1.0, 0.0).astype(F32)


def inverse_factor_of_panel(square):
    n = square.shape[0]
    work = jnp.concatenate([square, eye(n)], axis=1)
    tiles = [work[t : t + STEP] for t in range(0, n, STEP)]
    row = lax.broadcasted_iota(jnp.int32, tiles[0].shape, 0)
    for t in range(n // STEP):
        columns = {
            u: [
                jnp.broadcast_to(tiles[u][:, t * STEP + s :][:, :1], tiles[u].shape)
                for s in range(STEP)
            ]
            for u in range(t, n // STEP)
        }
        lower, scale, done = {}, [], []
        for s in range(STEP):
            pivot = columns[t][s][s : s + 1]
            for m in range(s):
                pivot = pivot - lower[s, m] * lower[s, m]
            scale.append(lax.rsqrt(pivot))
            for q in range(s + 1, STEP):
                entry = columns[t][s][q : q + 1]
                for m in range(s):
                    entry = entry - lower[q, m] * lower[s, m]
                lower[q, s] = entry * scale[s]
            line = tiles[t][s : s + 1]
            for m in range(s):
                line = line - lower[s, m] * done[m]
            done.append(line * scale[s])
        for u in range(t + 1, n // STEP):
            factors = []
            for s in range(STEP):
                factor = columns[u][s]
                for m in range(s):
                    factor = factor - factors[m] * lower[s, m]
                factors.append(factor * scale[s])
                tiles[u] = tiles[u] - factors[s] * done[s]
        for s in range(STEP):
            tiles[t] = jnp.where(row == s, done[s], tiles[t])
    return jnp.concatenate(tiles, axis=0)[:, n:]


def inverse_factor_kernel(packed_ref, inverse_ref, work_ref):
    n = inverse_ref.shape[0]
    block, width = n // XN, packed_ref.shape[2] // 2
    for b in range(XN):
        rows = jnp.concatenate([packed_ref[b, :, :width], packed_ref[b, :, width:]], axis=0)
        here = pl.ds(b * block, block)
        for j in range(XN - 1):
            c = (b + j) % XN * block
            work_ref[here, c : c + block] = rows[:, j * block : (j + 1) * block]
        below = (b + 1) % XN * block
        work_ref[below : below + block, b * block : (b + 1) * block] = rows[:, block : 2 * block].T
    work_ref[:, n:] = eye(n)
    for top in range(0, n, PANEL):
        end = top + PANEL
        own = inverse_factor_of_panel(work_ref[top:end, top:end])
        done = jnp.dot(own, work_ref[top:end], precision=HIGHEST, preferred_element_type=F32)
        inverse_ref[top:end] = done[:, n:]
        if end < n:
            below = lax.dot_general(
                work_ref[end:, top:end], own, (((1,), (1,)), ((), ())),
                precision=HIGHEST, preferred_element_type=F32,
            )
            work_ref[end:] = work_ref[end:] - jnp.dot(
                below, done, precision=HIGHEST, preferred_element_type=F32
            )


VMEM = pl.BlockSpec(memory_space=pltpu.VMEM)
SMEM = pl.BlockSpec(memory_space=pltpu.SMEM)


def inverse_factor(packed, n):
    return pl.pallas_call(
        inverse_factor_kernel,
        out_shape=jax.ShapeDtypeStruct((n, n), F32),
        in_specs=[VMEM],
        out_specs=VMEM,
        scratch_shapes=[pltpu.VMEM((n, 2 * n), F32)],
        compiler_params=pltpu.CompilerParams(vmem_limit_bytes=16 * MIB),
        cost_estimate=pl.CostEstimate(flops=FACTOR_COST, bytes_accessed=2**10, transcendentals=0),
        name="inverse_factor",
    )(packed)


def range_product(turned, own, base):
    total = None
    for step in range(3):
        part = turned.astype(BF16)
        turned = turned - part.astype(F32)
        term = jnp.dot(part, own, preferred_element_type=F32)
        term -= jnp.dot(part, base, preferred_element_type=F32)
        total = term if total is None else total + term
    return total


def first_products_kernel(place_ref, mine_ref, other_ref, own_ref, sketch_ref, out_ref, range_ref):
    half = mine_ref.shape[0]
    ff, rank = sketch_ref.shape
    block, slab, chunk = rank // XN, ff // XN, rank // 2
    core, x = place_ref[0], place_ref[1]
    gram = jnp.zeros((rank, rank), F32)
    delta = jnp.zeros((chunk, ff), F32)
    for load_ref, at_core in ((mine_ref, core), (other_ref, 1 - core)):
        rows = pl.ds(pl.multiple_of(at_core * half, half), half)
        own = own_ref[rows, :]
        base_sketch = (
            load_ref[:, ff : ff + rank].astype(F32)
            + load_ref[:, ff + rank : ff + 2 * rank].astype(F32)
            + load_ref[:, ff + 2 * rank :].astype(F32)
        )
        range_rows = jnp.dot(own, sketch_ref[...], preferred_element_type=F32) - base_sketch
        range_ref[rows, :] = range_rows
        turned = range_rows.T
        gram += jnp.dot(turned, range_rows, precision=HIGHEST, preferred_element_type=F32)
        delta += range_product(turned[:chunk], own, load_ref[:, :ff])
    for b in range(XN):
        mine = gram[b * block : (b + 1) * block]
        kept = jnp.concatenate(
            [mine[:, (b + j) % XN * block :][:, :block] for j in range(XN - 1)], axis=1
        )
        packed = jnp.concatenate([kept[: block // 2], kept[block // 2 :]], axis=1)
        out_ref[b ^ x, : block // 2, :] = packed
        out_ref[b ^ x, block // 2 :, :] = delta[:, b * slab : (b + 1) * slab]


def first_products(place, mine, other, own, sketch):
    rows, ff = own.shape
    rank = sketch.shape[1]
    return pl.pallas_call(
        first_products_kernel,
        out_shape=(
            jax.ShapeDtypeStruct((XN, rank // XN // 2 + rank // 2, ff // XN), F32),
            jax.ShapeDtypeStruct((rows, rank), F32),
        ),
        in_specs=[SMEM] + [VMEM] * 4,
        out_specs=(VMEM, VMEM),
        compiler_params=pltpu.CompilerParams(vmem_limit_bytes=40 * MIB),
        cost_estimate=pl.CostEstimate(flops=3 * 10**9, bytes_accessed=2**10, transcendentals=0),
        name="first_products",
    )(place, mine, other, own, sketch)


def second_products_kernel(place_ref, mine_ref, other_ref, own_ref, range_ref, out_ref):
    half = mine_ref.shape[0]
    ff, rank = own_ref.shape[1], range_ref.shape[1]
    slab, chunk = ff // XN, rank // 2
    core, x = place_ref[0], place_ref[1]
    delta = jnp.zeros((chunk, ff), F32)
    for load_ref, at_core in ((mine_ref, core), (other_ref, 1 - core)):
        rows = pl.ds(pl.multiple_of(at_core * half, half), half)
        delta += range_product(range_ref[rows, chunk:].T, own_ref[rows, :], load_ref[:, :ff])
    for b in range(XN):
        out_ref[b ^ x] = delta[:, b * slab : (b + 1) * slab]


def second_products(place, mine, other, own, range_rows):
    ff, rank = own.shape[1], range_rows.shape[1]
    return pl.pallas_call(
        second_products_kernel,
        out_shape=jax.ShapeDtypeStruct((XN, rank // 2, ff // XN), F32),
        in_specs=[SMEM] + [VMEM] * 4,
        out_specs=VMEM,
        compiler_params=pltpu.CompilerParams(vmem_limit_bytes=40 * MIB),
        cost_estimate=pl.CostEstimate(flops=2 * 10**9, bytes_accessed=2**10, transcendentals=0),
        name="second_products",
    )(place, mine, other, own, range_rows)


def finished_kernel(inverse_ref, *refs):
    out_ref = refs[-1]
    rank = inverse_ref.shape[0]
    chunk = rank // 2
    values = sum(
        jnp.dot(
            inverse_ref[:, i * chunk : (i + 1) * chunk], refs[2 * i][...] + refs[2 * i + 1][...],
            precision=HIGHEST, preferred_element_type=F32,
        )
        for i in range(2)
    )
    top = jnp.max(jnp.max(jnp.abs(values), axis=0, keepdims=True), axis=1, keepdims=True)
    power = jnp.floor(jnp.log(jnp.maximum(top, 1e-30)) * (1 / math.log(2)))
    out_ref[:rank] = values * jnp.exp2(TOP_POWER - power)
    out_ref[rank:] = jnp.broadcast_to(power, (out_ref.shape[0] - rank, out_ref.shape[1]))


def finished(inverse, chunks):
    rank, slab = inverse.shape[0], chunks[0].shape[1]
    return pl.pallas_call(
        finished_kernel,
        out_shape=jax.ShapeDtypeStruct((rank + 16, slab), F32),
        in_specs=[VMEM] * (1 + len(chunks)),
        out_specs=VMEM,
        compiler_params=pltpu.CompilerParams(vmem_limit_bytes=16 * MIB),
        name="finished",
    )(inverse, *chunks)


def assembled_kernel(place_ref, *refs):
    blocks, (out_ref, held_ref, sems) = refs[:XN], refs[XN:]
    rank, slab = held_ref.shape[1:]
    copies = []
    for k, ref in enumerate(blocks):
        held_ref[k] = ref[:rank] * jnp.exp2(ref[rank : rank + 1] - TOP_POWER)
        start = pl.multiple_of((place_ref[0] ^ k) * slab, slab)
        copy = pltpu.make_async_copy(
            held_ref.at[k], out_ref.at[:, pl.ds(start, slab)], sems.at[k]
        )
        copy.start()
        copies.append(copy)
    for copy in copies:
        copy.wait()


def assembled(place, blocks):
    rank, slab = blocks[0].shape[0] - 16, blocks[0].shape[1]
    return pl.pallas_call(
        assembled_kernel,
        out_shape=jax.ShapeDtypeStruct((rank, XN * slab), F32),
        in_specs=[SMEM] + [VMEM] * XN,
        out_specs=pl.BlockSpec(memory_space=pl.ANY),
        scratch_shapes=[pltpu.VMEM((XN, rank, slab), F32), pltpu.SemaphoreType.DMA((XN,))],
        compiler_params=pltpu.CompilerParams(vmem_limit_bytes=16 * MIB),
        name="assembled",
    )(place, *blocks)


def per_device(counts, up_weights, sketch):
    rows, ff = up_weights.shape[1:]
    rank = sketch.shape[1]
    piece = rows // 64
    own = up_weights[0].reshape(YN, FN, NN, CN, piece, ff).transpose(3, 0, 2, 1, 4, 5)
    members = CN * YN * NN
    own = own.reshape(members, FN * piece, ff)

    lane = lax.broadcasted_iota(jnp.int32, (members, FN * piece, 128), 2)
    count = counts[0]
    tag = jnp.where(lane == 0, count // 64, jnp.where(lane == 1, count % 64, 0)).astype(BF16)
    got = lax.all_to_all(
        jnp.concatenate([own, tag], axis=2), "exp", 0, 0, axis_index_groups=CYN_GROUPS
    )
    freq = got[:, 0, ff].astype(F32) * 64 + got[:, 0, ff + 1].astype(F32)
    weighted = jnp.sum(freq[:, None, None] * got[:, :, :ff].astype(F32), axis=0)
    freq_sum = jnp.broadcast_to(jnp.sum(freq), (FN, piece, 128))

    sums = lax.all_to_all(
        jnp.concatenate([weighted.reshape(FN, piece, ff), freq_sum], axis=2),
        "exp", 0, 0, axis_index_groups=FAR_GROUPS,
    )
    sums = jnp.sum(sums, axis=0)
    base_rows = sums[:, :ff] / sums[:, ff : ff + 1]
    base_piece = base_rows.astype(BF16)
    sketched = jnp.dot(base_rows, sketch.astype(F32), precision=HIGHEST)

    wide = ff + 3 * rank
    load = jnp.concatenate([base_piece] + parts_of(sketched), axis=1)
    load = lax.all_to_all(
        jnp.broadcast_to(load, (FN, piece, wide)), "exp", 0, 0, axis_index_groups=FAR_GROUPS
    ).reshape(FN * piece, wide)
    load = lax.all_to_all(
        jnp.broadcast_to(load, (YN * NN, FN * piece, wide)),
        "exp", 0, 0, axis_index_groups=YN_GROUPS,
    ).reshape(rows // CN, wide)
    other = lax.ppermute(load, "exp", OTHER_CORE)

    at_core, at_x = lax.axis_index("exp") % CN, lax.axis_index("grp") % XN
    place, own = jnp.stack([at_core, at_x]), own.reshape(rows, ff)

    def along_x(blocks):
        return [blocks[0]] + [lax.ppermute(blocks[k], "grp", ALONG_X[k]) for k in (2, 3, 1)]

    first, range_rows = first_products(place, load, other, own, sketch)
    first = along_x(first)
    second = along_x(second_products(place, load, other, own, range_rows))
    first = sum(first)
    packed = rank // XN // 2
    gram, first = first[:packed], first[packed:]
    gram_came = lax.ppermute(gram, "grp", OTHER_HALF)
    _, second = lax.optimization_barrier((gram_came, second))
    gram, second = gram + gram_came, sum(second)
    chunks = [first, lax.ppermute(first, "grp", OTHER_HALF)]
    chunks += [second, lax.ppermute(second, "grp", OTHER_HALF)]
    gram = lax.all_to_all(
        jnp.broadcast_to(gram, (XN,) + gram.shape), "grp", 0, 0, axis_index_groups=X_GROUPS
    )
    inverse = inverse_factor(gram, rank)
    inverse, chunks = lax.optimization_barrier((inverse, chunks))
    block = lax.optimization_barrier(finished(inverse, chunks).astype(jnp.float16))
    blocks = {0: block}
    for k in (2, 3, 1):
        blocks[k] = lax.ppermute(block, "grp", ALONG_X[k])
    coeff = assembled(at_x.reshape(1), [blocks[k].astype(F32) for k in range(XN)])

    ortho = lax.dot_general(
        range_rows, inverse, (((1,), (1,)), ((), ())), precision=HIGHEST
    )
    basis = ortho * math.sqrt(rows * lax.axis_size("grp"))
    basis = basis.reshape(CN, YN, NN, FN, piece, rank).transpose(1, 3, 2, 0, 4, 5)
    return (base_piece, basis.reshape(1, rows, rank), coeff[None])


def solution(mesh):
    placed = (P("exp"), P("exp", "grp", None), P())
    return jax.shard_map(
        per_device,
        mesh=mesh,
        in_specs=placed,
        out_specs=(P(("grp", "exp"), None), P("exp", "grp", None), P("exp", None, None)),
        check_vma=False,
    )
```

```python
import math

import jax
import jax.numpy as jnp
from jax import lax
from jax.experimental import pallas as pl
from jax.experimental.pallas import tpu as pltpu
from jax.sharding import PartitionSpec as P

F32, BF16 = jnp.float32, jnp.bfloat16
HIGHEST = lax.Precision.HIGHEST
MIB = 2**20

YN, FN, NN, CN, XN = 4, 4, 2, 2, 4


def at(y, far, near, core):
    return y * 16 + (2 * far + near) * 2 + core


CYN_GROUPS = [
    [at(y, f, n, c) for c in range(CN) for y in range(YN) for n in range(NN)] for f in range(FN)
]
YN_GROUPS = [
    [at(y, f, n, c) for y in range(YN) for n in range(NN)] for f in range(FN) for c in range(CN)
]
FAR_GROUPS = [
    [at(y, f, n, c) for f in range(FN)]
    for y in range(YN) for n in range(NN) for c in range(CN)
]
OTHER_CORE = [(i, i ^ 1) for i in range(64)]
OTHER_HALF = [(i, i ^ 4) for i in range(8)]
X_GROUPS = [[h * XN + x for x in range(XN)] for h in range(2)]
ALONG_X = [[(i, i ^ k) for i in range(8)] for k in range(XN)]

PANEL, STEP = 64, 8
TOP_POWER = 13
FIRST = 64
FACTOR_COST = 2**29


def parts_of(value):
    first = lax.reduce_precision(value, 8, 7)
    rest = value - first
    second = lax.reduce_precision(rest, 8, 7)
    return [first.astype(BF16), second.astype(BF16), (rest - second).astype(BF16)]


def eye(n):
    row, col = (lax.broadcasted_iota(jnp.int32, (n, n), d) for d in (0, 1))
    return jnp.where(row == col, 1.0, 0.0).astype(F32)


def inverse_factor_of_panel(square):
    n = square.shape[0]
    work = jnp.concatenate([square, eye(n)], axis=1)
    tiles = [work[t : t + STEP] for t in range(0, n, STEP)]
    row = lax.broadcasted_iota(jnp.int32, tiles[0].shape, 0)
    for t in range(n // STEP):
        columns = {
            u: [
                jnp.broadcast_to(tiles[u][:, t * STEP + s :][:, :1], tiles[u].shape)
                for s in range(STEP)
            ]
            for u in range(t, n // STEP)
        }
        lower, scale, done = {}, [], []
        for s in range(STEP):
            pivot = columns[t][s][s : s + 1]
            for m in range(s):
                pivot = pivot - lower[s, m] * lower[s, m]
            scale.append(lax.rsqrt(pivot))
            for q in range(s + 1, STEP):
                entry = columns[t][s][q : q + 1]
                for m in range(s):
                    entry = entry - lower[q, m] * lower[s, m]
                lower[q, s] = entry * scale[s]
            line = tiles[t][s : s + 1]
            for m in range(s):
                line = line - lower[s, m] * done[m]
            done.append(line * scale[s])
        for u in range(t + 1, n // STEP):
            factors = []
            for s in range(STEP):
                factor = columns[u][s]
                for m in range(s):
                    factor = factor - factors[m] * lower[s, m]
                factors.append(factor * scale[s])
                tiles[u] = tiles[u] - factors[s] * done[s]
        for s in range(STEP):
            tiles[t] = jnp.where(row == s, done[s], tiles[t])
    return jnp.concatenate(tiles, axis=0)[:, n:]


def inverse_factor_kernel(packed_ref, inverse_ref, work_ref):
    n = inverse_ref.shape[0]
    block, width = n // XN, packed_ref.shape[2] // 2
    for b in range(XN):
        rows = jnp.concatenate([packed_ref[b, :, :width], packed_ref[b, :, width:]], axis=0)
        here = pl.ds(b * block, block)
        for j in range(XN - 1):
            c = (b + j) % XN * block
            work_ref[here, c : c + block] = rows[:, j * block : (j + 1) * block]
        below = (b + 1) % XN * block
        work_ref[below : below + block, b * block : (b + 1) * block] = rows[:, block : 2 * block].T
    work_ref[:, n:] = eye(n)
    for top in range(0, n, PANEL):
        end = top + PANEL
        own = inverse_factor_of_panel(work_ref[top:end, top:end])
        done = jnp.dot(own, work_ref[top:end], precision=HIGHEST, preferred_element_type=F32)
        inverse_ref[top:end] = done[:, n:]
        if end < n:
            below = lax.dot_general(
                work_ref[end:, top:end], own, (((1,), (1,)), ((), ())),
                precision=HIGHEST, preferred_element_type=F32,
            )
            work_ref[end:] = work_ref[end:] - jnp.dot(
                below, done, precision=HIGHEST, preferred_element_type=F32
            )


VMEM = pl.BlockSpec(memory_space=pltpu.VMEM)
SMEM = pl.BlockSpec(memory_space=pltpu.SMEM)


def inverse_factor(packed, n):
    return pl.pallas_call(
        inverse_factor_kernel,
        out_shape=jax.ShapeDtypeStruct((n, n), F32),
        in_specs=[VMEM],
        out_specs=VMEM,
        scratch_shapes=[pltpu.VMEM((n, 2 * n), F32)],
        compiler_params=pltpu.CompilerParams(vmem_limit_bytes=16 * MIB),
        cost_estimate=pl.CostEstimate(flops=FACTOR_COST, bytes_accessed=2**10, transcendentals=0),
        name="inverse_factor",
    )(packed)


def range_product(turned, own, base):
    total = None
    for step in range(3):
        part = turned.astype(BF16)
        turned = turned - part.astype(F32)
        term = jnp.dot(part, own, preferred_element_type=F32)
        term -= jnp.dot(part, base, preferred_element_type=F32)
        total = term if total is None else total + term
    return total


def first_products_kernel(place_ref, mine_ref, other_ref, own_ref, sketch_ref, out_ref, range_ref):
    half = mine_ref.shape[0]
    ff, rank = sketch_ref.shape
    block, slab, chunk = rank // XN, ff // XN, FIRST
    core = place_ref[0]
    gram = jnp.zeros((rank, rank), F32)
    delta = jnp.zeros((chunk, ff), F32)
    for load_ref, at_core in ((mine_ref, core), (other_ref, 1 - core)):
        rows = pl.ds(pl.multiple_of(at_core * half, half), half)
        own = own_ref[rows, :]
        base_sketch = (
            load_ref[:, ff : ff + rank].astype(F32)
            + load_ref[:, ff + rank : ff + 2 * rank].astype(F32)
            + load_ref[:, ff + 2 * rank :].astype(F32)
        )
        range_rows = jnp.dot(own, sketch_ref[...], preferred_element_type=F32) - base_sketch
        range_ref[rows, :] = range_rows
        turned = range_rows.T
        gram += jnp.dot(turned, range_rows, precision=HIGHEST, preferred_element_type=F32)
        delta += range_product(turned[:chunk], own, load_ref[:, :ff])
    for b in range(XN):
        mine = gram[b * block : (b + 1) * block]
        kept = jnp.concatenate(
            [mine[:, (b + j) % XN * block :][:, :block] for j in range(XN - 1)], axis=1
        )
        packed = jnp.concatenate([kept[: block // 2], kept[block // 2 :]], axis=1)
        out_ref[b, : block // 2, :] = packed
        out_ref[b, block // 2 :, :] = delta[:, b * slab : (b + 1) * slab]


def first_products(place, mine, other, own, sketch):
    rows, ff = own.shape
    rank = sketch.shape[1]
    return pl.pallas_call(
        first_products_kernel,
        out_shape=(
            jax.ShapeDtypeStruct((XN, rank // XN // 2 + FIRST, ff // XN), F32),
            jax.ShapeDtypeStruct((rows, rank), F32),
        ),
        in_specs=[SMEM] + [VMEM] * 4,
        out_specs=(VMEM, VMEM),
        compiler_params=pltpu.CompilerParams(vmem_limit_bytes=40 * MIB),
        cost_estimate=pl.CostEstimate(flops=3 * 10**9, bytes_accessed=2**10, transcendentals=0),
        name="first_products",
    )(place, mine, other, own, sketch)


def second_products_kernel(place_ref, mine_ref, other_ref, own_ref, range_ref, out_ref):
    half = mine_ref.shape[0]
    ff, rank = own_ref.shape[1], range_ref.shape[1]
    slab, chunk = ff // XN, FIRST
    core = place_ref[0]
    delta = jnp.zeros((rank - chunk, ff), F32)
    for load_ref, at_core in ((mine_ref, core), (other_ref, 1 - core)):
        rows = pl.ds(pl.multiple_of(at_core * half, half), half)
        turned = range_ref[rows, :].T
        delta += range_product(turned[chunk:], own_ref[rows, :], load_ref[:, :ff])
    for b in range(XN):
        out_ref[b] = delta[:, b * slab : (b + 1) * slab]


def second_products(place, mine, other, own, range_rows):
    ff, rank = own.shape[1], range_rows.shape[1]
    return pl.pallas_call(
        second_products_kernel,
        out_shape=jax.ShapeDtypeStruct((XN, rank - FIRST, ff // XN), F32),
        in_specs=[SMEM] + [VMEM] * 4,
        out_specs=VMEM,
        compiler_params=pltpu.CompilerParams(vmem_limit_bytes=40 * MIB),
        cost_estimate=pl.CostEstimate(flops=2 * 10**9, bytes_accessed=2**10, transcendentals=0),
        name="second_products",
    )(place, mine, other, own, range_rows)


def finished_kernel(inverse_ref, *refs):
    pairs, (out_ref, sums_ref) = refs[:-2], refs[-2:]
    rank = inverse_ref.shape[0]
    top = 0
    for i in range(0, len(pairs), 2):
        end = top + pairs[i].shape[0]
        sums_ref[top:end] = pairs[i][...] + pairs[i + 1][...]
        top = end
    values = jnp.dot(
        inverse_ref[...], sums_ref[...], precision=HIGHEST, preferred_element_type=F32
    )
    most = jnp.max(jnp.max(jnp.abs(values), axis=0, keepdims=True), axis=1, keepdims=True)
    power = jnp.floor(jnp.log(jnp.maximum(most, 1e-30)) * (1 / math.log(2)))
    out_ref[:rank] = values * jnp.exp2(TOP_POWER - power)
    out_ref[rank:] = jnp.broadcast_to(power, (out_ref.shape[0] - rank, out_ref.shape[1]))


def finished(inverse, pairs):
    rank, slab = inverse.shape[0], pairs[0].shape[1]
    return pl.pallas_call(
        finished_kernel,
        out_shape=jax.ShapeDtypeStruct((rank + 16, slab), F32),
        in_specs=[VMEM] * (1 + len(pairs)),
        out_specs=VMEM,
        scratch_shapes=[pltpu.VMEM((rank, slab), F32)],
        compiler_params=pltpu.CompilerParams(vmem_limit_bytes=16 * MIB),
        name="finished",
    )(inverse, *pairs)


def assembled_kernel(place_ref, *refs):
    blocks, (out_ref, held_ref, sems) = refs[:XN], refs[XN:]
    rank, slab = held_ref.shape[1:]
    copies = []
    for k, ref in enumerate(blocks):
        held_ref[k] = ref[:rank] * jnp.exp2(ref[rank : rank + 1] - TOP_POWER)
        start = pl.multiple_of((place_ref[0] ^ k) * slab, slab)
        copy = pltpu.make_async_copy(
            held_ref.at[k], out_ref.at[:, pl.ds(start, slab)], sems.at[k]
        )
        copy.start()
        copies.append(copy)
    for copy in copies:
        copy.wait()


def assembled(place, blocks):
    rank, slab = blocks[0].shape[0] - 16, blocks[0].shape[1]
    return pl.pallas_call(
        assembled_kernel,
        out_shape=jax.ShapeDtypeStruct((rank, XN * slab), F32),
        in_specs=[SMEM] + [VMEM] * XN,
        out_specs=pl.BlockSpec(memory_space=pl.ANY),
        scratch_shapes=[pltpu.VMEM((XN, rank, slab), F32), pltpu.SemaphoreType.DMA((XN,))],
        compiler_params=pltpu.CompilerParams(vmem_limit_bytes=16 * MIB),
        name="assembled",
    )(place, *blocks)


def per_device(counts, up_weights, sketch):
    rows, ff = up_weights.shape[1:]
    rank = sketch.shape[1]
    piece = rows // 64
    own = up_weights[0].reshape(YN, FN, NN, CN, piece, ff).transpose(3, 0, 2, 1, 4, 5)
    members = CN * YN * NN
    own = own.reshape(members, FN * piece, ff)

    lane = lax.broadcasted_iota(jnp.int32, (members, FN * piece, 128), 2)
    count = counts[0]
    tag = jnp.where(lane == 0, count // 64, jnp.where(lane == 1, count % 64, 0)).astype(BF16)
    got = lax.all_to_all(
        jnp.concatenate([own, tag], axis=2), "exp", 0, 0, axis_index_groups=CYN_GROUPS
    )
    freq = got[:, 0, ff].astype(F32) * 64 + got[:, 0, ff + 1].astype(F32)
    weighted = jnp.sum(freq[:, None, None] * got[:, :, :ff].astype(F32), axis=0)
    freq_sum = jnp.broadcast_to(jnp.sum(freq), (FN, piece, 128))

    sums = lax.all_to_all(
        jnp.concatenate([weighted.reshape(FN, piece, ff), freq_sum], axis=2),
        "exp", 0, 0, axis_index_groups=FAR_GROUPS,
    )
    sums = jnp.sum(sums, axis=0)
    base_rows = sums[:, :ff] / sums[:, ff : ff + 1]
    base_piece = base_rows.astype(BF16)
    sketched = jnp.dot(base_rows, sketch.astype(F32), precision=HIGHEST)

    wide = ff + 3 * rank
    load = jnp.concatenate([base_piece] + parts_of(sketched), axis=1)
    load = lax.all_to_all(
        jnp.broadcast_to(load, (FN, piece, wide)), "exp", 0, 0, axis_index_groups=FAR_GROUPS
    ).reshape(FN * piece, wide)
    load = lax.all_to_all(
        jnp.broadcast_to(load, (YN * NN, FN * piece, wide)),
        "exp", 0, 0, axis_index_groups=YN_GROUPS,
    ).reshape(rows // CN, wide)
    other = lax.ppermute(load, "exp", OTHER_CORE)

    at_core, at_x = lax.axis_index("exp") % CN, lax.axis_index("grp") % XN
    place, own = at_core.reshape(1), own.reshape(rows, ff)

    def to_owners(blocks):
        return lax.all_to_all(blocks, "grp", 0, 0, axis_index_groups=X_GROUPS)

    first, range_rows = first_products(place, load, other, own, sketch)
    first = to_owners(first)
    second = to_owners(second_products(place, load, other, own, range_rows))
    first = jnp.sum(first, axis=0)
    first_came = lax.ppermute(first, "grp", OTHER_HALF)
    second = jnp.sum(second, axis=0)
    second_came = lax.ppermute(second, "grp", OTHER_HALF)
    packed = rank // XN // 2
    gram = first[:packed] + first_came[:packed]
    inverse = inverse_factor(to_owners(jnp.broadcast_to(gram, (XN,) + gram.shape)), rank)
    chunks = [first[packed:], first_came[packed:], second, second_came]
    inverse, chunks = lax.optimization_barrier((inverse, chunks))
    block = lax.optimization_barrier(finished(inverse, chunks).astype(jnp.float16))
    blocks = {0: block}
    for k in (2, 3, 1):
        blocks[k] = lax.ppermute(block, "grp", ALONG_X[k])
    coeff = assembled(at_x.reshape(1), [blocks[k].astype(F32) for k in range(XN)])

    ortho = lax.dot_general(
        range_rows, inverse, (((1,), (1,)), ((), ())), precision=HIGHEST
    )
    basis = ortho * math.sqrt(rows * lax.axis_size("grp"))
    basis = basis.reshape(CN, YN, NN, FN, piece, rank).transpose(1, 3, 2, 0, 4, 5)
    return (base_piece, basis.reshape(1, rows, rank), coeff[None])


def solution(mesh):
    placed = (P("exp"), P("exp", "grp", None), P())
    return jax.shard_map(
        per_device,
        mesh=mesh,
        in_specs=placed,
        out_specs=(P(("grp", "exp"), None), P("exp", "grp", None), P("exp", None, None)),
        check_vma=False,
    )
```

```python
import math

import jax
import jax.numpy as jnp
from jax import lax
from jax.experimental import pallas as pl
from jax.experimental.pallas import tpu as pltpu
from jax.sharding import PartitionSpec as P

F32, BF16 = jnp.float32, jnp.bfloat16
HIGHEST = lax.Precision.HIGHEST
MIB = 2**20

YN, FN, NN, CN, XN = 4, 4, 2, 2, 4


def at(y, far, near, core):
    return y * 16 + (2 * far + near) * 2 + core


CYN_GROUPS = [
    [at(y, f, n, c) for c in range(CN) for y in range(YN) for n in range(NN)] for f in range(FN)
]
YN_GROUPS = [
    [at(y, f, n, c) for y in range(YN) for n in range(NN)] for f in range(FN) for c in range(CN)
]
FAR_GROUPS = [
    [at(y, f, n, c) for f in range(FN)]
    for y in range(YN) for n in range(NN) for c in range(CN)
]
OTHER_CORE = [(i, i ^ 1) for i in range(64)]
OTHER_HALF = [(i, i ^ 4) for i in range(8)]
X_GROUPS = [[h * XN + x for x in range(XN)] for h in range(2)]

PANEL, STEP = 64, 8
TOP_POWER = 13
FIRST = 64
FACTOR_COST = 2**29


def parts_of(value):
    first = lax.reduce_precision(value, 8, 7)
    rest = value - first
    second = lax.reduce_precision(rest, 8, 7)
    return [first.astype(BF16), second.astype(BF16), (rest - second).astype(BF16)]


def eye(n):
    row, col = (lax.broadcasted_iota(jnp.int32, (n, n), d) for d in (0, 1))
    return jnp.where(row == col, 1.0, 0.0).astype(F32)


def inverse_factor_of_panel(square):
    n = square.shape[0]
    work = jnp.concatenate([square, eye(n)], axis=1)
    tiles = [work[t : t + STEP] for t in range(0, n, STEP)]
    row = lax.broadcasted_iota(jnp.int32, tiles[0].shape, 0)
    for t in range(n // STEP):
        columns = {
            u: [
                jnp.broadcast_to(tiles[u][:, t * STEP + s :][:, :1], tiles[u].shape)
                for s in range(STEP)
            ]
            for u in range(t, n // STEP)
        }
        lower, scale, done = {}, [], []
        for s in range(STEP):
            pivot = columns[t][s][s : s + 1]
            for m in range(s):
                pivot = pivot - lower[s, m] * lower[s, m]
            scale.append(lax.rsqrt(pivot))
            for q in range(s + 1, STEP):
                entry = columns[t][s][q : q + 1]
                for m in range(s):
                    entry = entry - lower[q, m] * lower[s, m]
                lower[q, s] = entry * scale[s]
            line = tiles[t][s : s + 1]
            for m in range(s):
                line = line - lower[s, m] * done[m]
            done.append(line * scale[s])
        for u in range(t + 1, n // STEP):
            factors = []
            for s in range(STEP):
                factor = columns[u][s]
                for m in range(s):
                    factor = factor - factors[m] * lower[s, m]
                factors.append(factor * scale[s])
                tiles[u] = tiles[u] - factors[s] * done[s]
        for s in range(STEP):
            tiles[t] = jnp.where(row == s, done[s], tiles[t])
    return jnp.concatenate(tiles, axis=0)[:, n:]


def inverse_factor_kernel(packed_ref, inverse_ref, work_ref):
    n = inverse_ref.shape[0]
    block, width = n // XN, packed_ref.shape[2] // 2
    for b in range(XN):
        rows = jnp.concatenate([packed_ref[b, :, :width], packed_ref[b, :, width:]], axis=0)
        here = pl.ds(b * block, block)
        for j in range(XN - 1):
            c = (b + j) % XN * block
            work_ref[here, c : c + block] = rows[:, j * block : (j + 1) * block]
        below = (b + 1) % XN * block
        work_ref[below : below + block, b * block : (b + 1) * block] = rows[:, block : 2 * block].T
    work_ref[:, n:] = eye(n)
    for top in range(0, n, PANEL):
        end = top + PANEL
        own = inverse_factor_of_panel(work_ref[top:end, top:end])
        done = jnp.dot(own, work_ref[top:end], precision=HIGHEST, preferred_element_type=F32)
        inverse_ref[top:end] = done[:, n:]
        if end < n:
            below = lax.dot_general(
                work_ref[end:, top:end], own, (((1,), (1,)), ((), ())),
                precision=HIGHEST, preferred_element_type=F32,
            )
            work_ref[end:] = work_ref[end:] - jnp.dot(
                below, done, precision=HIGHEST, preferred_element_type=F32
            )


VMEM = pl.BlockSpec(memory_space=pltpu.VMEM)
SMEM = pl.BlockSpec(memory_space=pltpu.SMEM)


def inverse_factor(packed, n):
    return pl.pallas_call(
        inverse_factor_kernel,
        out_shape=jax.ShapeDtypeStruct((n, n), F32),
        in_specs=[VMEM],
        out_specs=VMEM,
        scratch_shapes=[pltpu.VMEM((n, 2 * n), F32)],
        compiler_params=pltpu.CompilerParams(vmem_limit_bytes=16 * MIB),
        cost_estimate=pl.CostEstimate(flops=FACTOR_COST, bytes_accessed=2**10, transcendentals=0),
        name="inverse_factor",
    )(packed)


def range_product(turned, own, base):
    total = None
    for step in range(3):
        part = turned.astype(BF16)
        turned = turned - part.astype(F32)
        term = jnp.dot(part, own, preferred_element_type=F32)
        term -= jnp.dot(part, base, preferred_element_type=F32)
        total = term if total is None else total + term
    return total


def products_kernel(
    core_ref, mine_ref, other_ref, own_ref, sketch_ref,
    first_ref, second_ref, range_ref, held_first, held_second, held_range, sems,
):
    half = mine_ref.shape[0]
    ff, rank = sketch_ref.shape
    block, slab = rank // XN, ff // XN
    gram = jnp.zeros((rank, rank), F32)
    delta = jnp.zeros((rank, ff), F32)
    copies = []
    for i, load_ref in enumerate((mine_ref, other_ref)):
        rows = pl.ds(pl.multiple_of((core_ref[0] ^ i) * half, half), half)
        own = own_ref[rows, :]
        base_sketch = (
            load_ref[:, ff : ff + rank].astype(F32)
            + load_ref[:, ff + rank : ff + 2 * rank].astype(F32)
            + load_ref[:, ff + 2 * rank :].astype(F32)
        )
        range_rows = jnp.dot(own, sketch_ref[...], preferred_element_type=F32) - base_sketch
        held_range[i] = range_rows
        copies.append(pltpu.make_async_copy(held_range.at[i], range_ref.at[rows], sems.at[i]))
        copies[i].start()
        turned = range_rows.T
        gram += jnp.dot(turned, range_rows, precision=HIGHEST, preferred_element_type=F32)
        delta += range_product(turned, own, load_ref[:, :ff])
    for b in range(XN):
        mine = gram[b * block : (b + 1) * block]
        kept = jnp.concatenate(
            [mine[:, (b + j) % XN * block :][:, :block] for j in range(XN - 1)], axis=1
        )
        packed = jnp.concatenate([kept[: block // 2], kept[block // 2 :]], axis=1)
        held_first[b, : block // 2, :] = packed
        held_first[b, block // 2 :, :] = delta[:FIRST, b * slab : (b + 1) * slab]
    copies.append(pltpu.make_async_copy(held_first, first_ref, sems.at[2]))
    copies[2].start()
    for b in range(XN):
        held_second[b] = delta[FIRST:, b * slab : (b + 1) * slab]
    copies.append(pltpu.make_async_copy(held_second, second_ref, sems.at[3]))
    copies[3].start()
    for copy in copies:
        copy.wait()


def products(core, mine, other, own, sketch):
    rows, ff = own.shape
    rank = sketch.shape[1]
    first = (XN, rank // XN // 2 + FIRST, ff // XN)
    second = (XN, rank - FIRST, ff // XN)
    return pl.pallas_call(
        products_kernel,
        out_shape=[jax.ShapeDtypeStruct(shape, F32) for shape in (first, second, (rows, rank))],
        in_specs=[SMEM] + [VMEM] * 4,
        out_specs=[pl.BlockSpec(memory_space=pltpu.HBM)] * 3,
        scratch_shapes=[
            pltpu.VMEM(first, F32),
            pltpu.VMEM(second, F32),
            pltpu.VMEM((CN, rows // CN, rank), F32),
            pltpu.SemaphoreType.DMA((4,)),
        ],
        compiler_params=pltpu.CompilerParams(vmem_limit_bytes=32 * MIB),
        cost_estimate=pl.CostEstimate(flops=5 * 10**9, bytes_accessed=2**10, transcendentals=0),
        name="products",
    )(core, mine, other, own, sketch)


def finished_kernel(inverse_ref, *refs):
    pairs, (out_ref, sums_ref) = refs[:-2], refs[-2:]
    rank = inverse_ref.shape[0]
    top = 0
    for i in range(0, len(pairs), 2):
        end = top + pairs[i].shape[0]
        sums_ref[top:end] = pairs[i][...] + pairs[i + 1][...]
        top = end
    values = jnp.dot(
        inverse_ref[...], sums_ref[...], precision=HIGHEST, preferred_element_type=F32
    )
    most = jnp.max(jnp.max(jnp.abs(values), axis=0, keepdims=True), axis=1, keepdims=True)
    power = jnp.floor(jnp.log(jnp.maximum(most, 1e-30)) * (1 / math.log(2)))
    out_ref[:rank] = values * jnp.exp2(TOP_POWER - power)
    out_ref[rank:] = jnp.broadcast_to(power, (out_ref.shape[0] - rank, out_ref.shape[1]))


def finished(inverse, pairs):
    rank, slab = inverse.shape[0], pairs[0].shape[1]
    return pl.pallas_call(
        finished_kernel,
        out_shape=jax.ShapeDtypeStruct((rank + 16, slab), F32),
        in_specs=[VMEM] * (1 + len(pairs)),
        out_specs=VMEM,
        scratch_shapes=[pltpu.VMEM((rank, slab), F32)],
        compiler_params=pltpu.CompilerParams(vmem_limit_bytes=16 * MIB),
        name="finished",
    )(inverse, *pairs)


def assembled_kernel(blocks_ref, out_ref, held_ref, sems):
    rank, slab = held_ref.shape[1:]
    copies = []
    for b in range(XN):
        scale = jnp.exp2(blocks_ref[b, rank : rank + 1] - TOP_POWER)
        held_ref[b] = blocks_ref[b, :rank] * scale
        copy = pltpu.make_async_copy(
            held_ref.at[b], out_ref.at[:, pl.ds(b * slab, slab)], sems.at[b]
        )
        copy.start()
        copies.append(copy)
    for copy in copies:
        copy.wait()


def assembled(blocks):
    rank, slab = blocks.shape[1] - 16, blocks.shape[2]
    return pl.pallas_call(
        assembled_kernel,
        out_shape=jax.ShapeDtypeStruct((rank, XN * slab), F32),
        in_specs=[VMEM],
        out_specs=pl.BlockSpec(memory_space=pl.ANY),
        scratch_shapes=[pltpu.VMEM((XN, rank, slab), F32), pltpu.SemaphoreType.DMA((XN,))],
        compiler_params=pltpu.CompilerParams(vmem_limit_bytes=16 * MIB),
        name="assembled",
    )(blocks)


def per_device(counts, up_weights, sketch):
    rows, ff = up_weights.shape[1:]
    rank = sketch.shape[1]
    piece = rows // 64
    own = up_weights[0].reshape(YN, FN, NN, CN, piece, ff).transpose(3, 0, 2, 1, 4, 5)
    members = CN * YN * NN
    own = own.reshape(members, FN * piece, ff)

    lane = lax.broadcasted_iota(jnp.int32, (members, FN * piece, 128), 2)
    count = counts[0]
    tag = jnp.where(lane == 0, count // 64, jnp.where(lane == 1, count % 64, 0)).astype(BF16)
    got = lax.all_to_all(
        jnp.concatenate([own, tag], axis=2), "exp", 0, 0, axis_index_groups=CYN_GROUPS
    )
    freq = got[:, 0, ff].astype(F32) * 64 + got[:, 0, ff + 1].astype(F32)
    weighted = jnp.sum(freq[:, None, None] * got[:, :, :ff].astype(F32), axis=0)
    freq_sum = jnp.broadcast_to(jnp.sum(freq), (FN, piece, 128))

    sums = lax.all_to_all(
        jnp.concatenate([weighted.reshape(FN, piece, ff), freq_sum], axis=2),
        "exp", 0, 0, axis_index_groups=FAR_GROUPS,
    )
    sums = jnp.sum(sums, axis=0)
    base_rows = sums[:, :ff] / sums[:, ff : ff + 1]
    base_piece = base_rows.astype(BF16)
    sketched = jnp.dot(base_rows, sketch.astype(F32), precision=HIGHEST)

    wide = ff + 3 * rank
    load = jnp.concatenate([base_piece] + parts_of(sketched), axis=1)
    load = lax.all_to_all(
        jnp.broadcast_to(load, (FN, piece, wide)), "exp", 0, 0, axis_index_groups=FAR_GROUPS
    ).reshape(FN * piece, wide)
    load = lax.all_to_all(
        jnp.broadcast_to(load, (YN * NN, FN * piece, wide)),
        "exp", 0, 0, axis_index_groups=YN_GROUPS,
    ).reshape(rows // CN, wide)
    other = lax.ppermute(load, "exp", OTHER_CORE)

    core, own = (lax.axis_index("exp") % CN).reshape(1), own.reshape(rows, ff)

    def to_owners(blocks):
        return lax.all_to_all(blocks, "grp", 0, 0, axis_index_groups=X_GROUPS)

    first, second, range_rows = products(core, load, other, own, sketch)
    first, second = to_owners(first), to_owners(second)
    first = jnp.sum(first, axis=0)
    first_came = lax.ppermute(first, "grp", OTHER_HALF)
    second = jnp.sum(second, axis=0)
    second_came = lax.ppermute(second, "grp", OTHER_HALF)
    packed = rank // XN // 2
    gram = first[:packed] + first_came[:packed]
    inverse = inverse_factor(to_owners(jnp.broadcast_to(gram, (XN,) + gram.shape)), rank)
    chunks = [first[packed:], first_came[packed:], second, second_came]
    inverse, chunks = lax.optimization_barrier((inverse, chunks))
    block = finished(inverse, chunks).astype(jnp.float16)
    blocks = to_owners(jnp.broadcast_to(block, (XN,) + block.shape))
    coeff = assembled(blocks.astype(F32))

    ortho = lax.dot_general(
        range_rows, inverse, (((1,), (1,)), ((), ())), precision=HIGHEST
    )
    basis = ortho * math.sqrt(rows * lax.axis_size("grp"))
    basis = basis.reshape(CN, YN, NN, FN, piece, rank).transpose(1, 3, 2, 0, 4, 5)
    return (base_piece, basis.reshape(1, rows, rank), coeff[None])


def solution(mesh):
    placed = (P("exp"), P("exp", "grp", None), P())
    return jax.shard_map(
        per_device,
        mesh=mesh,
        in_specs=placed,
        out_specs=(P(("grp", "exp"), None), P("exp", "grp", None), P("exp", None, None)),
        check_vma=False,
    )
```

```python
import math

import jax
import jax.numpy as jnp
from jax import lax
from jax.experimental import pallas as pl
from jax.experimental.pallas import tpu as pltpu
from jax.sharding import PartitionSpec as P

F32, BF16 = jnp.float32, jnp.bfloat16
HIGHEST = lax.Precision.HIGHEST
MIB = 2**20

YN, FN, NN, CN, XN = 4, 4, 2, 2, 4


def at(y, far, near, core):
    return y * 16 + (2 * far + near) * 2 + core


CYN_GROUPS = [
    [at(y, f, n, c) for c in range(CN) for y in range(YN) for n in range(NN)] for f in range(FN)
]
YN_GROUPS = [
    [at(y, f, n, c) for y in range(YN) for n in range(NN)] for f in range(FN) for c in range(CN)
]
FAR_GROUPS = [
    [at(y, f, n, c) for f in range(FN)]
    for y in range(YN) for n in range(NN) for c in range(CN)
]
OTHER_CORE = [(i, i ^ 1) for i in range(64)]
OTHER_HALF = [(i, i ^ 4) for i in range(8)]
X_GROUPS = [[h * XN + x for x in range(XN)] for h in range(2)]

PANEL, STEP = 64, 8
TOP_POWER = 13
FIRST = 64
FACTOR_COST = 2**29


def parts_of(value):
    first = lax.reduce_precision(value, 8, 7)
    rest = value - first
    second = lax.reduce_precision(rest, 8, 7)
    return [first.astype(BF16), second.astype(BF16), (rest - second).astype(BF16)]


def eye(n):
    row, col = (lax.broadcasted_iota(jnp.int32, (n, n), d) for d in (0, 1))
    return jnp.where(row == col, 1.0, 0.0).astype(F32)


def inverse_factor_of_panel(square):
    n = square.shape[0]
    work = jnp.concatenate([square, eye(n)], axis=1)
    tiles = [work[t : t + STEP] for t in range(0, n, STEP)]
    row = lax.broadcasted_iota(jnp.int32, tiles[0].shape, 0)
    for t in range(n // STEP):
        columns = {
            u: [
                jnp.broadcast_to(tiles[u][:, t * STEP + s :][:, :1], tiles[u].shape)
                for s in range(STEP)
            ]
            for u in range(t, n // STEP)
        }
        lower, scale, done = {}, [], []
        for s in range(STEP):
            pivot = columns[t][s][s : s + 1]
            for m in range(s):
                pivot = pivot - lower[s, m] * lower[s, m]
            scale.append(lax.rsqrt(pivot))
            for q in range(s + 1, STEP):
                entry = columns[t][s][q : q + 1]
                for m in range(s):
                    entry = entry - lower[q, m] * lower[s, m]
                lower[q, s] = entry * scale[s]
            line = tiles[t][s : s + 1]
            for m in range(s):
                line = line - lower[s, m] * done[m]
            done.append(line * scale[s])
        for u in range(t + 1, n // STEP):
            factors = []
            for s in range(STEP):
                factor = columns[u][s]
                for m in range(s):
                    factor = factor - factors[m] * lower[s, m]
                factors.append(factor * scale[s])
                tiles[u] = tiles[u] - factors[s] * done[s]
        for s in range(STEP):
            tiles[t] = jnp.where(row == s, done[s], tiles[t])
    return jnp.concatenate(tiles, axis=0)[:, n:]


def inverse_factor_kernel(packed_ref, inverse_ref, work_ref):
    n = inverse_ref.shape[0]
    block, width = n // XN, packed_ref.shape[2] // 2
    for b in range(XN):
        rows = jnp.concatenate([packed_ref[b, :, :width], packed_ref[b, :, width:]], axis=0)
        here = pl.ds(b * block, block)
        for j in range(XN - 1):
            c = (b + j) % XN * block
            work_ref[here, c : c + block] = rows[:, j * block : (j + 1) * block]
        below = (b + 1) % XN * block
        work_ref[below : below + block, b * block : (b + 1) * block] = rows[:, block : 2 * block].T
    work_ref[:, n:] = eye(n)
    for top in range(0, n, PANEL):
        end = top + PANEL
        own = inverse_factor_of_panel(work_ref[top:end, top:end])
        done = jnp.dot(own, work_ref[top:end], precision=HIGHEST, preferred_element_type=F32)
        inverse_ref[top:end] = done[:, n:]
        if end < n:
            below = lax.dot_general(
                work_ref[end:, top:end], own, (((1,), (1,)), ((), ())),
                precision=HIGHEST, preferred_element_type=F32,
            )
            work_ref[end:] = work_ref[end:] - jnp.dot(
                below, done, precision=HIGHEST, preferred_element_type=F32
            )


VMEM = pl.BlockSpec(memory_space=pltpu.VMEM)
SMEM = pl.BlockSpec(memory_space=pltpu.SMEM)


def inverse_factor(packed, n):
    return pl.pallas_call(
        inverse_factor_kernel,
        out_shape=jax.ShapeDtypeStruct((n, n), F32),
        in_specs=[VMEM],
        out_specs=VMEM,
        scratch_shapes=[pltpu.VMEM((n, 2 * n), F32)],
        compiler_params=pltpu.CompilerParams(vmem_limit_bytes=16 * MIB),
        cost_estimate=pl.CostEstimate(flops=FACTOR_COST, bytes_accessed=2**10, transcendentals=0),
        name="inverse_factor",
    )(packed)


def range_product(turned, own, base):
    total = None
    for step in range(3):
        part = turned.astype(BF16)
        turned = turned - part.astype(F32)
        term = jnp.dot(part, own, preferred_element_type=F32)
        term -= jnp.dot(part, base, preferred_element_type=F32)
        total = term if total is None else total + term
    return total


def weighted_kernel(got_ref, out_ref):
    members, rows, wide = got_ref.shape
    ff = wide - 128
    piece = rows // FN
    total, freq_sum = jnp.zeros((rows, ff), F32), jnp.zeros((1, 1), F32)
    for j in range(members):
        tag = got_ref[j, :16, ff:].astype(F32)
        freq = tag[:1, :1] * 64 + tag[:1, 1:2]
        freq_sum += freq
        total += freq * got_ref[j, :, :ff].astype(F32)
    for f in range(FN):
        out_ref[f, :, :ff] = total[f * piece : (f + 1) * piece]
        out_ref[f, :, ff:] = jnp.broadcast_to(freq_sum, (piece, 128))


def weighted(got):
    members, rows, wide = got.shape
    return pl.pallas_call(
        weighted_kernel,
        out_shape=jax.ShapeDtypeStruct((FN, rows // FN, wide), F32),
        in_specs=[VMEM],
        out_specs=VMEM,
        compiler_params=pltpu.CompilerParams(vmem_limit_bytes=16 * MIB),
        cost_estimate=pl.CostEstimate(flops=2**20, bytes_accessed=2**21, transcendentals=0),
        name="weighted",
    )(got)


def half_products(core, load_ref, own_ref, sketch_ref, range_ref):
    half = load_ref.shape[0]
    ff, rank = sketch_ref.shape
    own = own_ref[pl.ds(pl.multiple_of(core * half, half), half), :]
    base_sketch = (
        load_ref[:, ff : ff + rank].astype(F32)
        + load_ref[:, ff + rank : ff + 2 * rank].astype(F32)
        + load_ref[:, ff + 2 * rank :].astype(F32)
    )
    range_rows = jnp.dot(own, sketch_ref[...], preferred_element_type=F32) - base_sketch
    range_ref[...] = range_rows
    turned = range_rows.T
    gram = jnp.dot(turned, range_rows, precision=HIGHEST, preferred_element_type=F32)
    return gram, range_product(turned, own, load_ref[:, :ff])


def own_products_kernel(core_ref, load_ref, own_ref, sketch_ref, gram_ref, delta_ref, range_ref):
    gram_ref[...], delta_ref[...] = half_products(
        core_ref[0], load_ref, own_ref, sketch_ref, range_ref
    )


def products_kernel(
    core_ref, load_ref, own_ref, sketch_ref, own_gram_ref, own_delta_ref,
    first_ref, second_ref, range_ref,
):
    ff, rank = sketch_ref.shape
    block, slab = rank // XN, ff // XN
    gram, delta = half_products(1 - core_ref[0], load_ref, own_ref, sketch_ref, range_ref)
    gram += own_gram_ref[...]
    delta += own_delta_ref[...]
    for b in range(XN):
        mine = gram[b * block : (b + 1) * block]
        kept = jnp.concatenate(
            [mine[:, (b + j) % XN * block :][:, :block] for j in range(XN - 1)], axis=1
        )
        packed = jnp.concatenate([kept[: block // 2], kept[block // 2 :]], axis=1)
        first_ref[b, : block // 2, :] = packed
        first_ref[b, block // 2 :, :] = delta[:FIRST, b * slab : (b + 1) * slab]
        second_ref[b] = delta[FIRST:, b * slab : (b + 1) * slab]


def own_products(core, load, own, sketch):
    half, (ff, rank) = load.shape[0], sketch.shape
    return pl.pallas_call(
        own_products_kernel,
        out_shape=[jax.ShapeDtypeStruct(shape, F32) for shape in ((rank, rank), (rank, ff), (half, rank))],
        in_specs=[SMEM] + [VMEM] * 3,
        out_specs=[VMEM] * 3,
        compiler_params=pltpu.CompilerParams(vmem_limit_bytes=32 * MIB),
        cost_estimate=pl.CostEstimate(flops=2 * 10**9, bytes_accessed=2**10, transcendentals=0),
        name="own_products",
    )(core, load, own, sketch)


def products(core, load, own, sketch, own_gram, own_delta):
    half, (ff, rank) = load.shape[0], sketch.shape
    first = (XN, rank // XN // 2 + FIRST, ff // XN)
    second = (XN, rank - FIRST, ff // XN)
    return pl.pallas_call(
        products_kernel,
        out_shape=[jax.ShapeDtypeStruct(shape, F32) for shape in (first, second, (half, rank))],
        in_specs=[SMEM] + [VMEM] * 5,
        out_specs=[VMEM] * 3,
        compiler_params=pltpu.CompilerParams(vmem_limit_bytes=32 * MIB),
        cost_estimate=pl.CostEstimate(flops=3 * 10**9, bytes_accessed=2**10, transcendentals=0),
        name="products",
    )(core, load, own, sketch, own_gram, own_delta)


def finished_kernel(inverse_ref, *refs):
    pairs, (out_ref, sums_ref) = refs[:-2], refs[-2:]
    rank = inverse_ref.shape[0]
    top = 0
    for i in range(0, len(pairs), 2):
        end = top + pairs[i].shape[0]
        sums_ref[top:end] = pairs[i][...] + pairs[i + 1][...]
        top = end
    values = jnp.dot(
        inverse_ref[...], sums_ref[...], precision=HIGHEST, preferred_element_type=F32
    )
    most = jnp.max(jnp.max(jnp.abs(values), axis=0, keepdims=True), axis=1, keepdims=True)
    power = jnp.floor(jnp.log(jnp.maximum(most, 1e-30)) * (1 / math.log(2)))
    out_ref[:rank] = values * jnp.exp2(TOP_POWER - power)
    out_ref[rank:] = jnp.broadcast_to(power, (out_ref.shape[0] - rank, out_ref.shape[1]))


def finished(inverse, pairs):
    rank, slab = inverse.shape[0], pairs[0].shape[1]
    return pl.pallas_call(
        finished_kernel,
        out_shape=jax.ShapeDtypeStruct((rank + 16, slab), F32),
        in_specs=[VMEM] * (1 + len(pairs)),
        out_specs=VMEM,
        scratch_shapes=[pltpu.VMEM((rank, slab), F32)],
        compiler_params=pltpu.CompilerParams(vmem_limit_bytes=16 * MIB),
        name="finished",
    )(inverse, *pairs)


def assembled_kernel(blocks_ref, out_ref, held_ref, sems):
    rank, slab = held_ref.shape[1:]
    copies = []
    for b in range(XN):
        scale = jnp.exp2(blocks_ref[b, rank : rank + 1] - TOP_POWER)
        held_ref[b] = blocks_ref[b, :rank] * scale
        copy = pltpu.make_async_copy(
            held_ref.at[b], out_ref.at[:, pl.ds(b * slab, slab)], sems.at[b]
        )
        copy.start()
        copies.append(copy)
    for copy in copies:
        copy.wait()


def assembled(blocks):
    rank, slab = blocks.shape[1] - 16, blocks.shape[2]
    return pl.pallas_call(
        assembled_kernel,
        out_shape=jax.ShapeDtypeStruct((rank, XN * slab), F32),
        in_specs=[VMEM],
        out_specs=pl.BlockSpec(memory_space=pl.ANY),
        scratch_shapes=[pltpu.VMEM((XN, rank, slab), F32), pltpu.SemaphoreType.DMA((XN,))],
        compiler_params=pltpu.CompilerParams(vmem_limit_bytes=16 * MIB),
        name="assembled",
    )(blocks)


def per_device(counts, up_weights, sketch):
    rows, ff = up_weights.shape[1:]
    rank = sketch.shape[1]
    piece = rows // 64
    own = up_weights[0].reshape(YN, FN, NN, CN, piece, ff).transpose(3, 0, 2, 1, 4, 5)
    members = CN * YN * NN
    own = own.reshape(members, FN * piece, ff)

    lane = lax.broadcasted_iota(jnp.int32, (members, FN * piece, 128), 2)
    count = counts[0]
    tag = jnp.where(lane == 0, count // 64, jnp.where(lane == 1, count % 64, 0)).astype(BF16)
    got = lax.all_to_all(
        jnp.concatenate([own, tag], axis=2), "exp", 0, 0, axis_index_groups=CYN_GROUPS
    )

    sums = lax.all_to_all(weighted(got), "exp", 0, 0, axis_index_groups=FAR_GROUPS)
    sums = jnp.sum(sums, axis=0)
    base_rows = sums[:, :ff] / sums[:, ff : ff + 1]
    base_piece = base_rows.astype(BF16)
    sketched = jnp.dot(base_rows, sketch.astype(F32), precision=HIGHEST)

    wide = ff + 3 * rank
    load = jnp.concatenate([base_piece] + parts_of(sketched), axis=1)
    load = lax.all_to_all(
        jnp.broadcast_to(load, (FN, piece, wide)), "exp", 0, 0, axis_index_groups=FAR_GROUPS
    ).reshape(FN * piece, wide)
    load = lax.all_to_all(
        jnp.broadcast_to(load, (YN * NN, FN * piece, wide)),
        "exp", 0, 0, axis_index_groups=YN_GROUPS,
    ).reshape(rows // CN, wide)
    other = lax.ppermute(load, "exp", OTHER_CORE)

    core, own = (lax.axis_index("exp") % CN).reshape(1), own.reshape(rows, ff)

    def to_owners(blocks):
        return lax.all_to_all(blocks, "grp", 0, 0, axis_index_groups=X_GROUPS)

    own_gram, own_delta, own_range = own_products(core, load, own, sketch)
    first, second, other_range = products(core, other, own, sketch, own_gram, own_delta)
    first, second = to_owners(first), to_owners(second)
    first = jnp.sum(first, axis=0)
    first_came = lax.ppermute(first, "grp", OTHER_HALF)
    second = jnp.sum(second, axis=0)
    second_came = lax.ppermute(second, "grp", OTHER_HALF)
    packed = rank // XN // 2
    gram = first[:packed] + first_came[:packed]
    inverse = inverse_factor(to_owners(jnp.broadcast_to(gram, (XN,) + gram.shape)), rank)
    chunks = [first[packed:], first_came[packed:], second, second_came]
    inverse, chunks = lax.optimization_barrier((inverse, chunks))
    block = finished(inverse, chunks).astype(jnp.float16)
    blocks = to_owners(jnp.broadcast_to(block, (XN,) + block.shape))
    coeff = assembled(blocks.astype(F32))

    scale = math.sqrt(rows * lax.axis_size("grp"))
    halves = [
        scale * lax.dot_general(half, inverse, (((1,), (1,)), ((), ())), precision=HIGHEST)
        for half in (own_range, other_range)
    ]
    on_first = core[0] == 0
    basis = jnp.stack(
        [jnp.where(on_first, halves[i], halves[1 - i]) for i in range(CN)]
    )
    basis = basis.reshape(CN, YN, NN, FN, piece, rank).transpose(1, 3, 2, 0, 4, 5)
    return (base_piece, basis.reshape(1, rows, rank), coeff[None])


def solution(mesh):
    placed = (P("exp"), P("exp", "grp", None), P())
    return jax.shard_map(
        per_device,
        mesh=mesh,
        in_specs=placed,
        out_specs=(P(("grp", "exp"), None), P("exp", "grp", None), P("exp", None, None)),
        check_vma=False,
    )
```

```python
import math

import jax
import jax.numpy as jnp
from jax import lax
from jax.experimental import pallas as pl
from jax.experimental.pallas import tpu as pltpu
from jax.sharding import PartitionSpec as P

F32, BF16 = jnp.float32, jnp.bfloat16
HIGHEST = lax.Precision.HIGHEST
MIB = 2**20

YN, FN, NN, CN, XN = 4, 4, 2, 2, 4


def at(y, far, near, core):
    return y * 16 + (2 * far + near) * 2 + core


CYN_GROUPS = [
    [at(y, f, n, c) for c in range(CN) for y in range(YN) for n in range(NN)] for f in range(FN)
]
YN_GROUPS = [
    [at(y, f, n, c) for y in range(YN) for n in range(NN)] for f in range(FN) for c in range(CN)
]
FAR_GROUPS = [
    [at(y, f, n, c) for f in range(FN)]
    for y in range(YN) for n in range(NN) for c in range(CN)
]
OTHER_CORE = [(i, i ^ 1) for i in range(64)]
ALONG_X = [[(i, i ^ k) for i in range(8)] for k in range(XN)]
OTHER_HALF = [(i, i ^ 4) for i in range(8)]
X_GROUPS = [[h * XN + x for x in range(XN)] for h in range(2)]

PANEL, STEP = 64, 8
TOP_POWER = 13
FIRST = 64
FACTOR_COST = 2**29


def parts_of(value):
    first = lax.reduce_precision(value, 8, 7)
    rest = value - first
    second = lax.reduce_precision(rest, 8, 7)
    return [first.astype(BF16), second.astype(BF16), (rest - second).astype(BF16)]


def eye(n):
    row, col = (lax.broadcasted_iota(jnp.int32, (n, n), d) for d in (0, 1))
    return jnp.where(row == col, 1.0, 0.0).astype(F32)


def inverse_factor_of_panel(square):
    n = square.shape[0]
    work = jnp.concatenate([square, eye(n)], axis=1)
    tiles = [work[t : t + STEP] for t in range(0, n, STEP)]
    row = lax.broadcasted_iota(jnp.int32, tiles[0].shape, 0)
    for t in range(n // STEP):
        columns = {
            u: [
                jnp.broadcast_to(tiles[u][:, t * STEP + s :][:, :1], tiles[u].shape)
                for s in range(STEP)
            ]
            for u in range(t, n // STEP)
        }
        lower, scale, done = {}, [], []
        for s in range(STEP):
            pivot = columns[t][s][s : s + 1]
            for m in range(s):
                pivot = pivot - lower[s, m] * lower[s, m]
            scale.append(lax.rsqrt(pivot))
            for q in range(s + 1, STEP):
                entry = columns[t][s][q : q + 1]
                for m in range(s):
                    entry = entry - lower[q, m] * lower[s, m]
                lower[q, s] = entry * scale[s]
            line = tiles[t][s : s + 1]
            for m in range(s):
                line = line - lower[s, m] * done[m]
            done.append(line * scale[s])
        for u in range(t + 1, n // STEP):
            factors = []
            for s in range(STEP):
                factor = columns[u][s]
                for m in range(s):
                    factor = factor - factors[m] * lower[s, m]
                factors.append(factor * scale[s])
                tiles[u] = tiles[u] - factors[s] * done[s]
        for s in range(STEP):
            tiles[t] = jnp.where(row == s, done[s], tiles[t])
    return jnp.concatenate(tiles, axis=0)[:, n:]


def inverse_factor_kernel(packed_ref, inverse_ref, work_ref):
    n = inverse_ref.shape[0]
    block, width = n // XN, packed_ref.shape[2] // 2
    for b in range(XN):
        rows = jnp.concatenate([packed_ref[b, :, :width], packed_ref[b, :, width:]], axis=0)
        here = pl.ds(b * block, block)
        for j in range(XN - 1):
            c = (b + j) % XN * block
            work_ref[here, c : c + block] = rows[:, j * block : (j + 1) * block]
        below = (b + 1) % XN * block
        work_ref[below : below + block, b * block : (b + 1) * block] = rows[:, block : 2 * block].T
    work_ref[:, n:] = eye(n)
    for top in range(0, n, PANEL):
        end = top + PANEL
        own = inverse_factor_of_panel(work_ref[top:end, top:end])
        done = jnp.dot(own, work_ref[top:end], precision=HIGHEST, preferred_element_type=F32)
        inverse_ref[top:end] = done[:, n:]
        if end < n:
            below = lax.dot_general(
                work_ref[end:, top:end], own, (((1,), (1,)), ((), ())),
                precision=HIGHEST, preferred_element_type=F32,
            )
            work_ref[end:] = work_ref[end:] - jnp.dot(
                below, done, precision=HIGHEST, preferred_element_type=F32
            )


VMEM = pl.BlockSpec(memory_space=pltpu.VMEM)
SMEM = pl.BlockSpec(memory_space=pltpu.SMEM)


def inverse_factor(packed, n):
    return pl.pallas_call(
        inverse_factor_kernel,
        out_shape=jax.ShapeDtypeStruct((n, n), F32),
        in_specs=[VMEM],
        out_specs=VMEM,
        scratch_shapes=[pltpu.VMEM((n, 2 * n), F32)],
        compiler_params=pltpu.CompilerParams(vmem_limit_bytes=16 * MIB),
        cost_estimate=pl.CostEstimate(flops=FACTOR_COST, bytes_accessed=2**10, transcendentals=0),
        name="inverse_factor",
    )(packed)


def range_product(turned, own, base):
    total = None
    for step in range(3):
        part = turned.astype(BF16)
        turned = turned - part.astype(F32)
        term = jnp.dot(part, own, preferred_element_type=F32)
        term -= jnp.dot(part, base, preferred_element_type=F32)
        total = term if total is None else total + term
    return total


def weighted_kernel(got_ref, out_ref):
    members, rows, wide = got_ref.shape
    ff = wide - 128
    piece = rows // FN
    total, freq_sum = jnp.zeros((rows, ff), F32), jnp.zeros((1, 1), F32)
    for j in range(members):
        tag = got_ref[j, :16, ff:].astype(F32)
        freq = tag[:1, :1] * 64 + tag[:1, 1:2]
        freq_sum += freq
        total += freq * got_ref[j, :, :ff].astype(F32)
    for f in range(FN):
        out_ref[f, :, :ff] = total[f * piece : (f + 1) * piece]
        out_ref[f, :, ff:] = jnp.broadcast_to(freq_sum, (piece, 128))


def weighted(got):
    members, rows, wide = got.shape
    return pl.pallas_call(
        weighted_kernel,
        out_shape=jax.ShapeDtypeStruct((FN, rows // FN, wide), F32),
        in_specs=[VMEM],
        out_specs=VMEM,
        compiler_params=pltpu.CompilerParams(vmem_limit_bytes=16 * MIB),
        cost_estimate=pl.CostEstimate(flops=2**20, bytes_accessed=2**21, transcendentals=0),
        name="weighted",
    )(got)


def half_products(core, load_ref, own_ref, sketch_ref, range_ref):
    half = load_ref.shape[0]
    ff, rank = sketch_ref.shape
    own = own_ref[pl.ds(pl.multiple_of(core * half, half), half), :]
    base_sketch = (
        load_ref[:, ff : ff + rank].astype(F32)
        + load_ref[:, ff + rank : ff + 2 * rank].astype(F32)
        + load_ref[:, ff + 2 * rank :].astype(F32)
    )
    range_rows = jnp.dot(own, sketch_ref[...], preferred_element_type=F32) - base_sketch
    range_ref[...] = range_rows
    turned = range_rows.T
    gram = jnp.dot(turned, range_rows, precision=HIGHEST, preferred_element_type=F32)
    return gram, range_product(turned, own, load_ref[:, :ff])


def own_products_kernel(core_ref, load_ref, own_ref, sketch_ref, gram_ref, delta_ref, range_ref):
    gram_ref[...], delta_ref[...] = half_products(
        core_ref[0], load_ref, own_ref, sketch_ref, range_ref
    )


def products_kernel(
    place_ref, load_ref, own_ref, sketch_ref, own_gram_ref, own_delta_ref,
    first_ref, second_ref, range_ref,
):
    ff, rank = sketch_ref.shape
    block, slab = rank // XN, ff // XN
    core, x = place_ref[0], place_ref[1]
    gram, delta = half_products(1 - core, load_ref, own_ref, sketch_ref, range_ref)
    gram += own_gram_ref[...]
    delta += own_delta_ref[...]
    for b in range(XN):
        mine = gram[b * block : (b + 1) * block]
        kept = jnp.concatenate(
            [mine[:, (b + j) % XN * block :][:, :block] for j in range(XN - 1)], axis=1
        )
        packed = jnp.concatenate([kept[: block // 2], kept[block // 2 :]], axis=1)
        first_ref[b ^ x, : block // 2, :] = packed
        first_ref[b ^ x, block // 2 :, :] = delta[:FIRST, b * slab : (b + 1) * slab]
        second_ref[b] = delta[FIRST:, b * slab : (b + 1) * slab]


def own_products(core, load, own, sketch):
    half, (ff, rank) = load.shape[0], sketch.shape
    return pl.pallas_call(
        own_products_kernel,
        out_shape=[jax.ShapeDtypeStruct(shape, F32) for shape in ((rank, rank), (rank, ff), (half, rank))],
        in_specs=[SMEM] + [VMEM] * 3,
        out_specs=[VMEM] * 3,
        compiler_params=pltpu.CompilerParams(vmem_limit_bytes=32 * MIB),
        cost_estimate=pl.CostEstimate(flops=2 * 10**9, bytes_accessed=2**10, transcendentals=0),
        name="own_products",
    )(core, load, own, sketch)


def products(place, load, own, sketch, own_gram, own_delta):
    half, (ff, rank) = load.shape[0], sketch.shape
    first = (XN, rank // XN // 2 + FIRST, ff // XN)
    second = (XN, rank - FIRST, ff // XN)
    return pl.pallas_call(
        products_kernel,
        out_shape=[jax.ShapeDtypeStruct(shape, F32) for shape in (first, second, (half, rank))],
        in_specs=[SMEM] + [VMEM] * 5,
        out_specs=[VMEM] * 3,
        compiler_params=pltpu.CompilerParams(vmem_limit_bytes=32 * MIB),
        cost_estimate=pl.CostEstimate(flops=3 * 10**9, bytes_accessed=2**10, transcendentals=0),
        name="products",
    )(place, load, own, sketch, own_gram, own_delta)


def finished_kernel(inverse_ref, *refs):
    pairs, (out_ref, sums_ref) = refs[:-2], refs[-2:]
    rank = inverse_ref.shape[0]
    top = 0
    for i in range(0, len(pairs), 2):
        end = top + pairs[i].shape[0]
        sums_ref[top:end] = pairs[i][...] + pairs[i + 1][...]
        top = end
    values = jnp.dot(
        inverse_ref[...], sums_ref[...], precision=HIGHEST, preferred_element_type=F32
    )
    most = jnp.max(jnp.max(jnp.abs(values), axis=0, keepdims=True), axis=1, keepdims=True)
    power = jnp.floor(jnp.log(jnp.maximum(most, 1e-30)) * (1 / math.log(2)))
    out_ref[:rank] = values * jnp.exp2(TOP_POWER - power)
    out_ref[rank:] = jnp.broadcast_to(power, (out_ref.shape[0] - rank, out_ref.shape[1]))


def finished(inverse, pairs):
    rank, slab = inverse.shape[0], pairs[0].shape[1]
    return pl.pallas_call(
        finished_kernel,
        out_shape=jax.ShapeDtypeStruct((rank + 16, slab), F32),
        in_specs=[VMEM] * (1 + len(pairs)),
        out_specs=VMEM,
        scratch_shapes=[pltpu.VMEM((rank, slab), F32)],
        compiler_params=pltpu.CompilerParams(vmem_limit_bytes=16 * MIB),
        name="finished",
    )(inverse, *pairs)


def assembled_kernel(blocks_ref, out_ref, held_ref, sems):
    rank, slab = held_ref.shape[1:]
    copies = []
    for b in range(XN):
        scale = jnp.exp2(blocks_ref[b, rank : rank + 1] - TOP_POWER)
        held_ref[b] = blocks_ref[b, :rank] * scale
        copy = pltpu.make_async_copy(
            held_ref.at[b], out_ref.at[:, pl.ds(b * slab, slab)], sems.at[b]
        )
        copy.start()
        copies.append(copy)
    for copy in copies:
        copy.wait()


def assembled(blocks):
    rank, slab = blocks.shape[1] - 16, blocks.shape[2]
    return pl.pallas_call(
        assembled_kernel,
        out_shape=jax.ShapeDtypeStruct((rank, XN * slab), F32),
        in_specs=[VMEM],
        out_specs=pl.BlockSpec(memory_space=pl.ANY),
        scratch_shapes=[pltpu.VMEM((XN, rank, slab), F32), pltpu.SemaphoreType.DMA((XN,))],
        compiler_params=pltpu.CompilerParams(vmem_limit_bytes=16 * MIB),
        name="assembled",
    )(blocks)


def per_device(counts, up_weights, sketch):
    rows, ff = up_weights.shape[1:]
    rank = sketch.shape[1]
    piece = rows // 64
    own = up_weights[0].reshape(YN, FN, NN, CN, piece, ff).transpose(3, 0, 2, 1, 4, 5)
    members = CN * YN * NN
    own = own.reshape(members, FN * piece, ff)

    lane = lax.broadcasted_iota(jnp.int32, (members, FN * piece, 128), 2)
    count = counts[0]
    tag = jnp.where(lane == 0, count // 64, jnp.where(lane == 1, count % 64, 0)).astype(BF16)
    got = lax.all_to_all(
        jnp.concatenate([own, tag], axis=2), "exp", 0, 0, axis_index_groups=CYN_GROUPS
    )

    sums = lax.all_to_all(weighted(got), "exp", 0, 0, axis_index_groups=FAR_GROUPS)
    sums = jnp.sum(sums, axis=0)
    base_rows = sums[:, :ff] / sums[:, ff : ff + 1]
    base_piece = base_rows.astype(BF16)
    sketched = jnp.dot(base_rows, sketch.astype(F32), precision=HIGHEST)

    wide = ff + 3 * rank
    load = jnp.concatenate([base_piece] + parts_of(sketched), axis=1)
    load = lax.all_to_all(
        jnp.broadcast_to(load, (FN, piece, wide)), "exp", 0, 0, axis_index_groups=FAR_GROUPS
    ).reshape(FN * piece, wide)
    load = lax.all_to_all(
        jnp.broadcast_to(load, (YN * NN, FN * piece, wide)),
        "exp", 0, 0, axis_index_groups=YN_GROUPS,
    ).reshape(rows // CN, wide)
    other = lax.ppermute(load, "exp", OTHER_CORE)

    core, own = (lax.axis_index("exp") % CN).reshape(1), own.reshape(rows, ff)

    def to_owners(blocks):
        return lax.all_to_all(blocks, "grp", 0, 0, axis_index_groups=X_GROUPS)

    own_gram, own_delta, own_range = own_products(core, load, own, sketch)
    place = jnp.concatenate([core, (lax.axis_index("grp") % XN).reshape(1)])
    first, second, other_range = products(place, other, own, sketch, own_gram, own_delta)
    first = first[0] + sum(lax.ppermute(first[k], "grp", ALONG_X[k]) for k in (2, 3, 1))
    first_came = lax.ppermute(first, "grp", OTHER_HALF)
    second = jnp.sum(to_owners(second), axis=0)
    second_came = lax.ppermute(second, "grp", OTHER_HALF)
    packed = rank // XN // 2
    gram = first[:packed] + first_came[:packed]
    inverse = inverse_factor(to_owners(jnp.broadcast_to(gram, (XN,) + gram.shape)), rank)
    chunks = [first[packed:], first_came[packed:], second, second_came]
    inverse, chunks = lax.optimization_barrier((inverse, chunks))
    block = finished(inverse, chunks).astype(jnp.float16)
    blocks = to_owners(jnp.broadcast_to(block, (XN,) + block.shape))
    coeff = assembled(blocks.astype(F32))

    scale = math.sqrt(rows * lax.axis_size("grp"))
    halves = [
        scale * lax.dot_general(half, inverse, (((1,), (1,)), ((), ())), precision=HIGHEST)
        for half in (own_range, other_range)
    ]
    on_first = core[0] == 0
    basis = jnp.stack(
        [jnp.where(on_first, halves[i], halves[1 - i]) for i in range(CN)]
    )
    basis = basis.reshape(CN, YN, NN, FN, piece, rank).transpose(1, 3, 2, 0, 4, 5)
    return (base_piece, basis.reshape(1, rows, rank), coeff[None])


def solution(mesh):
    placed = (P("exp"), P("exp", "grp", None), P())
    return jax.shard_map(
        per_device,
        mesh=mesh,
        in_specs=placed,
        out_specs=(P(("grp", "exp"), None), P("exp", "grp", None), P("exp", None, None)),
        check_vma=False,
    )
```

```python
import math

import jax
import jax.numpy as jnp
from jax import lax
from jax.experimental import pallas as pl
from jax.experimental.pallas import tpu as pltpu
from jax.sharding import PartitionSpec as P

F32, BF16 = jnp.float32, jnp.bfloat16
HIGHEST = lax.Precision.HIGHEST
MIB = 2**20

YN, FN, NN, CN, XN = 4, 4, 2, 2, 4


def at(y, far, near, core):
    return y * 16 + (2 * far + near) * 2 + core


CYN_GROUPS = [
    [at(y, f, n, c) for c in range(CN) for y in range(YN) for n in range(NN)] for f in range(FN)
]
YN_GROUPS = [
    [at(y, f, n, c) for y in range(YN) for n in range(NN)] for f in range(FN) for c in range(CN)
]
FAR_GROUPS = [
    [at(y, f, n, c) for f in range(FN)]
    for y in range(YN) for n in range(NN) for c in range(CN)
]
OTHER_CORE = [(i, i ^ 1) for i in range(64)]
OTHER_HALF = [(i, i ^ 4) for i in range(8)]
X_GROUPS = [[h * XN + x for x in range(XN)] for h in range(2)]

PANEL, STEP = 64, 8
TOP_POWER = 13
FIRST = 96
FACTOR_COST = 2**29


def parts_of(value):
    first = lax.reduce_precision(value, 8, 7)
    rest = value - first
    second = lax.reduce_precision(rest, 8, 7)
    return [first.astype(BF16), second.astype(BF16), (rest - second).astype(BF16)]


def eye(n):
    row, col = (lax.broadcasted_iota(jnp.int32, (n, n), d) for d in (0, 1))
    return jnp.where(row == col, 1.0, 0.0).astype(F32)


def inverse_factor_of_panel(square):
    n = square.shape[0]
    work = jnp.concatenate([square, eye(n)], axis=1)
    tiles = [work[t : t + STEP] for t in range(0, n, STEP)]
    row = lax.broadcasted_iota(jnp.int32, tiles[0].shape, 0)
    for t in range(n // STEP):
        columns = {
            u: [
                jnp.broadcast_to(tiles[u][:, t * STEP + s :][:, :1], tiles[u].shape)
                for s in range(STEP)
            ]
            for u in range(t, n // STEP)
        }
        lower, scale, done = {}, [], []
        for s in range(STEP):
            pivot = columns[t][s][s : s + 1]
            for m in range(s):
                pivot = pivot - lower[s, m] * lower[s, m]
            scale.append(lax.rsqrt(pivot))
            for q in range(s + 1, STEP):
                entry = columns[t][s][q : q + 1]
                for m in range(s):
                    entry = entry - lower[q, m] * lower[s, m]
                lower[q, s] = entry * scale[s]
            line = tiles[t][s : s + 1]
            for m in range(s):
                line = line - lower[s, m] * done[m]
            done.append(line * scale[s])
        for u in range(t + 1, n // STEP):
            factors = []
            for s in range(STEP):
                factor = columns[u][s]
                for m in range(s):
                    factor = factor - factors[m] * lower[s, m]
                factors.append(factor * scale[s])
                tiles[u] = tiles[u] - factors[s] * done[s]
        for s in range(STEP):
            tiles[t] = jnp.where(row == s, done[s], tiles[t])
    return jnp.concatenate(tiles, axis=0)[:, n:]


def inverse_factor_kernel(packed_ref, inverse_ref, work_ref):
    n = inverse_ref.shape[0]
    block, width = n // XN, packed_ref.shape[2] // 2
    for b in range(XN):
        rows = jnp.concatenate([packed_ref[b, :, :width], packed_ref[b, :, width:]], axis=0)
        here = pl.ds(b * block, block)
        for j in range(XN - 1):
            c = (b + j) % XN * block
            work_ref[here, c : c + block] = rows[:, j * block : (j + 1) * block]
        below = (b + 1) % XN * block
        work_ref[below : below + block, b * block : (b + 1) * block] = rows[:, block : 2 * block].T
    work_ref[:, n:] = eye(n)
    for top in range(0, n, PANEL):
        end = top + PANEL
        own = inverse_factor_of_panel(work_ref[top:end, top:end])
        done = jnp.dot(own, work_ref[top:end], precision=HIGHEST, preferred_element_type=F32)
        inverse_ref[top:end] = done[:, n:]
        if end < n:
            below = lax.dot_general(
                work_ref[end:, top:end], own, (((1,), (1,)), ((), ())),
                precision=HIGHEST, preferred_element_type=F32,
            )
            work_ref[end:] = work_ref[end:] - jnp.dot(
                below, done, precision=HIGHEST, preferred_element_type=F32
            )


VMEM = pl.BlockSpec(memory_space=pltpu.VMEM)
SMEM = pl.BlockSpec(memory_space=pltpu.SMEM)


def inverse_factor(packed, n):
    return pl.pallas_call(
        inverse_factor_kernel,
        out_shape=jax.ShapeDtypeStruct((n, n), F32),
        in_specs=[VMEM],
        out_specs=VMEM,
        scratch_shapes=[pltpu.VMEM((n, 2 * n), F32)],
        compiler_params=pltpu.CompilerParams(vmem_limit_bytes=16 * MIB),
        cost_estimate=pl.CostEstimate(flops=FACTOR_COST, bytes_accessed=2**10, transcendentals=0),
        name="inverse_factor",
    )(packed)


def range_product(turned, own, base):
    total = None
    for step in range(3):
        part = turned.astype(BF16)
        turned = turned - part.astype(F32)
        term = jnp.dot(part, own, preferred_element_type=F32)
        term -= jnp.dot(part, base, preferred_element_type=F32)
        total = term if total is None else total + term
    return total


def weighted_kernel(got_ref, out_ref):
    members, rows, wide = got_ref.shape
    ff = wide - 128
    piece = rows // FN
    total, freq_sum = jnp.zeros((rows, ff), F32), jnp.zeros((1, 1), F32)
    for j in range(members):
        tag = got_ref[j, :16, ff:].astype(F32)
        freq = tag[:1, :1] * 64 + tag[:1, 1:2]
        freq_sum += freq
        total += freq * got_ref[j, :, :ff].astype(F32)
    for f in range(FN):
        out_ref[f, :, :ff] = total[f * piece : (f + 1) * piece]
        out_ref[f, :, ff:] = jnp.broadcast_to(freq_sum, (piece, 128))


def weighted(got):
    members, rows, wide = got.shape
    return pl.pallas_call(
        weighted_kernel,
        out_shape=jax.ShapeDtypeStruct((FN, rows // FN, wide), F32),
        in_specs=[VMEM],
        out_specs=VMEM,
        compiler_params=pltpu.CompilerParams(vmem_limit_bytes=16 * MIB),
        cost_estimate=pl.CostEstimate(flops=2**20, bytes_accessed=2**21, transcendentals=0),
        name="weighted",
    )(got)


def half_products(core, load_ref, own_ref, sketch_ref, range_ref):
    half = load_ref.shape[0]
    ff, rank = sketch_ref.shape
    own = own_ref[pl.ds(pl.multiple_of(core * half, half), half), :]
    base_sketch = (
        load_ref[:, ff : ff + rank].astype(F32)
        + load_ref[:, ff + rank : ff + 2 * rank].astype(F32)
        + load_ref[:, ff + 2 * rank :].astype(F32)
    )
    range_rows = jnp.dot(own, sketch_ref[...], preferred_element_type=F32) - base_sketch
    range_ref[...] = range_rows
    turned = range_rows.T
    gram = jnp.dot(turned, range_rows, precision=HIGHEST, preferred_element_type=F32)
    return gram, range_product(turned, own, load_ref[:, :ff])


def own_products_kernel(core_ref, load_ref, own_ref, sketch_ref, gram_ref, delta_ref, range_ref):
    gram_ref[...], delta_ref[...] = half_products(
        core_ref[0], load_ref, own_ref, sketch_ref, range_ref
    )


def products_kernel(
    core_ref, load_ref, own_ref, sketch_ref, own_gram_ref, own_delta_ref,
    first_ref, second_ref, range_ref,
):
    ff, rank = sketch_ref.shape
    block, slab = rank // XN, ff // XN
    gram, delta = half_products(1 - core_ref[0], load_ref, own_ref, sketch_ref, range_ref)
    gram += own_gram_ref[...]
    delta += own_delta_ref[...]
    for b in range(XN):
        mine = gram[b * block : (b + 1) * block]
        kept = jnp.concatenate(
            [mine[:, (b + j) % XN * block :][:, :block] for j in range(XN - 1)], axis=1
        )
        packed = jnp.concatenate([kept[: block // 2], kept[block // 2 :]], axis=1)
        first_ref[b, : block // 2, :] = packed
        first_ref[b, block // 2 :, :] = delta[:FIRST, b * slab : (b + 1) * slab]
        second_ref[b] = delta[FIRST:, b * slab : (b + 1) * slab]


def own_products(core, load, own, sketch):
    half, (ff, rank) = load.shape[0], sketch.shape
    return pl.pallas_call(
        own_products_kernel,
        out_shape=[jax.ShapeDtypeStruct(shape, F32) for shape in ((rank, rank), (rank, ff), (half, rank))],
        in_specs=[SMEM] + [VMEM] * 3,
        out_specs=[VMEM] * 3,
        compiler_params=pltpu.CompilerParams(vmem_limit_bytes=32 * MIB),
        cost_estimate=pl.CostEstimate(flops=2 * 10**9, bytes_accessed=2**10, transcendentals=0),
        name="own_products",
    )(core, load, own, sketch)


def products(core, load, own, sketch, own_gram, own_delta):
    half, (ff, rank) = load.shape[0], sketch.shape
    first = (XN, rank // XN // 2 + FIRST, ff // XN)
    second = (XN, rank - FIRST, ff // XN)
    return pl.pallas_call(
        products_kernel,
        out_shape=[jax.ShapeDtypeStruct(shape, F32) for shape in (first, second, (half, rank))],
        in_specs=[SMEM] + [VMEM] * 5,
        out_specs=[VMEM] * 3,
        compiler_params=pltpu.CompilerParams(vmem_limit_bytes=32 * MIB),
        cost_estimate=pl.CostEstimate(flops=3 * 10**9, bytes_accessed=2**10, transcendentals=0),
        name="products",
    )(core, load, own, sketch, own_gram, own_delta)


def finished_kernel(inverse_ref, *refs):
    pairs, (out_ref, sums_ref) = refs[:-2], refs[-2:]
    rank = inverse_ref.shape[0]
    top = 0
    for i in range(0, len(pairs), 2):
        end = top + pairs[i].shape[0]
        sums_ref[top:end] = pairs[i][...] + pairs[i + 1][...]
        top = end
    values = jnp.dot(
        inverse_ref[...], sums_ref[...], precision=HIGHEST, preferred_element_type=F32
    )
    most = jnp.max(jnp.max(jnp.abs(values), axis=0, keepdims=True), axis=1, keepdims=True)
    power = jnp.floor(jnp.log(jnp.maximum(most, 1e-30)) * (1 / math.log(2)))
    out_ref[:rank] = values * jnp.exp2(TOP_POWER - power)
    out_ref[rank:] = jnp.broadcast_to(power, (out_ref.shape[0] - rank, out_ref.shape[1]))


def finished(inverse, pairs):
    rank, slab = inverse.shape[0], pairs[0].shape[1]
    return pl.pallas_call(
        finished_kernel,
        out_shape=jax.ShapeDtypeStruct((rank + 16, slab), F32),
        in_specs=[VMEM] * (1 + len(pairs)),
        out_specs=VMEM,
        scratch_shapes=[pltpu.VMEM((rank, slab), F32)],
        compiler_params=pltpu.CompilerParams(vmem_limit_bytes=16 * MIB),
        name="finished",
    )(inverse, *pairs)


def assembled_kernel(blocks_ref, out_ref, held_ref, sems):
    rank, slab = held_ref.shape[1:]
    copies = []
    for b in range(XN):
        scale = jnp.exp2(blocks_ref[b, rank : rank + 1] - TOP_POWER)
        held_ref[b] = blocks_ref[b, :rank] * scale
        copy = pltpu.make_async_copy(
            held_ref.at[b], out_ref.at[:, pl.ds(b * slab, slab)], sems.at[b]
        )
        copy.start()
        copies.append(copy)
    for copy in copies:
        copy.wait()


def assembled(blocks):
    rank, slab = blocks.shape[1] - 16, blocks.shape[2]
    return pl.pallas_call(
        assembled_kernel,
        out_shape=jax.ShapeDtypeStruct((rank, XN * slab), F32),
        in_specs=[VMEM],
        out_specs=pl.BlockSpec(memory_space=pl.ANY),
        scratch_shapes=[pltpu.VMEM((XN, rank, slab), F32), pltpu.SemaphoreType.DMA((XN,))],
        compiler_params=pltpu.CompilerParams(vmem_limit_bytes=16 * MIB),
        name="assembled",
    )(blocks)


def per_device(counts, up_weights, sketch):
    rows, ff = up_weights.shape[1:]
    rank = sketch.shape[1]
    piece = rows // 64
    own = up_weights[0].reshape(YN, FN, NN, CN, piece, ff).transpose(3, 0, 2, 1, 4, 5)
    members = CN * YN * NN
    own = own.reshape(members, FN * piece, ff)

    lane = lax.broadcasted_iota(jnp.int32, (members, FN * piece, 128), 2)
    count = counts[0]
    tag = jnp.where(lane == 0, count // 64, jnp.where(lane == 1, count % 64, 0)).astype(BF16)
    got = lax.all_to_all(
        jnp.concatenate([own, tag], axis=2), "exp", 0, 0, axis_index_groups=CYN_GROUPS
    )

    sums = lax.all_to_all(weighted(got), "exp", 0, 0, axis_index_groups=FAR_GROUPS)
    sums = jnp.sum(sums, axis=0)
    base_rows = sums[:, :ff] / sums[:, ff : ff + 1]
    base_piece = base_rows.astype(BF16)
    sketched = jnp.dot(base_rows, sketch.astype(F32), precision=HIGHEST)

    wide = ff + 3 * rank
    load = jnp.concatenate([base_piece] + parts_of(sketched), axis=1)
    load = lax.all_to_all(
        jnp.broadcast_to(load, (FN, piece, wide)), "exp", 0, 0, axis_index_groups=FAR_GROUPS
    ).reshape(FN * piece, wide)
    load = lax.all_to_all(
        jnp.broadcast_to(load, (YN * NN, FN * piece, wide)),
        "exp", 0, 0, axis_index_groups=YN_GROUPS,
    ).reshape(rows // CN, wide)
    other = lax.ppermute(load, "exp", OTHER_CORE)

    core, own = (lax.axis_index("exp") % CN).reshape(1), own.reshape(rows, ff)

    def to_owners(blocks):
        return lax.all_to_all(blocks, "grp", 0, 0, axis_index_groups=X_GROUPS)

    own_gram, own_delta, own_range = own_products(core, load, own, sketch)
    first, second, other_range = products(core, other, own, sketch, own_gram, own_delta)
    first, second = to_owners(first), to_owners(second)
    first = jnp.sum(first, axis=0)
    first_came = lax.ppermute(first, "grp", OTHER_HALF)
    second = jnp.sum(second, axis=0)
    second_came = lax.ppermute(second, "grp", OTHER_HALF)
    packed = rank // XN // 2
    gram = first[:packed] + first_came[:packed]
    inverse = inverse_factor(to_owners(jnp.broadcast_to(gram, (XN,) + gram.shape)), rank)
    chunks = [first[packed:], first_came[packed:], second, second_came]
    inverse, chunks = lax.optimization_barrier((inverse, chunks))
    block = finished(inverse, chunks).astype(jnp.float16)
    blocks = to_owners(jnp.broadcast_to(block, (XN,) + block.shape))
    coeff = assembled(blocks.astype(F32))

    scale = math.sqrt(rows * lax.axis_size("grp"))
    halves = [
        scale * lax.dot_general(half, inverse, (((1,), (1,)), ((), ())), precision=HIGHEST)
        for half in (own_range, other_range)
    ]
    on_first = core[0] == 0
    basis = jnp.stack(
        [jnp.where(on_first, halves[i], halves[1 - i]) for i in range(CN)]
    )
    basis = basis.reshape(CN, YN, NN, FN, piece, rank).transpose(1, 3, 2, 0, 4, 5)
    return (base_piece, basis.reshape(1, rows, rank), coeff[None])


def solution(mesh):
    placed = (P("exp"), P("exp", "grp", None), P())
    return jax.shard_map(
        per_device,
        mesh=mesh,
        in_specs=placed,
        out_specs=(P(("grp", "exp"), None), P("exp", "grp", None), P("exp", None, None)),
        check_vma=False,
    )
```

```python
import math

import jax
import jax.numpy as jnp
from jax import lax
from jax.experimental import pallas as pl
from jax.experimental.pallas import tpu as pltpu
from jax.sharding import PartitionSpec as P

F32, BF16 = jnp.float32, jnp.bfloat16
HIGHEST = lax.Precision.HIGHEST
MIB = 2**20

YN, FN, NN, CN, XN = 4, 4, 2, 2, 4


def at(y, far, near, core):
    return y * 16 + (2 * far + near) * 2 + core


CYN_GROUPS = [
    [at(y, f, n, c) for c in range(CN) for y in range(YN) for n in range(NN)] for f in range(FN)
]
YN_GROUPS = [
    [at(y, f, n, c) for y in range(YN) for n in range(NN)] for f in range(FN) for c in range(CN)
]
FAR_GROUPS = [
    [at(y, f, n, c) for f in range(FN)]
    for y in range(YN) for n in range(NN) for c in range(CN)
]
OTHER_CORE = [(i, i ^ 1) for i in range(64)]
OTHER_HALF = [(i, i ^ 4) for i in range(8)]
X_GROUPS = [[h * XN + x for x in range(XN)] for h in range(2)]

PANEL, STEP = 64, 8
TOP_POWER = 13
FIRST = 64
FACTOR_COST = 2**29


def parts_of(value):
    first = lax.reduce_precision(value, 8, 7)
    return [first.astype(BF16), (value - first).astype(BF16)]


def eye(n):
    row, col = (lax.broadcasted_iota(jnp.int32, (n, n), d) for d in (0, 1))
    return jnp.where(row == col, 1.0, 0.0).astype(F32)


def inverse_factor_of_panel(square):
    n = square.shape[0]
    work = jnp.concatenate([square, eye(n)], axis=1)
    tiles = [work[t : t + STEP] for t in range(0, n, STEP)]
    row = lax.broadcasted_iota(jnp.int32, tiles[0].shape, 0)
    for t in range(n // STEP):
        columns = {
            u: [
                jnp.broadcast_to(tiles[u][:, t * STEP + s :][:, :1], tiles[u].shape)
                for s in range(STEP)
            ]
            for u in range(t, n // STEP)
        }
        lower, scale, done = {}, [], []
        for s in range(STEP):
            pivot = columns[t][s][s : s + 1]
            for m in range(s):
                pivot = pivot - lower[s, m] * lower[s, m]
            scale.append(lax.rsqrt(pivot))
            for q in range(s + 1, STEP):
                entry = columns[t][s][q : q + 1]
                for m in range(s):
                    entry = entry - lower[q, m] * lower[s, m]
                lower[q, s] = entry * scale[s]
            line = tiles[t][s : s + 1]
            for m in range(s):
                line = line - lower[s, m] * done[m]
            done.append(line * scale[s])
        for u in range(t + 1, n // STEP):
            factors = []
            for s in range(STEP):
                factor = columns[u][s]
                for m in range(s):
                    factor = factor - factors[m] * lower[s, m]
                factors.append(factor * scale[s])
                tiles[u] = tiles[u] - factors[s] * done[s]
        for s in range(STEP):
            tiles[t] = jnp.where(row == s, done[s], tiles[t])
    return jnp.concatenate(tiles, axis=0)[:, n:]


def inverse_factor_kernel(packed_ref, inverse_ref, work_ref):
    n = inverse_ref.shape[0]
    block, width = n // XN, packed_ref.shape[2] // 2
    for b in range(XN):
        rows = jnp.concatenate([packed_ref[b, :, :width], packed_ref[b, :, width:]], axis=0)
        here = pl.ds(b * block, block)
        for j in range(XN - 1):
            c = (b + j) % XN * block
            work_ref[here, c : c + block] = rows[:, j * block : (j + 1) * block]
        below = (b + 1) % XN * block
        work_ref[below : below + block, b * block : (b + 1) * block] = rows[:, block : 2 * block].T
    work_ref[:, n:] = eye(n)
    for top in range(0, n, PANEL):
        end = top + PANEL
        own = inverse_factor_of_panel(work_ref[top:end, top:end])
        done = jnp.dot(own, work_ref[top:end], precision=HIGHEST, preferred_element_type=F32)
        inverse_ref[top:end] = done[:, n:]
        if end < n:
            below = lax.dot_general(
                work_ref[end:, top:end], own, (((1,), (1,)), ((), ())),
                precision=HIGHEST, preferred_element_type=F32,
            )
            work_ref[end:] = work_ref[end:] - jnp.dot(
                below, done, precision=HIGHEST, preferred_element_type=F32
            )


VMEM = pl.BlockSpec(memory_space=pltpu.VMEM)
SMEM = pl.BlockSpec(memory_space=pltpu.SMEM)


def inverse_factor(packed, n):
    return pl.pallas_call(
        inverse_factor_kernel,
        out_shape=jax.ShapeDtypeStruct((n, n), F32),
        in_specs=[VMEM],
        out_specs=VMEM,
        scratch_shapes=[pltpu.VMEM((n, 2 * n), F32)],
        compiler_params=pltpu.CompilerParams(vmem_limit_bytes=16 * MIB),
        cost_estimate=pl.CostEstimate(flops=FACTOR_COST, bytes_accessed=2**10, transcendentals=0),
        name="inverse_factor",
    )(packed)


def range_product(turned, own, base):
    total = None
    for step in range(3):
        part = turned.astype(BF16)
        turned = turned - part.astype(F32)
        term = jnp.dot(part, own, preferred_element_type=F32)
        term -= jnp.dot(part, base, preferred_element_type=F32)
        total = term if total is None else total + term
    return total


def weighted_kernel(got_ref, out_ref):
    members, rows, wide = got_ref.shape
    ff = wide - 128
    piece = rows // FN
    total, freq_sum = jnp.zeros((rows, ff), F32), jnp.zeros((1, 1), F32)
    for j in range(members):
        tag = got_ref[j, :16, ff:].astype(F32)
        freq = tag[:1, :1] * 64 + tag[:1, 1:2]
        freq_sum += freq
        total += freq * got_ref[j, :, :ff].astype(F32)
    for f in range(FN):
        out_ref[f, :, :ff] = total[f * piece : (f + 1) * piece]
        out_ref[f, :, ff:] = jnp.broadcast_to(freq_sum, (piece, 128))


def weighted(got):
    members, rows, wide = got.shape
    return pl.pallas_call(
        weighted_kernel,
        out_shape=jax.ShapeDtypeStruct((FN, rows // FN, wide), F32),
        in_specs=[VMEM],
        out_specs=VMEM,
        compiler_params=pltpu.CompilerParams(vmem_limit_bytes=16 * MIB),
        cost_estimate=pl.CostEstimate(flops=2**20, bytes_accessed=2**21, transcendentals=0),
        name="weighted",
    )(got)


def half_products(core, load_ref, own_ref, sketch_ref, range_ref):
    half = load_ref.shape[0]
    ff, rank = sketch_ref.shape
    own = own_ref[pl.ds(pl.multiple_of(core * half, half), half), :]
    base_sketch = load_ref[:, ff : ff + rank].astype(F32) + load_ref[:, ff + rank :].astype(F32)
    range_rows = jnp.dot(own, sketch_ref[...], preferred_element_type=F32) - base_sketch
    range_ref[...] = range_rows
    turned = range_rows.T
    gram = jnp.dot(turned, range_rows, precision=HIGHEST, preferred_element_type=F32)
    return gram, range_product(turned, own, load_ref[:, :ff])


def own_products_kernel(core_ref, load_ref, own_ref, sketch_ref, gram_ref, delta_ref, range_ref):
    gram_ref[...], delta_ref[...] = half_products(
        core_ref[0], load_ref, own_ref, sketch_ref, range_ref
    )


def products_kernel(
    core_ref, load_ref, own_ref, sketch_ref, own_gram_ref, own_delta_ref,
    first_ref, second_ref, range_ref,
):
    ff, rank = sketch_ref.shape
    block, slab = rank // XN, ff // XN
    gram, delta = half_products(1 - core_ref[0], load_ref, own_ref, sketch_ref, range_ref)
    gram += own_gram_ref[...]
    delta += own_delta_ref[...]
    for b in range(XN):
        mine = gram[b * block : (b + 1) * block]
        kept = jnp.concatenate(
            [mine[:, (b + j) % XN * block :][:, :block] for j in range(XN - 1)], axis=1
        )
        packed = jnp.concatenate([kept[: block // 2], kept[block // 2 :]], axis=1)
        first_ref[b, : block // 2, :] = packed
        first_ref[b, block // 2 :, :] = delta[:FIRST, b * slab : (b + 1) * slab]
        second_ref[b] = delta[FIRST:, b * slab : (b + 1) * slab]


def own_products(core, load, own, sketch):
    half, (ff, rank) = load.shape[0], sketch.shape
    return pl.pallas_call(
        own_products_kernel,
        out_shape=[jax.ShapeDtypeStruct(shape, F32) for shape in ((rank, rank), (rank, ff), (half, rank))],
        in_specs=[SMEM] + [VMEM] * 3,
        out_specs=[VMEM] * 3,
        compiler_params=pltpu.CompilerParams(vmem_limit_bytes=32 * MIB),
        cost_estimate=pl.CostEstimate(flops=2 * 10**9, bytes_accessed=2**10, transcendentals=0),
        name="own_products",
    )(core, load, own, sketch)


def products(core, load, own, sketch, own_gram, own_delta):
    half, (ff, rank) = load.shape[0], sketch.shape
    first = (XN, rank // XN // 2 + FIRST, ff // XN)
    second = (XN, rank - FIRST, ff // XN)
    return pl.pallas_call(
        products_kernel,
        out_shape=[jax.ShapeDtypeStruct(shape, F32) for shape in (first, second, (half, rank))],
        in_specs=[SMEM] + [VMEM] * 5,
        out_specs=[VMEM] * 3,
        compiler_params=pltpu.CompilerParams(vmem_limit_bytes=32 * MIB),
        cost_estimate=pl.CostEstimate(flops=3 * 10**9, bytes_accessed=2**10, transcendentals=0),
        name="products",
    )(core, load, own, sketch, own_gram, own_delta)


def finished_kernel(inverse_ref, *refs):
    pairs, (out_ref, sums_ref) = refs[:-2], refs[-2:]
    rank = inverse_ref.shape[0]
    top = 0
    for i in range(0, len(pairs), 2):
        end = top + pairs[i].shape[0]
        sums_ref[top:end] = pairs[i][...] + pairs[i + 1][...]
        top = end
    values = jnp.dot(
        inverse_ref[...], sums_ref[...], precision=HIGHEST, preferred_element_type=F32
    )
    most = jnp.max(jnp.max(jnp.abs(values), axis=0, keepdims=True), axis=1, keepdims=True)
    power = jnp.floor(jnp.log(jnp.maximum(most, 1e-30)) * (1 / math.log(2)))
    out_ref[:rank] = values * jnp.exp2(TOP_POWER - power)
    out_ref[rank:] = jnp.broadcast_to(power, (out_ref.shape[0] - rank, out_ref.shape[1]))


def finished(inverse, pairs):
    rank, slab = inverse.shape[0], pairs[0].shape[1]
    return pl.pallas_call(
        finished_kernel,
        out_shape=jax.ShapeDtypeStruct((rank + 16, slab), F32),
        in_specs=[VMEM] * (1 + len(pairs)),
        out_specs=VMEM,
        scratch_shapes=[pltpu.VMEM((rank, slab), F32)],
        compiler_params=pltpu.CompilerParams(vmem_limit_bytes=16 * MIB),
        name="finished",
    )(inverse, *pairs)


def assembled_kernel(blocks_ref, out_ref, held_ref, sems):
    rank, slab = held_ref.shape[1:]
    copies = []
    for b in range(XN):
        scale = jnp.exp2(blocks_ref[b, rank : rank + 1] - TOP_POWER)
        held_ref[b] = blocks_ref[b, :rank] * scale
        copy = pltpu.make_async_copy(
            held_ref.at[b], out_ref.at[:, pl.ds(b * slab, slab)], sems.at[b]
        )
        copy.start()
        copies.append(copy)
    for copy in copies:
        copy.wait()


def assembled(blocks):
    rank, slab = blocks.shape[1] - 16, blocks.shape[2]
    return pl.pallas_call(
        assembled_kernel,
        out_shape=jax.ShapeDtypeStruct((rank, XN * slab), F32),
        in_specs=[VMEM],
        out_specs=pl.BlockSpec(memory_space=pl.ANY),
        scratch_shapes=[pltpu.VMEM((XN, rank, slab), F32), pltpu.SemaphoreType.DMA((XN,))],
        compiler_params=pltpu.CompilerParams(vmem_limit_bytes=16 * MIB),
        name="assembled",
    )(blocks)


def per_device(counts, up_weights, sketch):
    rows, ff = up_weights.shape[1:]
    rank = sketch.shape[1]
    piece = rows // 64
    own = up_weights[0].reshape(YN, FN, NN, CN, piece, ff).transpose(3, 0, 2, 1, 4, 5)
    members = CN * YN * NN
    own = own.reshape(members, FN * piece, ff)

    lane = lax.broadcasted_iota(jnp.int32, (members, FN * piece, 128), 2)
    count = counts[0]
    tag = jnp.where(lane == 0, count // 64, jnp.where(lane == 1, count % 64, 0)).astype(BF16)
    got = lax.all_to_all(
        jnp.concatenate([own, tag], axis=2), "exp", 0, 0, axis_index_groups=CYN_GROUPS
    )

    sums = lax.all_to_all(weighted(got), "exp", 0, 0, axis_index_groups=FAR_GROUPS)
    sums = jnp.sum(sums, axis=0)
    base_rows = sums[:, :ff] / sums[:, ff : ff + 1]
    base_piece = base_rows.astype(BF16)
    sketched = jnp.dot(base_rows, sketch.astype(F32), precision=HIGHEST)

    wide = ff + 2 * rank
    load = jnp.concatenate([base_piece] + parts_of(sketched), axis=1)
    load = lax.all_to_all(
        jnp.broadcast_to(load, (FN, piece, wide)), "exp", 0, 0, axis_index_groups=FAR_GROUPS
    ).reshape(FN * piece, wide)
    load = lax.all_to_all(
        jnp.broadcast_to(load, (YN * NN, FN * piece, wide)),
        "exp", 0, 0, axis_index_groups=YN_GROUPS,
    ).reshape(rows // CN, wide)
    other = lax.ppermute(load, "exp", OTHER_CORE)

    core, own = (lax.axis_index("exp") % CN).reshape(1), own.reshape(rows, ff)

    def to_owners(blocks):
        return lax.all_to_all(blocks, "grp", 0, 0, axis_index_groups=X_GROUPS)

    own_gram, own_delta, own_range = own_products(core, load, own, sketch)
    first, second, other_range = products(core, other, own, sketch, own_gram, own_delta)
    first, second = to_owners(first), to_owners(second)
    first = jnp.sum(first, axis=0)
    first_came = lax.ppermute(first, "grp", OTHER_HALF)
    second = jnp.sum(second, axis=0)
    second_came = lax.ppermute(second, "grp", OTHER_HALF)
    packed = rank // XN // 2
    gram = first[:packed] + first_came[:packed]
    inverse = inverse_factor(to_owners(jnp.broadcast_to(gram, (XN,) + gram.shape)), rank)
    chunks = [first[packed:], first_came[packed:], second, second_came]
    inverse, chunks = lax.optimization_barrier((inverse, chunks))
    block = finished(inverse, chunks).astype(jnp.float16)
    blocks = to_owners(jnp.broadcast_to(block, (XN,) + block.shape))
    coeff = assembled(blocks.astype(F32))

    scale = math.sqrt(rows * lax.axis_size("grp"))
    halves = [
        scale * lax.dot_general(half, inverse, (((1,), (1,)), ((), ())), precision=HIGHEST)
        for half in (own_range, other_range)
    ]
    on_first = core[0] == 0
    basis = jnp.stack(
        [jnp.where(on_first, halves[i], halves[1 - i]) for i in range(CN)]
    )
    basis = basis.reshape(CN, YN, NN, FN, piece, rank).transpose(1, 3, 2, 0, 4, 5)
    return (base_piece, basis.reshape(1, rows, rank), coeff[None])


def solution(mesh):
    placed = (P("exp"), P("exp", "grp", None), P())
    return jax.shard_map(
        per_device,
        mesh=mesh,
        in_specs=placed,
        out_specs=(P(("grp", "exp"), None), P("exp", "grp", None), P("exp", None, None)),
        check_vma=False,
    )
```

```python
import math

import jax
import jax.numpy as jnp
from jax import lax
from jax.experimental import pallas as pl
from jax.experimental.pallas import tpu as pltpu
from jax.sharding import PartitionSpec as P

F32, BF16 = jnp.float32, jnp.bfloat16
HIGHEST = lax.Precision.HIGHEST
MIB = 2**20

YN, FN, NN, CN, XN = 4, 4, 2, 2, 4


def at(y, far, near, core):
    return y * 16 + (2 * far + near) * 2 + core


CYN_GROUPS = [
    [at(y, f, n, c) for c in range(CN) for y in range(YN) for n in range(NN)] for f in range(FN)
]
YN_GROUPS = [
    [at(y, f, n, c) for y in range(YN) for n in range(NN)] for f in range(FN) for c in range(CN)
]
FAR_GROUPS = [
    [at(y, f, n, c) for f in range(FN)]
    for y in range(YN) for n in range(NN) for c in range(CN)
]
OTHER_CORE = [(i, i ^ 1) for i in range(64)]
ALONG_X = [[(i, i ^ k) for i in range(8)] for k in range(XN)]
OTHER_HALF = [(i, i ^ 4) for i in range(8)]
X_GROUPS = [[h * XN + x for x in range(XN)] for h in range(2)]

PANEL, STEP = 64, 8
TOP_POWER = 13
FIRST = 64
FACTOR_COST = 2**29


def parts_of(value):
    first = lax.reduce_precision(value, 8, 7)
    return [first.astype(BF16), (value - first).astype(BF16)]


def eye(n):
    row, col = (lax.broadcasted_iota(jnp.int32, (n, n), d) for d in (0, 1))
    return jnp.where(row == col, 1.0, 0.0).astype(F32)


def inverse_factor_of_panel(square):
    n = square.shape[0]
    work = jnp.concatenate([square, eye(n)], axis=1)
    tiles = [work[t : t + STEP] for t in range(0, n, STEP)]
    row = lax.broadcasted_iota(jnp.int32, tiles[0].shape, 0)
    for t in range(n // STEP):
        columns = {
            u: [
                jnp.broadcast_to(tiles[u][:, t * STEP + s :][:, :1], tiles[u].shape)
                for s in range(STEP)
            ]
            for u in range(t, n // STEP)
        }
        lower, scale, done = {}, [], []
        for s in range(STEP):
            pivot = columns[t][s][s : s + 1]
            for m in range(s):
                pivot = pivot - lower[s, m] * lower[s, m]
            scale.append(lax.rsqrt(pivot))
            for q in range(s + 1, STEP):
                entry = columns[t][s][q : q + 1]
                for m in range(s):
                    entry = entry - lower[q, m] * lower[s, m]
                lower[q, s] = entry * scale[s]
            line = tiles[t][s : s + 1]
            for m in range(s):
                line = line - lower[s, m] * done[m]
            done.append(line * scale[s])
        for u in range(t + 1, n // STEP):
            factors = []
            for s in range(STEP):
                factor = columns[u][s]
                for m in range(s):
                    factor = factor - factors[m] * lower[s, m]
                factors.append(factor * scale[s])
                tiles[u] = tiles[u] - factors[s] * done[s]
        for s in range(STEP):
            tiles[t] = jnp.where(row == s, done[s], tiles[t])
    return jnp.concatenate(tiles, axis=0)[:, n:]


def inverse_factor_kernel(packed_ref, inverse_ref, work_ref):
    n = inverse_ref.shape[0]
    block, width = n // XN, packed_ref.shape[2] // 2
    for b in range(XN):
        rows = jnp.concatenate([packed_ref[b, :, :width], packed_ref[b, :, width:]], axis=0)
        here = pl.ds(b * block, block)
        for j in range(XN - 1):
            c = (b + j) % XN * block
            work_ref[here, c : c + block] = rows[:, j * block : (j + 1) * block]
        below = (b + 1) % XN * block
        work_ref[below : below + block, b * block : (b + 1) * block] = rows[:, block : 2 * block].T
    work_ref[:, n:] = eye(n)
    for top in range(0, n, PANEL):
        end = top + PANEL
        own = inverse_factor_of_panel(work_ref[top:end, top:end])
        done = jnp.dot(own, work_ref[top:end], precision=HIGHEST, preferred_element_type=F32)
        inverse_ref[top:end] = done[:, n:]
        if end < n:
            below = lax.dot_general(
                work_ref[end:, top:end], own, (((1,), (1,)), ((), ())),
                precision=HIGHEST, preferred_element_type=F32,
            )
            work_ref[end:] = work_ref[end:] - jnp.dot(
                below, done, precision=HIGHEST, preferred_element_type=F32
            )


VMEM = pl.BlockSpec(memory_space=pltpu.VMEM)
SMEM = pl.BlockSpec(memory_space=pltpu.SMEM)


def inverse_factor(packed, n):
    return pl.pallas_call(
        inverse_factor_kernel,
        out_shape=jax.ShapeDtypeStruct((n, n), F32),
        in_specs=[VMEM],
        out_specs=VMEM,
        scratch_shapes=[pltpu.VMEM((n, 2 * n), F32)],
        compiler_params=pltpu.CompilerParams(vmem_limit_bytes=16 * MIB),
        cost_estimate=pl.CostEstimate(flops=FACTOR_COST, bytes_accessed=2**10, transcendentals=0),
        name="inverse_factor",
    )(packed)


def range_product(turned, own, base):
    total = None
    for step in range(3):
        part = turned.astype(BF16)
        turned = turned - part.astype(F32)
        term = jnp.dot(part, own, preferred_element_type=F32)
        term -= jnp.dot(part, base, preferred_element_type=F32)
        total = term if total is None else total + term
    return total


def weighted_kernel(got_ref, out_ref):
    members, rows, wide = got_ref.shape
    ff = wide - 128
    piece = rows // FN
    total, freq_sum = jnp.zeros((rows, ff), F32), jnp.zeros((1, 1), F32)
    for j in range(members):
        tag = got_ref[j, :16, ff:].astype(F32)
        freq = tag[:1, :1] * 64 + tag[:1, 1:2]
        freq_sum += freq
        total += freq * got_ref[j, :, :ff].astype(F32)
    for f in range(FN):
        out_ref[f, :, :ff] = total[f * piece : (f + 1) * piece]
        out_ref[f, :, ff:] = jnp.broadcast_to(freq_sum, (piece, 128))


def weighted(got):
    members, rows, wide = got.shape
    return pl.pallas_call(
        weighted_kernel,
        out_shape=jax.ShapeDtypeStruct((FN, rows // FN, wide), F32),
        in_specs=[VMEM],
        out_specs=VMEM,
        compiler_params=pltpu.CompilerParams(vmem_limit_bytes=16 * MIB),
        cost_estimate=pl.CostEstimate(flops=2**20, bytes_accessed=2**21, transcendentals=0),
        name="weighted",
    )(got)


def half_products(core, load_ref, own_ref, sketch_ref, range_ref):
    half = load_ref.shape[0]
    ff, rank = sketch_ref.shape
    own = own_ref[pl.ds(pl.multiple_of(core * half, half), half), :]
    base_sketch = load_ref[:, ff : ff + rank].astype(F32) + load_ref[:, ff + rank :].astype(F32)
    range_rows = jnp.dot(own, sketch_ref[...], preferred_element_type=F32) - base_sketch
    range_ref[...] = range_rows
    turned = range_rows.T
    gram = jnp.dot(turned, range_rows, precision=HIGHEST, preferred_element_type=F32)
    return gram, range_product(turned, own, load_ref[:, :ff])


def own_products_kernel(core_ref, load_ref, own_ref, sketch_ref, gram_ref, delta_ref, range_ref):
    gram_ref[...], delta_ref[...] = half_products(
        core_ref[0], load_ref, own_ref, sketch_ref, range_ref
    )


def products_kernel(
    place_ref, load_ref, own_ref, sketch_ref, own_gram_ref, own_delta_ref,
    first_ref, second_ref, range_ref,
):
    ff, rank = sketch_ref.shape
    block, slab = rank // XN, ff // XN
    core, x = place_ref[0], place_ref[1]
    gram, delta = half_products(1 - core, load_ref, own_ref, sketch_ref, range_ref)
    gram += own_gram_ref[...]
    delta += own_delta_ref[...]
    for b in range(XN):
        mine = gram[b * block : (b + 1) * block]
        kept = jnp.concatenate(
            [mine[:, (b + j) % XN * block :][:, :block] for j in range(XN - 1)], axis=1
        )
        packed = jnp.concatenate([kept[: block // 2], kept[block // 2 :]], axis=1)
        first_ref[b, : block // 2, :] = packed
        first_ref[b, block // 2 :, :] = delta[:FIRST, b * slab : (b + 1) * slab]
        second_ref[b ^ x] = delta[FIRST:, b * slab : (b + 1) * slab]


def own_products(core, load, own, sketch):
    half, (ff, rank) = load.shape[0], sketch.shape
    return pl.pallas_call(
        own_products_kernel,
        out_shape=[jax.ShapeDtypeStruct(shape, F32) for shape in ((rank, rank), (rank, ff), (half, rank))],
        in_specs=[SMEM] + [VMEM] * 3,
        out_specs=[VMEM] * 3,
        compiler_params=pltpu.CompilerParams(vmem_limit_bytes=32 * MIB),
        cost_estimate=pl.CostEstimate(flops=2 * 10**9, bytes_accessed=2**10, transcendentals=0),
        name="own_products",
    )(core, load, own, sketch)


def products(place, load, own, sketch, own_gram, own_delta):
    half, (ff, rank) = load.shape[0], sketch.shape
    first = (XN, rank // XN // 2 + FIRST, ff // XN)
    second = (XN, rank - FIRST, ff // XN)
    return pl.pallas_call(
        products_kernel,
        out_shape=[jax.ShapeDtypeStruct(shape, F32) for shape in (first, second, (half, rank))],
        in_specs=[SMEM] + [VMEM] * 5,
        out_specs=[VMEM] * 3,
        compiler_params=pltpu.CompilerParams(vmem_limit_bytes=32 * MIB),
        cost_estimate=pl.CostEstimate(flops=3 * 10**9, bytes_accessed=2**10, transcendentals=0),
        name="products",
    )(place, load, own, sketch, own_gram, own_delta)


def finished_kernel(inverse_ref, *refs):
    pairs, (out_ref, sums_ref) = refs[:-2], refs[-2:]
    rank = inverse_ref.shape[0]
    top = 0
    for i in range(0, len(pairs), 2):
        end = top + pairs[i].shape[0]
        sums_ref[top:end] = pairs[i][...] + pairs[i + 1][...]
        top = end
    values = jnp.dot(
        inverse_ref[...], sums_ref[...], precision=HIGHEST, preferred_element_type=F32
    )
    most = jnp.max(jnp.max(jnp.abs(values), axis=0, keepdims=True), axis=1, keepdims=True)
    power = jnp.floor(jnp.log(jnp.maximum(most, 1e-30)) * (1 / math.log(2)))
    out_ref[:rank] = values * jnp.exp2(TOP_POWER - power)
    out_ref[rank:] = jnp.broadcast_to(power, (out_ref.shape[0] - rank, out_ref.shape[1]))


def finished(inverse, pairs):
    rank, slab = inverse.shape[0], pairs[0].shape[1]
    return pl.pallas_call(
        finished_kernel,
        out_shape=jax.ShapeDtypeStruct((rank + 16, slab), F32),
        in_specs=[VMEM] * (1 + len(pairs)),
        out_specs=VMEM,
        scratch_shapes=[pltpu.VMEM((rank, slab), F32)],
        compiler_params=pltpu.CompilerParams(vmem_limit_bytes=16 * MIB),
        name="finished",
    )(inverse, *pairs)


def assembled_kernel(blocks_ref, out_ref, held_ref, sems):
    rank, slab = held_ref.shape[1:]
    copies = []
    for b in range(XN):
        scale = jnp.exp2(blocks_ref[b, rank : rank + 1] - TOP_POWER)
        held_ref[b] = blocks_ref[b, :rank] * scale
        copy = pltpu.make_async_copy(
            held_ref.at[b], out_ref.at[:, pl.ds(b * slab, slab)], sems.at[b]
        )
        copy.start()
        copies.append(copy)
    for copy in copies:
        copy.wait()


def assembled(blocks):
    rank, slab = blocks.shape[1] - 16, blocks.shape[2]
    return pl.pallas_call(
        assembled_kernel,
        out_shape=jax.ShapeDtypeStruct((rank, XN * slab), F32),
        in_specs=[VMEM],
        out_specs=pl.BlockSpec(memory_space=pl.ANY),
        scratch_shapes=[pltpu.VMEM((XN, rank, slab), F32), pltpu.SemaphoreType.DMA((XN,))],
        compiler_params=pltpu.CompilerParams(vmem_limit_bytes=16 * MIB),
        name="assembled",
    )(blocks)


def per_device(counts, up_weights, sketch):
    rows, ff = up_weights.shape[1:]
    rank = sketch.shape[1]
    piece = rows // 64
    own = up_weights[0].reshape(YN, FN, NN, CN, piece, ff).transpose(3, 0, 2, 1, 4, 5)
    members = CN * YN * NN
    own = own.reshape(members, FN * piece, ff)

    lane = lax.broadcasted_iota(jnp.int32, (members, FN * piece, 128), 2)
    count = counts[0]
    tag = jnp.where(lane == 0, count // 64, jnp.where(lane == 1, count % 64, 0)).astype(BF16)
    got = lax.all_to_all(
        jnp.concatenate([own, tag], axis=2), "exp", 0, 0, axis_index_groups=CYN_GROUPS
    )

    sums = lax.all_to_all(weighted(got), "exp", 0, 0, axis_index_groups=FAR_GROUPS)
    sums = jnp.sum(sums, axis=0)
    base_rows = sums[:, :ff] / sums[:, ff : ff + 1]
    base_piece = base_rows.astype(BF16)
    sketched = jnp.dot(base_rows, sketch.astype(F32), precision=HIGHEST)

    wide = ff + 2 * rank
    load = jnp.concatenate([base_piece] + parts_of(sketched), axis=1)
    load = lax.all_to_all(
        jnp.broadcast_to(load, (FN, piece, wide)), "exp", 0, 0, axis_index_groups=FAR_GROUPS
    ).reshape(FN * piece, wide)
    load = lax.all_to_all(
        jnp.broadcast_to(load, (YN * NN, FN * piece, wide)),
        "exp", 0, 0, axis_index_groups=YN_GROUPS,
    ).reshape(rows // CN, wide)
    other = lax.ppermute(load, "exp", OTHER_CORE)

    core, own = (lax.axis_index("exp") % CN).reshape(1), own.reshape(rows, ff)

    def to_owners(blocks):
        return lax.all_to_all(blocks, "grp", 0, 0, axis_index_groups=X_GROUPS)

    own_gram, own_delta, own_range = own_products(core, load, own, sketch)
    place = jnp.concatenate([core, (lax.axis_index("grp") % XN).reshape(1)])
    first, second, other_range = products(place, other, own, sketch, own_gram, own_delta)
    first = jnp.sum(to_owners(first), axis=0)
    first_came = lax.ppermute(first, "grp", OTHER_HALF)
    second = second[0] + sum(lax.ppermute(second[k], "grp", ALONG_X[k]) for k in (2, 3, 1))
    second_came = lax.ppermute(second, "grp", OTHER_HALF)
    packed = rank // XN // 2
    gram = first[:packed] + first_came[:packed]
    inverse = inverse_factor(to_owners(jnp.broadcast_to(gram, (XN,) + gram.shape)), rank)
    chunks = [first[packed:], first_came[packed:], second, second_came]
    inverse, chunks = lax.optimization_barrier((inverse, chunks))
    block = finished(inverse, chunks).astype(jnp.float16)
    blocks = to_owners(jnp.broadcast_to(block, (XN,) + block.shape))
    coeff = assembled(blocks.astype(F32))

    scale = math.sqrt(rows * lax.axis_size("grp"))
    halves = [
        scale * lax.dot_general(half, inverse, (((1,), (1,)), ((), ())), precision=HIGHEST)
        for half in (own_range, other_range)
    ]
    on_first = core[0] == 0
    basis = jnp.stack(
        [jnp.where(on_first, halves[i], halves[1 - i]) for i in range(CN)]
    )
    basis = basis.reshape(CN, YN, NN, FN, piece, rank).transpose(1, 3, 2, 0, 4, 5)
    return (base_piece, basis.reshape(1, rows, rank), coeff[None])


def solution(mesh):
    placed = (P("exp"), P("exp", "grp", None), P())
    return jax.shard_map(
        per_device,
        mesh=mesh,
        in_specs=placed,
        out_specs=(P(("grp", "exp"), None), P("exp", "grp", None), P("exp", None, None)),
        check_vma=False,
    )
```

```python
import math

import jax
import jax.numpy as jnp
from jax import lax
from jax.experimental import pallas as pl
from jax.experimental.pallas import tpu as pltpu
from jax.sharding import PartitionSpec as P

F32, BF16 = jnp.float32, jnp.bfloat16
HIGHEST = lax.Precision.HIGHEST
MIB = 2**20

YN, FN, NN, CN, XN = 4, 4, 2, 2, 4


def at(y, far, near, core):
    return y * 16 + (2 * far + near) * 2 + core


CYN_GROUPS = [
    [at(y, f, n, c) for c in range(CN) for y in range(YN) for n in range(NN)] for f in range(FN)
]
YN_GROUPS = [
    [at(y, f, n, c) for y in range(YN) for n in range(NN)] for f in range(FN) for c in range(CN)
]
FAR_GROUPS = [
    [at(y, f, n, c) for f in range(FN)]
    for y in range(YN) for n in range(NN) for c in range(CN)
]
OTHER_CORE = [(i, i ^ 1) for i in range(64)]
ALONG_X = [[(i, i ^ k) for i in range(8)] for k in range(XN)]
OTHER_HALF = [(i, i ^ 4) for i in range(8)]
X_GROUPS = [[h * XN + x for x in range(XN)] for h in range(2)]

PANEL, STEP = 64, 8
TOP_POWER = 13
FIRST = 72
FACTOR_COST = 2**29


def parts_of(value):
    first = lax.reduce_precision(value, 8, 7)
    return [first.astype(BF16), (value - first).astype(BF16)]


def eye(n):
    row, col = (lax.broadcasted_iota(jnp.int32, (n, n), d) for d in (0, 1))
    return jnp.where(row == col, 1.0, 0.0).astype(F32)


def inverse_factor_of_panel(square):
    n = square.shape[0]
    work = jnp.concatenate([square, eye(n)], axis=1)
    tiles = [work[t : t + STEP] for t in range(0, n, STEP)]
    row = lax.broadcasted_iota(jnp.int32, tiles[0].shape, 0)
    for t in range(n // STEP):
        columns = {
            u: [
                jnp.broadcast_to(tiles[u][:, t * STEP + s :][:, :1], tiles[u].shape)
                for s in range(STEP)
            ]
            for u in range(t, n // STEP)
        }
        lower, scale, done = {}, [], []
        for s in range(STEP):
            pivot = columns[t][s][s : s + 1]
            for m in range(s):
                pivot = pivot - lower[s, m] * lower[s, m]
            scale.append(lax.rsqrt(pivot))
            for q in range(s + 1, STEP):
                entry = columns[t][s][q : q + 1]
                for m in range(s):
                    entry = entry - lower[q, m] * lower[s, m]
                lower[q, s] = entry * scale[s]
            line = tiles[t][s : s + 1]
            for m in range(s):
                line = line - lower[s, m] * done[m]
            done.append(line * scale[s])
        for u in range(t + 1, n // STEP):
            factors = []
            for s in range(STEP):
                factor = columns[u][s]
                for m in range(s):
                    factor = factor - factors[m] * lower[s, m]
                factors.append(factor * scale[s])
                tiles[u] = tiles[u] - factors[s] * done[s]
        for s in range(STEP):
            tiles[t] = jnp.where(row == s, done[s], tiles[t])
    return jnp.concatenate(tiles, axis=0)[:, n:]


def inverse_factor_kernel(packed_ref, inverse_ref, work_ref):
    n = inverse_ref.shape[0]
    block, width = n // XN, packed_ref.shape[2] // 2
    for b in range(XN):
        rows = jnp.concatenate([packed_ref[b, :, :width], packed_ref[b, :, width:]], axis=0)
        here = pl.ds(b * block, block)
        for j in range(XN - 1):
            c = (b + j) % XN * block
            work_ref[here, c : c + block] = rows[:, j * block : (j + 1) * block]
        below = (b + 1) % XN * block
        work_ref[below : below + block, b * block : (b + 1) * block] = rows[:, block : 2 * block].T
    work_ref[:, n:] = eye(n)
    for top in range(0, n, PANEL):
        end = top + PANEL
        own = inverse_factor_of_panel(work_ref[top:end, top:end])
        done = jnp.dot(own, work_ref[top:end], precision=HIGHEST, preferred_element_type=F32)
        inverse_ref[top:end] = done[:, n:]
        if end < n:
            below = lax.dot_general(
                work_ref[end:, top:end], own, (((1,), (1,)), ((), ())),
                precision=HIGHEST, preferred_element_type=F32,
            )
            work_ref[end:] = work_ref[end:] - jnp.dot(
                below, done, precision=HIGHEST, preferred_element_type=F32
            )


VMEM = pl.BlockSpec(memory_space=pltpu.VMEM)
SMEM = pl.BlockSpec(memory_space=pltpu.SMEM)


def inverse_factor(packed, n):
    return pl.pallas_call(
        inverse_factor_kernel,
        out_shape=jax.ShapeDtypeStruct((n, n), F32),
        in_specs=[VMEM],
        out_specs=VMEM,
        scratch_shapes=[pltpu.VMEM((n, 2 * n), F32)],
        compiler_params=pltpu.CompilerParams(vmem_limit_bytes=16 * MIB),
        cost_estimate=pl.CostEstimate(flops=FACTOR_COST, bytes_accessed=2**10, transcendentals=0),
        name="inverse_factor",
    )(packed)


def range_product(turned, own, base):
    total = None
    for step in range(3):
        part = turned.astype(BF16)
        turned = turned - part.astype(F32)
        term = jnp.dot(part, own, preferred_element_type=F32)
        term -= jnp.dot(part, base, preferred_element_type=F32)
        total = term if total is None else total + term
    return total


def weighted_kernel(got_ref, out_ref):
    members, rows, wide = got_ref.shape
    ff = wide - 128
    piece = rows // FN
    total, freq_sum = jnp.zeros((rows, ff), F32), jnp.zeros((1, 1), F32)
    for j in range(members):
        tag = got_ref[j, :16, ff:].astype(F32)
        freq = tag[:1, :1] * 64 + tag[:1, 1:2]
        freq_sum += freq
        total += freq * got_ref[j, :, :ff].astype(F32)
    for f in range(FN):
        out_ref[f, :, :ff] = total[f * piece : (f + 1) * piece]
        out_ref[f, :, ff:] = jnp.broadcast_to(freq_sum, (piece, 128))


def weighted(got):
    members, rows, wide = got.shape
    return pl.pallas_call(
        weighted_kernel,
        out_shape=jax.ShapeDtypeStruct((FN, rows // FN, wide), F32),
        in_specs=[VMEM],
        out_specs=VMEM,
        compiler_params=pltpu.CompilerParams(vmem_limit_bytes=16 * MIB),
        cost_estimate=pl.CostEstimate(flops=2**20, bytes_accessed=2**21, transcendentals=0),
        name="weighted",
    )(got)


def half_products(core, load_ref, own_ref, sketch_ref, range_ref):
    half = load_ref.shape[0]
    ff, rank = sketch_ref.shape
    own = own_ref[pl.ds(pl.multiple_of(core * half, half), half), :]
    base_sketch = load_ref[:, ff : ff + rank].astype(F32) + load_ref[:, ff + rank :].astype(F32)
    range_rows = jnp.dot(own, sketch_ref[...], preferred_element_type=F32) - base_sketch
    range_ref[...] = range_rows
    turned = range_rows.T
    gram = jnp.dot(turned, range_rows, precision=HIGHEST, preferred_element_type=F32)
    return gram, range_product(turned, own, load_ref[:, :ff])


def own_products_kernel(core_ref, load_ref, own_ref, sketch_ref, gram_ref, delta_ref, range_ref):
    gram_ref[...], delta_ref[...] = half_products(
        core_ref[0], load_ref, own_ref, sketch_ref, range_ref
    )


def products_kernel(
    place_ref, load_ref, own_ref, sketch_ref, own_gram_ref, own_delta_ref, own_range_ref,
    first_ref, second_ref, range_ref,
):
    ff, rank = sketch_ref.shape
    block, slab = rank // XN, ff // XN
    core, x = place_ref[0], place_ref[1]
    range_ref[core] = own_range_ref[...]
    gram, delta = half_products(
        1 - core, load_ref, own_ref, sketch_ref, range_ref.at[1 - core]
    )
    gram += own_gram_ref[...]
    delta += own_delta_ref[...]
    for b in range(XN):
        mine = gram[b * block : (b + 1) * block]
        kept = jnp.concatenate(
            [mine[:, (b + j) % XN * block :][:, :block] for j in range(XN - 1)], axis=1
        )
        packed = jnp.concatenate([kept[: block // 2], kept[block // 2 :]], axis=1)
        first_ref[b, : block // 2, :] = packed
        first_ref[b, block // 2 :, :] = delta[:FIRST, b * slab : (b + 1) * slab]
        second_ref[b ^ x] = delta[FIRST:, b * slab : (b + 1) * slab]


def own_products(core, load, own, sketch):
    half, (ff, rank) = load.shape[0], sketch.shape
    return pl.pallas_call(
        own_products_kernel,
        out_shape=[jax.ShapeDtypeStruct(shape, F32) for shape in ((rank, rank), (rank, ff), (half, rank))],
        in_specs=[SMEM] + [VMEM] * 3,
        out_specs=[VMEM] * 3,
        compiler_params=pltpu.CompilerParams(vmem_limit_bytes=32 * MIB),
        cost_estimate=pl.CostEstimate(flops=2 * 10**9, bytes_accessed=2**10, transcendentals=0),
        name="own_products",
    )(core, load, own, sketch)


def products(place, load, own, sketch, own_gram, own_delta, own_range):
    half, (ff, rank) = load.shape[0], sketch.shape
    first = (XN, rank // XN // 2 + FIRST, ff // XN)
    second = (XN, rank - FIRST, ff // XN)
    return pl.pallas_call(
        products_kernel,
        out_shape=[jax.ShapeDtypeStruct(shape, F32) for shape in (first, second, (CN, half, rank))],
        in_specs=[SMEM] + [VMEM] * 6,
        out_specs=[VMEM] * 3,
        compiler_params=pltpu.CompilerParams(vmem_limit_bytes=32 * MIB),
        cost_estimate=pl.CostEstimate(flops=3 * 10**9, bytes_accessed=2**10, transcendentals=0),
        name="products",
    )(place, load, own, sketch, own_gram, own_delta, own_range)


def finished_kernel(inverse_ref, *refs):
    pairs, (out_ref, sums_ref) = refs[:-2], refs[-2:]
    rank = inverse_ref.shape[0]
    top = 0
    for i in range(0, len(pairs), 2):
        end = top + pairs[i].shape[0]
        sums_ref[top:end] = pairs[i][...] + pairs[i + 1][...]
        top = end
    values = jnp.dot(
        inverse_ref[...], sums_ref[...], precision=HIGHEST, preferred_element_type=F32
    )
    most = jnp.max(jnp.max(jnp.abs(values), axis=0, keepdims=True), axis=1, keepdims=True)
    power = jnp.floor(jnp.log(jnp.maximum(most, 1e-30)) * (1 / math.log(2)))
    out_ref[:rank] = values * jnp.exp2(TOP_POWER - power)
    out_ref[rank:] = jnp.broadcast_to(power, (out_ref.shape[0] - rank, out_ref.shape[1]))


def finished(inverse, pairs):
    rank, slab = inverse.shape[0], pairs[0].shape[1]
    return pl.pallas_call(
        finished_kernel,
        out_shape=jax.ShapeDtypeStruct((rank + 16, slab), F32),
        in_specs=[VMEM] * (1 + len(pairs)),
        out_specs=VMEM,
        scratch_shapes=[pltpu.VMEM((rank, slab), F32)],
        compiler_params=pltpu.CompilerParams(vmem_limit_bytes=16 * MIB),
        name="finished",
    )(inverse, *pairs)


def assembled_kernel(blocks_ref, out_ref, held_ref, sems):
    rank, slab = held_ref.shape[1:]
    copies = []
    for b in range(XN):
        scale = jnp.exp2(blocks_ref[b, rank : rank + 1] - TOP_POWER)
        held_ref[b] = blocks_ref[b, :rank] * scale
        copy = pltpu.make_async_copy(
            held_ref.at[b], out_ref.at[:, pl.ds(b * slab, slab)], sems.at[b]
        )
        copy.start()
        copies.append(copy)
    for copy in copies:
        copy.wait()


def assembled(blocks):
    rank, slab = blocks.shape[1] - 16, blocks.shape[2]
    return pl.pallas_call(
        assembled_kernel,
        out_shape=jax.ShapeDtypeStruct((rank, XN * slab), F32),
        in_specs=[VMEM],
        out_specs=pl.BlockSpec(memory_space=pl.ANY),
        scratch_shapes=[pltpu.VMEM((XN, rank, slab), F32), pltpu.SemaphoreType.DMA((XN,))],
        compiler_params=pltpu.CompilerParams(vmem_limit_bytes=16 * MIB),
        name="assembled",
    )(blocks)


def per_device(counts, up_weights, sketch):
    rows, ff = up_weights.shape[1:]
    rank = sketch.shape[1]
    piece = rows // 64
    own = up_weights[0].reshape(YN, FN, NN, CN, piece, ff).transpose(3, 0, 2, 1, 4, 5)
    members = CN * YN * NN
    own = own.reshape(members, FN * piece, ff)

    lane = lax.broadcasted_iota(jnp.int32, (members, FN * piece, 128), 2)
    count = counts[0]
    tag = jnp.where(lane == 0, count // 64, jnp.where(lane == 1, count % 64, 0)).astype(BF16)
    got = lax.all_to_all(
        jnp.concatenate([own, tag], axis=2), "exp", 0, 0, axis_index_groups=CYN_GROUPS
    )

    sums = lax.all_to_all(weighted(got), "exp", 0, 0, axis_index_groups=FAR_GROUPS)
    sums = jnp.sum(sums, axis=0)
    base_rows = sums[:, :ff] / sums[:, ff : ff + 1]
    base_piece = base_rows.astype(BF16)
    sketched = jnp.dot(base_rows, sketch.astype(F32), precision=HIGHEST)

    wide = ff + 2 * rank
    load = jnp.concatenate([base_piece] + parts_of(sketched), axis=1)
    load = lax.all_to_all(
        jnp.broadcast_to(load, (FN, piece, wide)), "exp", 0, 0, axis_index_groups=FAR_GROUPS
    ).reshape(FN * piece, wide)
    load = lax.all_to_all(
        jnp.broadcast_to(load, (YN * NN, FN * piece, wide)),
        "exp", 0, 0, axis_index_groups=YN_GROUPS,
    ).reshape(rows // CN, wide)
    other = lax.ppermute(load, "exp", OTHER_CORE)

    core, own = (lax.axis_index("exp") % CN).reshape(1), own.reshape(rows, ff)

    def to_owners(blocks):
        return lax.all_to_all(blocks, "grp", 0, 0, axis_index_groups=X_GROUPS)

    held = own_products(core, load, own, sketch)
    place = jnp.concatenate([core, (lax.axis_index("grp") % XN).reshape(1)])
    first, second, range_rows = products(place, other, own, sketch, *held)
    first = jnp.sum(to_owners(first), axis=0)
    first_came = lax.ppermute(first, "grp", OTHER_HALF)
    second = second[0] + sum(lax.ppermute(second[k], "grp", ALONG_X[k]) for k in (2, 3, 1))
    second_came = lax.ppermute(second, "grp", OTHER_HALF)
    packed = rank // XN // 2
    gram = first[:packed] + first_came[:packed]
    inverse = inverse_factor(to_owners(jnp.broadcast_to(gram, (XN,) + gram.shape)), rank)
    chunks = [first[packed:], first_came[packed:], second, second_came]
    inverse, chunks = lax.optimization_barrier((inverse, chunks))
    block = finished(inverse, chunks).astype(jnp.float16)
    blocks = to_owners(jnp.broadcast_to(block, (XN,) + block.shape))
    coeff = assembled(blocks.astype(F32))

    ortho = lax.dot_general(
        range_rows.reshape(rows, rank), inverse, (((1,), (1,)), ((), ())), precision=HIGHEST
    )
    basis = ortho * math.sqrt(rows * lax.axis_size("grp"))
    basis = basis.reshape(CN, YN, NN, FN, piece, rank).transpose(1, 3, 2, 0, 4, 5)
    return (base_piece, basis.reshape(1, rows, rank), coeff[None])


def solution(mesh):
    placed = (P("exp"), P("exp", "grp", None), P())
    return jax.shard_map(
        per_device,
        mesh=mesh,
        in_specs=placed,
        out_specs=(P(("grp", "exp"), None), P("exp", "grp", None), P("exp", None, None)),
        check_vma=False,
    )
```

```python
import math

import jax
import jax.numpy as jnp
from jax import lax
from jax.experimental import pallas as pl
from jax.experimental.pallas import tpu as pltpu
from jax.sharding import PartitionSpec as P

F32, BF16 = jnp.float32, jnp.bfloat16
HIGHEST = lax.Precision.HIGHEST
MIB = 2**20

YN, FN, NN, CN, XN = 4, 4, 2, 2, 4


def at(y, far, near, core):
    return y * 16 + (2 * far + near) * 2 + core


CYN_GROUPS = [
    [at(y, f, n, c) for c in range(CN) for y in range(YN) for n in range(NN)] for f in range(FN)
]
YN_GROUPS = [
    [at(y, f, n, c) for y in range(YN) for n in range(NN)] for f in range(FN) for c in range(CN)
]
FAR_GROUPS = [
    [at(y, f, n, c) for f in range(FN)]
    for y in range(YN) for n in range(NN) for c in range(CN)
]
OTHER_CORE = [(i, i ^ 1) for i in range(64)]
ALONG_X = [[(i, i ^ k) for i in range(8)] for k in range(XN)]
OTHER_HALF = [(i, i ^ 4) for i in range(8)]
X_GROUPS = [[h * XN + x for x in range(XN)] for h in range(2)]

PANEL, STEP = 64, 8
TOP_POWER = 13
FIRST = 64
FACTOR_COST = 2**29


def parts_of(value):
    first = lax.reduce_precision(value, 8, 7)
    return [first.astype(BF16), (value - first).astype(BF16)]


def eye(n):
    row, col = (lax.broadcasted_iota(jnp.int32, (n, n), d) for d in (0, 1))
    return jnp.where(row == col, 1.0, 0.0).astype(F32)


def inverse_factor_of_panel(square):
    n = square.shape[0]
    work = jnp.concatenate([square, eye(n)], axis=1)
    tiles = [work[t : t + STEP] for t in range(0, n, STEP)]
    row = lax.broadcasted_iota(jnp.int32, tiles[0].shape, 0)
    for t in range(n // STEP):
        columns = {
            u: [
                jnp.broadcast_to(tiles[u][:, t * STEP + s :][:, :1], tiles[u].shape)
                for s in range(STEP)
            ]
            for u in range(t, n // STEP)
        }
        lower, scale, done = {}, [], []
        for s in range(STEP):
            pivot = columns[t][s][s : s + 1]
            for m in range(s):
                pivot = pivot - lower[s, m] * lower[s, m]
            scale.append(lax.rsqrt(pivot))
            for q in range(s + 1, STEP):
                entry = columns[t][s][q : q + 1]
                for m in range(s):
                    entry = entry - lower[q, m] * lower[s, m]
                lower[q, s] = entry * scale[s]
            line = tiles[t][s : s + 1]
            for m in range(s):
                line = line - lower[s, m] * done[m]
            done.append(line * scale[s])
        for u in range(t + 1, n // STEP):
            factors = []
            for s in range(STEP):
                factor = columns[u][s]
                for m in range(s):
                    factor = factor - factors[m] * lower[s, m]
                factors.append(factor * scale[s])
                tiles[u] = tiles[u] - factors[s] * done[s]
        for s in range(STEP):
            tiles[t] = jnp.where(row == s, done[s], tiles[t])
    return jnp.concatenate(tiles, axis=0)[:, n:]


def inverse_factor_kernel(packed_ref, inverse_ref, work_ref):
    n = inverse_ref.shape[0]
    block, width = n // XN, packed_ref.shape[2] // 2
    for b in range(XN):
        rows = jnp.concatenate([packed_ref[b, :, :width], packed_ref[b, :, width:]], axis=0)
        here = pl.ds(b * block, block)
        for j in range(XN - 1):
            c = (b + j) % XN * block
            work_ref[here, c : c + block] = rows[:, j * block : (j + 1) * block]
        below = (b + 1) % XN * block
        work_ref[below : below + block, b * block : (b + 1) * block] = rows[:, block : 2 * block].T
    work_ref[:, n:] = eye(n)
    for top in range(0, n, PANEL):
        end = top + PANEL
        own = inverse_factor_of_panel(work_ref[top:end, top:end])
        done = jnp.dot(own, work_ref[top:end], precision=HIGHEST, preferred_element_type=F32)
        inverse_ref[top:end] = done[:, n:]
        if end < n:
            below = lax.dot_general(
                work_ref[end:, top:end], own, (((1,), (1,)), ((), ())),
                precision=HIGHEST, preferred_element_type=F32,
            )
            work_ref[end:] = work_ref[end:] - jnp.dot(
                below, done, precision=HIGHEST, preferred_element_type=F32
            )


VMEM = pl.BlockSpec(memory_space=pltpu.VMEM)
SMEM = pl.BlockSpec(memory_space=pltpu.SMEM)


def inverse_factor(packed, n):
    return pl.pallas_call(
        inverse_factor_kernel,
        out_shape=jax.ShapeDtypeStruct((n, n), F32),
        in_specs=[VMEM],
        out_specs=VMEM,
        scratch_shapes=[pltpu.VMEM((n, 2 * n), F32)],
        compiler_params=pltpu.CompilerParams(vmem_limit_bytes=16 * MIB),
        cost_estimate=pl.CostEstimate(flops=FACTOR_COST, bytes_accessed=2**10, transcendentals=0),
        name="inverse_factor",
    )(packed)


def range_product(turned, own, base):
    total = None
    for step in range(3):
        part = turned.astype(BF16)
        turned = turned - part.astype(F32)
        term = jnp.dot(part, own, preferred_element_type=F32)
        term -= jnp.dot(part, base, preferred_element_type=F32)
        total = term if total is None else total + term
    return total


def weighted_kernel(got_ref, out_ref):
    members, rows, wide = got_ref.shape
    ff = wide - 128
    piece = rows // FN
    total, freq_sum = jnp.zeros((rows, ff), F32), jnp.zeros((1, 1), F32)
    for j in range(members):
        tag = got_ref[j, :16, ff:].astype(F32)
        freq = tag[:1, :1] * 64 + tag[:1, 1:2]
        freq_sum += freq
        total += freq * got_ref[j, :, :ff].astype(F32)
    for f in range(FN):
        out_ref[f, :, :ff] = total[f * piece : (f + 1) * piece]
        out_ref[f, :, ff:] = jnp.broadcast_to(freq_sum, (piece, 128))


def weighted(got):
    members, rows, wide = got.shape
    return pl.pallas_call(
        weighted_kernel,
        out_shape=jax.ShapeDtypeStruct((FN, rows // FN, wide), F32),
        in_specs=[VMEM],
        out_specs=VMEM,
        compiler_params=pltpu.CompilerParams(vmem_limit_bytes=16 * MIB),
        cost_estimate=pl.CostEstimate(flops=2**20, bytes_accessed=2**21, transcendentals=0),
        name="weighted",
    )(got)


def half_products(core, load_ref, own_ref, sketch_ref, range_ref):
    half = load_ref.shape[0]
    ff, rank = sketch_ref.shape
    own = own_ref[pl.ds(pl.multiple_of(core * half, half), half), :]
    base_sketch = load_ref[:, ff : ff + rank].astype(F32) + load_ref[:, ff + rank :].astype(F32)
    range_rows = jnp.dot(own, sketch_ref[...], preferred_element_type=F32) - base_sketch
    range_ref[...] = range_rows
    turned = range_rows.T
    gram = jnp.dot(turned, range_rows, precision=HIGHEST, preferred_element_type=F32)
    return gram, range_product(turned, own, load_ref[:, :ff])


def own_products_kernel(core_ref, load_ref, own_ref, sketch_ref, gram_ref, delta_ref, range_ref):
    gram_ref[...], delta_ref[...] = half_products(
        core_ref[0], load_ref, own_ref, sketch_ref, range_ref
    )


def products_kernel(
    place_ref, load_ref, own_ref, sketch_ref, own_gram_ref, own_delta_ref, own_range_ref,
    first_ref, second_ref, range_ref,
):
    ff, rank = sketch_ref.shape
    block, slab = rank // XN, ff // XN
    core, x = place_ref[0], place_ref[1]
    range_ref[core] = own_range_ref[...]
    gram, delta = half_products(
        1 - core, load_ref, own_ref, sketch_ref, range_ref.at[1 - core]
    )
    gram += own_gram_ref[...]
    delta += own_delta_ref[...]
    for b in range(XN):
        mine = gram[b * block : (b + 1) * block]
        kept = jnp.concatenate(
            [mine[:, (b + j) % XN * block :][:, :block] for j in range(XN - 1)], axis=1
        )
        packed = jnp.concatenate([kept[: block // 2], kept[block // 2 :]], axis=1)
        first_ref[b, : block // 2, :] = packed
        first_ref[b, block // 2 :, :] = delta[:FIRST, b * slab : (b + 1) * slab]
        second_ref[b ^ x] = delta[FIRST:, b * slab : (b + 1) * slab]


def own_products(core, load, own, sketch):
    half, (ff, rank) = load.shape[0], sketch.shape
    return pl.pallas_call(
        own_products_kernel,
        out_shape=[jax.ShapeDtypeStruct(shape, F32) for shape in ((rank, rank), (rank, ff), (half, rank))],
        in_specs=[SMEM] + [VMEM] * 3,
        out_specs=[VMEM] * 3,
        compiler_params=pltpu.CompilerParams(vmem_limit_bytes=32 * MIB),
        cost_estimate=pl.CostEstimate(flops=2 * 10**9, bytes_accessed=2**10, transcendentals=0),
        name="own_products",
    )(core, load, own, sketch)


def products(place, load, own, sketch, own_gram, own_delta, own_range):
    half, (ff, rank) = load.shape[0], sketch.shape
    first = (XN, rank // XN // 2 + FIRST, ff // XN)
    second = (XN, rank - FIRST, ff // XN)
    return pl.pallas_call(
        products_kernel,
        out_shape=[jax.ShapeDtypeStruct(shape, F32) for shape in (first, second, (CN, half, rank))],
        in_specs=[SMEM] + [VMEM] * 6,
        out_specs=[VMEM] * 3,
        compiler_params=pltpu.CompilerParams(vmem_limit_bytes=32 * MIB),
        cost_estimate=pl.CostEstimate(flops=3 * 10**9, bytes_accessed=2**10, transcendentals=0),
        name="products",
    )(place, load, own, sketch, own_gram, own_delta, own_range)


def finished_kernel(inverse_ref, *refs):
    pairs, (out_ref, sums_ref) = refs[:-2], refs[-2:]
    rank = inverse_ref.shape[0]
    top = 0
    for i in range(0, len(pairs), 2):
        end = top + pairs[i].shape[0]
        sums_ref[top:end] = pairs[i][...] + pairs[i + 1][...]
        top = end
    values = jnp.dot(
        inverse_ref[...], sums_ref[...], precision=HIGHEST, preferred_element_type=F32
    )
    most = jnp.max(jnp.max(jnp.abs(values), axis=0, keepdims=True), axis=1, keepdims=True)
    power = jnp.floor(jnp.log(jnp.maximum(most, 1e-30)) * (1 / math.log(2)))
    out_ref[:rank] = values * jnp.exp2(TOP_POWER - power)
    out_ref[rank:] = jnp.broadcast_to(power, (out_ref.shape[0] - rank, out_ref.shape[1]))


def finished(inverse, pairs):
    rank, slab = inverse.shape[0], pairs[0].shape[1]
    return pl.pallas_call(
        finished_kernel,
        out_shape=jax.ShapeDtypeStruct((rank + 16, slab), F32),
        in_specs=[VMEM] * (1 + len(pairs)),
        out_specs=VMEM,
        scratch_shapes=[pltpu.VMEM((rank, slab), F32)],
        compiler_params=pltpu.CompilerParams(vmem_limit_bytes=16 * MIB),
        name="finished",
    )(inverse, *pairs)


def assembled_kernel(blocks_ref, out_ref, held_ref, sems):
    rank, slab = held_ref.shape[1:]
    copies = []
    for b in range(XN):
        scale = jnp.exp2(blocks_ref[b, rank : rank + 1] - TOP_POWER)
        held_ref[b] = blocks_ref[b, :rank] * scale
        copy = pltpu.make_async_copy(
            held_ref.at[b], out_ref.at[:, pl.ds(b * slab, slab)], sems.at[b]
        )
        copy.start()
        copies.append(copy)
    for copy in copies:
        copy.wait()


def assembled(blocks):
    rank, slab = blocks.shape[1] - 16, blocks.shape[2]
    return pl.pallas_call(
        assembled_kernel,
        out_shape=jax.ShapeDtypeStruct((rank, XN * slab), F32),
        in_specs=[VMEM],
        out_specs=pl.BlockSpec(memory_space=pl.ANY),
        scratch_shapes=[pltpu.VMEM((XN, rank, slab), F32), pltpu.SemaphoreType.DMA((XN,))],
        compiler_params=pltpu.CompilerParams(vmem_limit_bytes=16 * MIB),
        name="assembled",
    )(blocks)


def per_device(counts, up_weights, sketch):
    rows, ff = up_weights.shape[1:]
    rank = sketch.shape[1]
    piece = rows // 64
    own = up_weights[0].reshape(YN, FN, NN, CN, piece, ff).transpose(3, 0, 2, 1, 4, 5)
    members = CN * YN * NN
    own = own.reshape(members, FN * piece, ff)

    lane = lax.broadcasted_iota(jnp.int32, (members, FN * piece, 128), 2)
    count = counts[0]
    tag = jnp.where(lane == 0, count // 64, jnp.where(lane == 1, count % 64, 0)).astype(BF16)
    got = lax.all_to_all(
        jnp.concatenate([own, tag], axis=2), "exp", 0, 0, axis_index_groups=CYN_GROUPS
    )

    sums = lax.all_to_all(weighted(got), "exp", 0, 0, axis_index_groups=FAR_GROUPS)
    sums = jnp.sum(sums, axis=0)
    base_rows = sums[:, :ff] / sums[:, ff : ff + 1]
    base_piece = base_rows.astype(BF16)
    sketched = jnp.dot(base_rows, sketch.astype(F32), precision=HIGHEST)

    wide = ff + 2 * rank
    load = jnp.concatenate([base_piece] + parts_of(sketched), axis=1)
    load = lax.all_to_all(
        jnp.broadcast_to(load, (FN, piece, wide)), "exp", 0, 0, axis_index_groups=FAR_GROUPS
    ).reshape(FN * piece, wide)
    load = lax.all_to_all(
        jnp.broadcast_to(load, (YN * NN, FN * piece, wide)),
        "exp", 0, 0, axis_index_groups=YN_GROUPS,
    ).reshape(rows // CN, wide)
    other = lax.ppermute(load, "exp", OTHER_CORE)

    core, own = (lax.axis_index("exp") % CN).reshape(1), own.reshape(rows, ff)

    def to_owners(blocks):
        return lax.all_to_all(blocks, "grp", 0, 0, axis_index_groups=X_GROUPS)

    held = own_products(core, load, own, sketch)
    place = jnp.concatenate([core, (lax.axis_index("grp") % XN).reshape(1)])
    first, second, range_rows = products(place, other, own, sketch, *held)
    first = jnp.sum(to_owners(first), axis=0)
    first_came = lax.ppermute(first, "grp", OTHER_HALF)
    second = second[0] + sum(lax.ppermute(second[k], "grp", ALONG_X[k]) for k in (2, 3, 1))
    second_came = lax.ppermute(second, "grp", OTHER_HALF)
    packed = rank // XN // 2
    gram = first[:packed] + first_came[:packed]
    inverse = inverse_factor(to_owners(jnp.broadcast_to(gram, (XN,) + gram.shape)), rank)
    chunks = [first[packed:], first_came[packed:], second, second_came]
    inverse, chunks = lax.optimization_barrier((inverse, chunks))
    block = finished(inverse, chunks).astype(jnp.float16)
    blocks = to_owners(jnp.broadcast_to(block, (XN,) + block.shape))
    coeff = assembled(blocks.astype(F32))

    ortho = lax.dot_general(
        range_rows.reshape(rows, rank), inverse, (((1,), (1,)), ((), ())), precision=HIGHEST
    )
    basis = ortho * math.sqrt(rows * lax.axis_size("grp"))
    basis = basis.reshape(CN, YN, NN, FN, piece, rank).transpose(1, 3, 2, 0, 4, 5)
    return (base_piece, basis.reshape(1, rows, rank), coeff[None])


def solution(mesh):
    placed = (P("exp"), P("exp", "grp", None), P())
    return jax.shard_map(
        per_device,
        mesh=mesh,
        in_specs=placed,
        out_specs=(P(("grp", "exp"), None), P("exp", "grp", None), P("exp", None, None)),
        check_vma=False,
    )
```
